128 devices in a mesh: gx: 16 (over z, y), gy: 8 (over x, core).
Axes of the slice: x: 4, y: 4, z: 4, core: 2. Of those that a mesh axis runs over, the one named last changes fastest.
Arguments:
- sky_bottom_quantities: bfloat16 [2048, 8, 256], P(('gx', 'gy')), may hold values from -6 to 6
- link_weight_array: bfloat16 [2048, 256, 256], P(('gx', 'gy')), as said below
- link_sky_block: int32 [2048], P(('gx', 'gy')), may hold values from 0 to 15
- link_target_device: int32 [2048, 1], P(('gx', 'gy')), may hold values from 0 to 127, as said below
- link_sea_block: int32 [2048], P(('gx', 'gy')), may hold values from 0 to 15
- sea_warmth_anomaly: float32 [2048, 256], P(('gx', 'gy')), may hold values from -6 to 6
- marine_indicator: int32 [2048, 256], P(('gx', 'gy')), may hold values 0 or 1
Outputs:
- sea_top_forcings: float32 [2048, 4, 256], P(('gx', 'gy'))
- atm_back: float32 [2048, 5, 256], P(('gx', 'gy'))
The draws below stay inside these ranges and needn't reach their ends.
Inputs may be any that keep to these rules, and one draw needn't show every extreme that they name: `link_target_device`: devices are numbered gx-major (index along gx times 8 plus index along gy). Among the pairs of one device at most 2 name the same owner. Exactly 2 pairs of each device name each of these three: the device whose number is its own plus 128 // 2, its own plus 1, and its own minus 1, all taken modulo 128. `link_weight_array`: entries are nonnegative and zero unless the atmosphere cell and the ocean cell lie within 4 of each other modulo 256.
All inputs are finite; a program needn't handle non-finite values. No bound on the sum of `marine_indicator` on one device may be relied on, other than what follows from the above.
Results may differ from the reference program's by a relative error of at most 0.0026.
Values may be sent and summed in bfloat16 or wider, within the bound.
No kernel may reach another device: no remote copies, remote signals or barrier semaphores. Data moves between devices by JAX's collectives and lax.ppermute only.
A program may use at most 64 MiB of HBM per device.

```python
import jax
import jax.numpy as jnp
from jax import lax

FIELDS = 8
BACK = 5
POINTS_IN_BLOCK = 256
TILES_DEV = 16
PAIRS_DEV = 16
ATILES = 2048
SEA_BLOCK_TOTAL = 2048
PAIRS = 2048
CAP = 2
DEVICES = 128


def draw_link_target_device(key, part):
    first_key = jax.random.fold_in(key, 11)
    second_key = jax.random.fold_in(key, 12)
    offset_index = jnp.arange(DEVICES, dtype=jnp.int32)[None, :]
    offset_scores = jax.random.randint(first_key, (DEVICES, DEVICES), 0, 1 << 20) * DEVICES + offset_index
    offset_scores = jnp.where(offset_index == DEVICES // 2, -3, offset_scores)
    offset_scores = jnp.where(offset_index == 1, -2, offset_scores)
    offset_scores = jnp.where(offset_index == DEVICES - 1, -1, offset_scores)
    offset_order = jnp.argsort(offset_scores, axis=1, stable=True).astype(jnp.int32)
    pair_scores = jax.random.randint(second_key, (DEVICES, PAIRS_DEV), 0, 1 << 20) * PAIRS_DEV + jnp.arange(PAIRS_DEV, dtype=jnp.int32)[None, :]
    order = jnp.argsort(pair_scores, axis=1, stable=True).astype(jnp.int32)
    ranks = jnp.argsort(order, axis=1, stable=True).astype(jnp.int32)
    chosen = jnp.take_along_axis(offset_order, ranks // CAP, axis=1)
    device = jnp.arange(DEVICES, dtype=jnp.int32)[:, None]
    owner = (device + chosen) % DEVICES
    return owner.reshape(PAIRS, 1).astype(jnp.int32)


def draw_link_weight_array(key, part):
    first_key = jax.random.fold_in(key, 21)
    second_key = jax.random.fold_in(key, 22)
    atm_cell = jnp.arange(POINTS_IN_BLOCK, dtype=jnp.int32)[:, None]
    ocean_cell = jnp.arange(POINTS_IN_BLOCK, dtype=jnp.int32)[None, :]
    distance = (atm_cell - ocean_cell) % POINTS_IN_BLOCK
    in_band = jnp.logical_or(distance <= 4, distance >= POINTS_IN_BLOCK - 4)
    on_diag = distance == 0
    side = jax.random.uniform(first_key, (PAIRS, POINTS_IN_BLOCK, POINTS_IN_BLOCK), jnp.float32, 0.05, 0.6)
    main = jax.random.uniform(second_key, (PAIRS, 1, POINTS_IN_BLOCK), jnp.float32, 5.0, 7.0)
    scale = 1.0 / (8.6 * max(1, PAIRS_DEV // TILES_DEV))
    values = jnp.where(on_diag[None], main, jnp.where(in_band[None], side, 0.0)) * scale
    return values.astype(jnp.bfloat16)


def set_ends(values, key, smallest, top_value):
    shape = values.shape
    index_at = [jax.random.randint(jax.random.fold_in(key, axis), (), 0, shape[axis]) for axis in range(len(shape))]
    values = values.at[tuple(index_at)].set(smallest)
    longest = shape.index(max(shape))
    index_at[longest] = (index_at[longest] + 1) % shape[longest]
    return values.at[tuple(index_at)].set(top_value)


def shard_levels(stream_key, shape, split, smallest, high):
    loudness = 1.0
    for axis_at, blocks in split:
        steps = jax.random.uniform(jax.random.fold_in(jax.random.fold_in(stream_key, 6), axis_at), (blocks,), jnp.float32, smallest / len(split), high / len(split))
        loudness = loudness * jnp.repeat(jnp.exp(steps), shape[axis_at] // blocks).reshape((-1,) + (1,) * (len(shape) - 1 - axis_at))
    return loudness


def gaussian(stream_key, dims, width, bound, cuts=(), kind=jnp.bfloat16):
    entries = jax.random.normal(stream_key, dims, jnp.float32) * width
    if len(cuts) > 0:
        entries = shard_levels(stream_key, dims, cuts, -0.22, 0.18) * entries
    return jnp.clip(entries, min=-bound, max=bound).astype(kind)


def setup_inputs(seed: int = 0) -> dict:
    key_list = jax.random.split(jax.random.key(seed), 8)
    sky_bottom_quantities = gaussian(key_list[0], (ATILES, FIELDS, POINTS_IN_BLOCK), 1.0, 6.0, ((0, 128),))
    link_weight_array = draw_link_weight_array(jax.random.fold_in(key_list[7], 71), 0)
    link_sky_block = set_ends(jax.random.randint(key_list[2], (PAIRS,), 0, TILES_DEV), jax.random.fold_in(key_list[2], 1), 0, TILES_DEV - 1).astype(jnp.int32)
    link_target_device = draw_link_target_device(jax.random.fold_in(key_list[7], 71), 0)
    link_sea_block = set_ends(jax.random.randint(key_list[4], (PAIRS,), 0, TILES_DEV), jax.random.fold_in(key_list[4], 1), 0, TILES_DEV - 1).astype(jnp.int32)
    sea_warmth_anomaly = gaussian(key_list[5], (SEA_BLOCK_TOTAL, POINTS_IN_BLOCK), 1.0, 6.0, ((0, 128),), jnp.float32)
    marine_indicator = set_ends((jax.random.randint(key_list[6], (SEA_BLOCK_TOTAL, POINTS_IN_BLOCK), 0, 3) < 2).astype(jnp.int32), jax.random.fold_in(key_list[6], 1), 0, 1)
    return {"sky_bottom_quantities": sky_bottom_quantities, "link_weight_array": link_weight_array, "link_sky_block": link_sky_block, "link_target_device": link_target_device, "link_sea_block": link_sea_block, "sea_warmth_anomaly": sea_warmth_anomaly, "marine_indicator": marine_indicator}


def bulk_exchange_rates(regridded_quantities, sea_warmth_anomaly, marine_indicator):
    marine_points = marine_indicator.astype(jnp.float32)
    wind_u = regridded_quantities[:, 0]
    wind_v = regridded_quantities[:, 1]
    lower_layer_warmth = regridded_quantities[:, 2]
    vapour_moisture = regridded_quantities[:, 3]
    solar_radiation = regridded_quantities[:, 4]
    infrared_radiation = regridded_quantities[:, 5]
    precip = regridded_quantities[:, 6]
    bottom_barometric_load = regridded_quantities[:, 7]
    wind_speed = jnp.sqrt(wind_u * wind_u + wind_v * wind_v + 0.25)
    warmth_contrast = sea_warmth_anomaly - lower_layer_warmth
    moisture_contrast = 0.4 * sea_warmth_anomaly - vapour_moisture + 0.3 * bottom_barometric_load
    upward_lift = warmth_contrast + 0.5 * moisture_contrast
    steadiness_scaling = jnp.zeros_like(sea_warmth_anomaly)
    for iteration in range(3):
        coeff = 1.0 + 0.5 * jnp.tanh(steadiness_scaling)
        steadiness_scaling = 2.0 * upward_lift / (1.0 + coeff * wind_speed * wind_speed)
    coeff = 1.0 + 0.5 * jnp.tanh(steadiness_scaling)
    exchange_coefficient = coeff * wind_speed
    eastward_drag = exchange_coefficient * wind_u * marine_points
    northward_drag = exchange_coefficient * wind_v * marine_points
    warming_balance = (0.5 * solar_radiation + 0.3 * infrared_radiation - exchange_coefficient * warmth_contrast - exchange_coefficient * moisture_contrast) * marine_points
    rainfall_minus_evaporation = (precip - 0.5 * exchange_coefficient * moisture_contrast) * marine_points
    transfer_result = jnp.stack([eastward_drag, northward_drag, warming_balance, rainfall_minus_evaporation], axis=1)
    delivered_quantities = jnp.stack([eastward_drag, northward_drag, warming_balance, rainfall_minus_evaporation, sea_warmth_anomaly * marine_points], axis=1).astype(jnp.bfloat16)
    return (transfer_result, delivered_quantities)

def reference(sky_bottom_quantities, link_weight_array, link_sky_block, link_target_device, link_sea_block, sea_warmth_anomaly, marine_indicator):
    weights = link_weight_array.reshape(DEVICES, PAIRS_DEV, POINTS_IN_BLOCK, POINTS_IN_BLOCK)
    pair_index = jnp.arange(PAIRS, dtype=jnp.int32)
    source_tile = (pair_index // PAIRS_DEV * TILES_DEV + link_sky_block).astype(jnp.int32).reshape(DEVICES, PAIRS_DEV)
    dest_tile = (link_target_device[:, 0] * TILES_DEV + link_sea_block).astype(jnp.int32).reshape(DEVICES, PAIRS_DEV)

    def forward(total, block):
        weight_block, src_block, dst_block = block
        contrib = jnp.einsum('pfa,pat->pft', sky_bottom_quantities[src_block].astype(jnp.float32), weight_block.astype(jnp.float32))
        return (total.at[dst_block].add(contrib), None)
    regridded_quantities, _ = lax.scan(forward, jnp.zeros((SEA_BLOCK_TOTAL, FIELDS, POINTS_IN_BLOCK), jnp.float32), (weights, source_tile, dest_tile))
    sea_top_forcings, delivered_quantities = bulk_exchange_rates(regridded_quantities, sea_warmth_anomaly, marine_indicator)

    def backward(total, block):
        weight_block, src_block, dst_block = block
        back_terms = jnp.einsum('pft,pat->pfa', delivered_quantities[dst_block].astype(jnp.float32), weight_block.astype(jnp.float32))
        return (total.at[src_block].add(back_terms), None)
    atm_back, _ = lax.scan(backward, jnp.zeros((ATILES, BACK, POINTS_IN_BLOCK), jnp.float32), (weights, source_tile, dest_tile))
    return (sea_top_forcings, atm_back)
```

```python
import jax
import jax.numpy as jnp
from jax import lax
from jax.experimental import pallas as pl
from jax.experimental.pallas import tpu as pltpu
from jax.sharding import PartitionSpec as P

PAIRS = 16
TILES = 16
FIELDS = 8
CELLS = 256
HALF = 128
SLOTS = 2
SENT = 7
BACK = 5
ROWS_DEST = 2 * SLOTS
BF = jnp.bfloat16
F32 = jnp.float32
VMEM_LIMIT = 24 * 1024 * 1024


def iota(shape, dim):
    return lax.broadcasted_iota(jnp.int32, shape, dim)


def halves_to_rows(plane):
    return jnp.concatenate([plane[:, :HALF], plane[:, HALF:]], axis=0)


def field_rows(scratch, f):
    parts = [scratch[h, pl.ds(f, PAIRS, stride=FIELDS), :] for h in range(2)]
    return jnp.concatenate(parts, axis=0)


def slot_column(target_row):
    row = target_row.astype(F32)
    later, other = iota((PAIRS, PAIRS), 0), iota((PAIRS, PAIRS), 1)
    column = jnp.sum(jnp.where(later == other, row, 0.0), axis=1, keepdims=True)
    earlier = jnp.where((column == row) & (other < later), 1.0, 0.0)
    return SLOTS * column + jnp.sum(earlier, axis=1, keepdims=True)


def contribute(src, target, sea, sky, weights, out, scratch):
    rows = out.shape[0]
    for p in range(PAIRS):
        term = jnp.dot(sky[src[p]], weights[p], preferred_element_type=F32)
        for h in range(2):
            scratch[h, p * FIELDS : (p + 1) * FIELDS, :] = term[:, h * HALF : (h + 1) * HALF]
    u, v, ta, qa, sw, lw, pr, ps = (field_rows(scratch, f) for f in range(FIELDS))
    sent = [x.astype(BF) for x in (u, v, ta, qa - 0.3 * ps, 0.5 * sw + 0.3 * lw, pr)]
    both = 2 * PAIRS
    mine = (iota((both, PAIRS), 0) % PAIRS) == iota((both, PAIRS), 1)
    tile = jnp.sum(jnp.where(mine, sea[...].astype(F32), 0.0), axis=1, keepdims=True)
    label = tile + (iota((both, 1), 0) // PAIRS * TILES + 1).astype(F32)
    rest = u - sent[0].astype(F32)
    sent.append(jnp.where(iota((both, HALF), 1) == 0, label, rest).astype(BF))
    slot = slot_column(target[...])
    pair = iota((PAIRS, both), 1) % PAIRS == iota((PAIRS, both), 0)
    place = 2.0 * jnp.sum(jnp.where(pair, slot, 0.0), axis=0, keepdims=True)
    place = place.astype(jnp.int32) + iota((1, both), 1) // PAIRS
    chosen = jnp.where(iota((rows, both), 0) == place, 1.0, 0.0).astype(BF)
    out[...] = jnp.dot(chosen, jnp.concatenate(sent, axis=1), preferred_element_type=F32).astype(BF)


def exchange(arrived, sst, marine, fluxes, out):
    rows = arrived.shape[0]
    both = 2 * TILES
    label = arrived[:, (SENT - 1) * HALF :].astype(F32)[:, :1].astype(jnp.int32)
    chosen = jnp.where(label == iota((rows, both), 1) + 1, 1.0, 0.0).astype(BF)
    total = lax.dot_general(
        chosen, arrived[...], (((0,), (0,)), ((), ())), preferred_element_type=F32
    )
    u, v, ta, q, rad, pr, rest = (total[:, f * HALF : (f + 1) * HALF] for f in range(SENT))
    u = u + jnp.where(iota((both, HALF), 1) == 0, 0.0, rest)
    sst_rows = halves_to_rows(sst[...])
    w = halves_to_rows(marine[...].astype(F32))
    square = u * u + v * v + 0.25
    speed = jnp.sqrt(square)
    dth = sst_rows - ta
    dq = 0.4 * sst_rows - q
    lift = 2.0 * (dth + 0.5 * dq)
    c = jnp.ones_like(speed)
    for _ in range(3):
        c = 1.0 + 0.5 * jnp.tanh(lift / (1.0 + c * speed * speed))
    k = c * speed
    found = (k * u * w, k * v * w, (rad - k * dth - k * dq) * w, (pr - 0.5 * k * dq) * w)
    for f, x in enumerate(found):
        fluxes[f, :, :HALF] = x[:TILES]
        fluxes[f, :, HALF:] = x[TILES:]
    back = jnp.concatenate([x.astype(BF) for x in found + (sst_rows * w,)], axis=1)
    out[...] = jnp.dot(chosen, back, preferred_element_type=F32).astype(BF)


def deliver(src, target, returned, weights, out, values, sums):
    rows = returned.shape[0]
    both = 2 * PAIRS
    slot = slot_column(target[...])
    place = jnp.concatenate([2.0 * slot, 2.0 * slot + 1.0], axis=0).astype(jnp.int32)
    chosen = jnp.where(iota((both, rows), 1) == place, 1.0, 0.0).astype(BF)
    picked = jnp.dot(chosen, returned[...], preferred_element_type=F32)
    values[...] = jnp.zeros_like(values)
    for f in range(BACK):
        for h in range(2):
            part = picked[h * PAIRS : (h + 1) * PAIRS, f * HALF : (f + 1) * HALF]
            values[h, pl.ds(f, PAIRS, stride=FIELDS), :] = part
    sums[...] = jnp.zeros_like(sums)
    for p in range(PAIRS):
        block = pl.ds(p * FIELDS, FIELDS)
        term = lax.dot_general(
            jnp.concatenate([values[h, block, :] for h in range(2)], axis=1).astype(BF),
            weights[p],
            (((1,), (1,)), ((), ())),
            preferred_element_type=F32,
        )
        at = pl.ds(pl.multiple_of(src[p] * FIELDS, FIELDS), FIELDS)
        for h in range(2):
            sums[h, at, :] += term[:, h * HALF : (h + 1) * HALF]
    for f in range(BACK):
        for h in range(2):
            out[f, :, h * HALF : (h + 1) * HALF] = sums[h, pl.ds(f, TILES, stride=FIELDS), :]


SMEM = pl.BlockSpec(memory_space=pltpu.SMEM)
VMEM = pl.BlockSpec(memory_space=pltpu.VMEM)


def on_device(sky, weights, sky_block, target_device, sea_block, sst, marine):
    devices = lax.axis_size(("gx", "gy"))
    rows = devices * ROWS_DEST
    params = pltpu.CompilerParams(vmem_limit_bytes=VMEM_LIMIT)
    target = target_device.reshape(1, PAIRS)
    sea = sea_block.reshape(1, PAIRS)

    def swap(x):
        width = x.shape[1]
        y = lax.all_to_all(
            x.reshape(devices, ROWS_DEST, width),
            ("gx", "gy"),
            split_axis=0,
            concat_axis=0,
            tiled=True,
        )
        return y.reshape(rows, width)

    outgoing = pl.pallas_call(
        contribute,
        out_shape=jax.ShapeDtypeStruct((rows, SENT * HALF), BF),
        in_specs=[SMEM] + [VMEM] * 4,
        out_specs=VMEM,
        scratch_shapes=[pltpu.VMEM((2, PAIRS * FIELDS, HALF), F32)],
        compiler_params=params,
    )(sky_block, target, sea, sky, weights)
    fluxes, back = pl.pallas_call(
        exchange,
        out_shape=(
            jax.ShapeDtypeStruct((4, TILES, CELLS), F32),
            jax.ShapeDtypeStruct((rows, BACK * HALF), BF),
        ),
        in_specs=[VMEM] * 3,
        out_specs=(VMEM, VMEM),
        compiler_params=params,
    )(swap(outgoing), sst, marine)
    atm_back = pl.pallas_call(
        deliver,
        out_shape=jax.ShapeDtypeStruct((BACK, TILES, CELLS), F32),
        in_specs=[SMEM] + [VMEM] * 3,
        out_specs=VMEM,
        scratch_shapes=[
            pltpu.VMEM((2, PAIRS * FIELDS, HALF), F32),
            pltpu.VMEM((2, TILES * FIELDS, HALF), F32),
        ],
        compiler_params=params,
    )(sky_block, target, swap(back), weights)
    return jnp.transpose(fluxes, (1, 0, 2)), jnp.transpose(atm_back, (1, 0, 2))


def solution(mesh):
    tiles = P(("gx", "gy"), None, None)
    cells = P(("gx", "gy"), None)
    flat = P(("gx", "gy"))
    return jax.shard_map(
        on_device,
        mesh=mesh,
        in_specs=(tiles, tiles, flat, cells, flat, cells, cells),
        out_specs=(tiles, tiles),
        check_vma=False,
    )
```

```python
import jax
import jax.numpy as jnp
from jax import lax
from jax.experimental import pallas as pl
from jax.experimental.pallas import tpu as pltpu
from jax.sharding import PartitionSpec as P

PAIRS = 16
TILES = 16
FIELDS = 8
CELLS = 256
HALF = 128
SLOTS = 2
SENT = 7
BACK = 5
CORES = 2
CHIP_ROWS = CORES * 2 * TILES
GROUP = 4
BF = jnp.bfloat16
F32 = jnp.float32
VMEM_LIMIT = 24 * 1024 * 1024


def iota(shape, dim):
    return lax.broadcasted_iota(jnp.int32, shape, dim)


def halves_to_rows(plane):
    return jnp.concatenate([plane[:, :HALF], plane[:, HALF:]], axis=0)


def field_rows(scratch, f):
    parts = [scratch[h, pl.ds(f, PAIRS, stride=FIELDS), :] for h in range(2)]
    return jnp.concatenate(parts, axis=0)


def slot_column(target_row):
    row = target_row.astype(F32)
    later, other = iota((PAIRS, PAIRS), 0), iota((PAIRS, PAIRS), 1)
    column = jnp.sum(jnp.where(later == other, row, 0.0), axis=1, keepdims=True)
    earlier = jnp.where((column == row) & (other < later), 1.0, 0.0)
    return SLOTS * column + jnp.sum(earlier, axis=1, keepdims=True)


def contribute(
    src_hbm, target_hbm, sea_hbm, sky_hbm, weights_hbm, out,
    src, target, sea, sky, weights, scratch, sems,
):
    rows = out.shape[0]
    small = ((src_hbm, src), (sky_hbm, sky), (target_hbm, target), (sea_hbm, sea))
    copies = [pltpu.make_async_copy(a, b, sems.at[i]) for i, (a, b) in enumerate(small)]
    for i in range(PAIRS // GROUP):
        part = pl.ds(i * GROUP, GROUP)
        copies.append(
            pltpu.make_async_copy(weights_hbm.at[part], weights.at[part], sems.at[len(small) + i])
        )
    for copy in copies:
        copy.start()
    for copy in copies[: len(small)]:
        copy.wait()
    core = lax.axis_index("gy") % CORES
    for p in range(PAIRS):
        if p % GROUP == 0:
            copies[len(small) + p // GROUP].wait()
        term = jnp.dot(sky[src[p]], weights[p], preferred_element_type=F32)
        for h in range(2):
            scratch[h, p * FIELDS : (p + 1) * FIELDS, :] = term[:, h * HALF : (h + 1) * HALF]
    u, v, ta, qa, sw, lw, pr, ps = (field_rows(scratch, f) for f in range(FIELDS))
    sent = [x.astype(BF) for x in (u, v, ta, qa - 0.3 * ps, 0.5 * sw + 0.3 * lw, pr)]
    both = 2 * PAIRS
    mine = (iota((both, PAIRS), 0) % PAIRS) == iota((both, PAIRS), 1)
    tile = jnp.sum(jnp.where(mine, sea[...].astype(F32), 0.0), axis=1, keepdims=True)
    owner = jnp.sum(jnp.where(mine, target[...].astype(F32), 0.0), axis=1, keepdims=True)
    other = (owner.astype(jnp.int32) + core) % CORES * (2 * TILES)
    label = tile + (other + iota((both, 1), 0) // PAIRS * TILES + 1).astype(F32)
    rest = u - sent[0].astype(F32)
    sent.append(jnp.where(iota((both, HALF), 1) == 0, label, rest).astype(BF))
    slot = slot_column(target[...])
    pair = iota((PAIRS, both), 1) % PAIRS == iota((PAIRS, both), 0)
    place = 2.0 * jnp.sum(jnp.where(pair, slot, 0.0), axis=0, keepdims=True)
    place = place.astype(jnp.int32) + iota((1, both), 1) // PAIRS
    chosen = jnp.where(iota((rows, both), 0) == place, 1.0, 0.0).astype(BF)
    out[...] = jnp.dot(chosen, jnp.concatenate(sent, axis=1), preferred_element_type=F32).astype(BF)


def combine(arrived, partial, chosen):
    rows = arrived.shape[0]
    label = arrived[:, (SENT - 1) * HALF :].astype(F32)[:, :1].astype(jnp.int32)
    chosen[...] = jnp.where(label == iota((rows, CHIP_ROWS), 1) + 1, 1.0, 0.0).astype(BF)
    total = lax.dot_general(
        chosen[...], arrived[...], (((0,), (0,)), ((), ())), preferred_element_type=F32
    )
    partial[...] = total[:, : (SENT - 1) * HALF]
    rest = total[:, (SENT - 1) * HALF :]
    partial[:, :HALF] += jnp.where(iota((CHIP_ROWS, HALF), 1) == 0, 0.0, rest)


def exchange(own, swapped, chosen, sst, sst_other, marine, marine_other, fluxes, out):
    both = 2 * TILES
    total = own[...] + jnp.concatenate([swapped[both:], swapped[:both]], axis=0)
    u, v, ta, q, rad, pr = (total[:, f * HALF : (f + 1) * HALF] for f in range(SENT - 1))
    sst_rows = jnp.concatenate([halves_to_rows(x[...]) for x in (sst, sst_other)], axis=0)
    w = jnp.concatenate(
        [halves_to_rows(x[...].astype(F32)) for x in (marine, marine_other)], axis=0
    )
    square = u * u + v * v + 0.25
    speed = jnp.sqrt(square)
    dth = sst_rows - ta
    dq = 0.4 * sst_rows - q
    lift = 2.0 * (dth + 0.5 * dq)
    c = jnp.ones_like(speed)
    for _ in range(3):
        c = 1.0 + 0.5 * jnp.tanh(lift / (1.0 + c * speed * speed))
    k = c * speed
    found = (k * u * w, k * v * w, (rad - k * dth - k * dq) * w, (pr - 0.5 * k * dq) * w)
    for f, x in enumerate(found):
        fluxes[f, :, :HALF] = x[:TILES]
        fluxes[f, :, HALF:] = x[TILES:both]
    back = jnp.concatenate([x.astype(BF) for x in found + (sst_rows * w,)], axis=1)
    out[...] = jnp.dot(chosen[...], back, preferred_element_type=F32).astype(BF)


def deliver(src, target, returned, weights, out, values, sums):
    rows = returned.shape[0]
    both = 2 * PAIRS
    slot = slot_column(target[...])
    place = jnp.concatenate([2.0 * slot, 2.0 * slot + 1.0], axis=0).astype(jnp.int32)
    chosen = jnp.where(iota((both, rows), 1) == place, 1.0, 0.0).astype(BF)
    picked = jnp.dot(chosen, returned[...], preferred_element_type=F32)
    values[...] = jnp.zeros_like(values)
    for f in range(BACK):
        for h in range(2):
            part = picked[h * PAIRS : (h + 1) * PAIRS, f * HALF : (f + 1) * HALF]
            values[h, pl.ds(f, PAIRS, stride=FIELDS), :] = part
    sums[...] = jnp.zeros_like(sums)
    for p in range(PAIRS):
        block = pl.ds(p * FIELDS, FIELDS)
        term = lax.dot_general(
            jnp.concatenate([values[h, block, :] for h in range(2)], axis=1).astype(BF),
            weights[p],
            (((1,), (1,)), ((), ())),
            preferred_element_type=F32,
        )
        at = pl.ds(pl.multiple_of(src[p] * FIELDS, FIELDS), FIELDS)
        for h in range(2):
            sums[h, at, :] += term[:, h * HALF : (h + 1) * HALF]
    for f in range(BACK):
        for h in range(2):
            out[f, :, h * HALF : (h + 1) * HALF] = sums[h, pl.ds(f, TILES, stride=FIELDS), :]


SMEM = pl.BlockSpec(memory_space=pltpu.SMEM)
VMEM = pl.BlockSpec(memory_space=pltpu.VMEM)
HBM = pl.BlockSpec(memory_space=pltpu.HBM)


def on_device(sky, weights, sky_block, target_device, sea_block, sst, marine):
    devices = lax.axis_size(("gx", "gy"))
    chips = devices // CORES
    rows = devices * SLOTS * 2
    params = pltpu.CompilerParams(vmem_limit_bytes=VMEM_LIMIT)
    target = target_device.reshape(1, PAIRS)
    sea = sea_block.reshape(1, PAIRS)
    same_core = [list(range(core, devices, CORES)) for core in range(CORES)]

    def swap(x):
        width = x.shape[1]
        y = lax.all_to_all(
            x.reshape(chips, rows // chips, width),
            ("gx", "gy"),
            split_axis=0,
            concat_axis=0,
            axis_index_groups=same_core,
            tiled=True,
        )
        return y.reshape(rows, width)

    def other_core(x):
        return lax.ppermute(x, ("gx", "gy"), [(d, d ^ 1) for d in range(devices)])

    outgoing = pl.pallas_call(
        contribute,
        out_shape=jax.ShapeDtypeStruct((rows, SENT * HALF), BF),
        in_specs=[HBM] * 5,
        out_specs=VMEM,
        scratch_shapes=[
            pltpu.SMEM((PAIRS,), jnp.int32),
            pltpu.VMEM((1, PAIRS), jnp.int32),
            pltpu.VMEM((1, PAIRS), jnp.int32),
            pltpu.VMEM((TILES, FIELDS, CELLS), BF),
            pltpu.VMEM((PAIRS, CELLS, CELLS), BF),
            pltpu.VMEM((2, PAIRS * FIELDS, HALF), F32),
            pltpu.SemaphoreType.DMA((4 + PAIRS // GROUP,)),
        ],
        compiler_params=params,
    )(sky_block, target, sea, sky, weights)
    sst_other, marine_other = other_core(sst), other_core(marine)
    partial, chosen = pl.pallas_call(
        combine,
        out_shape=(
            jax.ShapeDtypeStruct((CHIP_ROWS, (SENT - 1) * HALF), F32),
            jax.ShapeDtypeStruct((rows, CHIP_ROWS), BF),
        ),
        in_specs=[VMEM],
        out_specs=(VMEM, VMEM),
        compiler_params=params,
    )(swap(outgoing))
    fluxes, back = pl.pallas_call(
        exchange,
        out_shape=(
            jax.ShapeDtypeStruct((4, TILES, CELLS), F32),
            jax.ShapeDtypeStruct((rows, BACK * HALF), BF),
        ),
        in_specs=[VMEM] * 7,
        out_specs=(VMEM, VMEM),
        compiler_params=params,
    )(partial, other_core(partial), chosen, sst, sst_other, marine, marine_other)
    atm_back = pl.pallas_call(
        deliver,
        out_shape=jax.ShapeDtypeStruct((BACK, TILES, CELLS), F32),
        in_specs=[SMEM] + [VMEM] * 3,
        out_specs=VMEM,
        scratch_shapes=[
            pltpu.VMEM((2, PAIRS * FIELDS, HALF), F32),
            pltpu.VMEM((2, TILES * FIELDS, HALF), F32),
        ],
        compiler_params=params,
    )(sky_block, target, swap(back), weights)
    return jnp.transpose(fluxes, (1, 0, 2)), jnp.transpose(atm_back, (1, 0, 2))


def solution(mesh):
    tiles = P(("gx", "gy"), None, None)
    cells = P(("gx", "gy"), None)
    flat = P(("gx", "gy"))
    return jax.shard_map(
        on_device,
        mesh=mesh,
        in_specs=(tiles, tiles, flat, cells, flat, cells, cells),
        out_specs=(tiles, tiles),
        check_vma=False,
    )
```

```python
import jax
import jax.numpy as jnp
from jax import lax
from jax.experimental import pallas as pl
from jax.experimental.pallas import tpu as pltpu
from jax.sharding import PartitionSpec as P

PAIRS = 16
TILES = 16
FIELDS = 8
CELLS = 256
HALF = 128
SLOTS = 2
SENT = 7
BACK = 5
CORES = 2
CHIP_ROWS = CORES * 2 * TILES
GROUP = 4
BF = jnp.bfloat16
F32 = jnp.float32
VMEM_LIMIT = 24 * 1024 * 1024


def iota(shape, dim):
    return lax.broadcasted_iota(jnp.int32, shape, dim)


def halves_to_rows(plane):
    return jnp.concatenate([plane[:, :HALF], plane[:, HALF:]], axis=0)


def field_rows(scratch, f):
    parts = [scratch[h, pl.ds(f, PAIRS, stride=FIELDS), :] for h in range(2)]
    return jnp.concatenate(parts, axis=0)


def slot_column(target_row):
    row = target_row.astype(F32)
    later, other = iota((PAIRS, PAIRS), 0), iota((PAIRS, PAIRS), 1)
    column = jnp.sum(jnp.where(later == other, row, 0.0), axis=1, keepdims=True)
    earlier = jnp.where((column == row) & (other < later), 1.0, 0.0)
    return SLOTS * column + jnp.sum(earlier, axis=1, keepdims=True)


def contribute(
    src_hbm, target_hbm, sea_hbm, sky_hbm, weights_hbm, out,
    src, target, sea, sky, weights, scratch, sems,
):
    rows = out.shape[0]
    small = ((src_hbm, src), (sky_hbm, sky), (target_hbm, target), (sea_hbm, sea))
    copies = [pltpu.make_async_copy(a, b, sems.at[i]) for i, (a, b) in enumerate(small)]
    for i in range(PAIRS // GROUP):
        part = pl.ds(i * GROUP, GROUP)
        copies.append(
            pltpu.make_async_copy(weights_hbm.at[part], weights.at[part], sems.at[len(small) + i])
        )
    for copy in copies:
        copy.start()
    for copy in copies[: len(small)]:
        copy.wait()
    core = lax.axis_index("gy") % CORES
    for p in range(PAIRS):
        if p % GROUP == 0:
            copies[len(small) + p // GROUP].wait()
        term = jnp.dot(sky[src[p]], weights[p], preferred_element_type=F32)
        for h in range(2):
            scratch[h, p * FIELDS : (p + 1) * FIELDS, :] = term[:, h * HALF : (h + 1) * HALF]
    u, v, ta, qa, sw, lw, pr, ps = (field_rows(scratch, f) for f in range(FIELDS))
    sent = [x.astype(BF) for x in (u, v, ta, qa - 0.3 * ps, 0.5 * sw + 0.3 * lw, pr)]
    both = 2 * PAIRS
    mine = (iota((both, PAIRS), 0) % PAIRS) == iota((both, PAIRS), 1)
    tile = jnp.sum(jnp.where(mine, sea[...].astype(F32), 0.0), axis=1, keepdims=True)
    owner = jnp.sum(jnp.where(mine, target[...].astype(F32), 0.0), axis=1, keepdims=True)
    other = (owner.astype(jnp.int32) + core) % CORES * (2 * TILES)
    label = tile + (other + iota((both, 1), 0) // PAIRS * TILES + 1).astype(F32)
    rest = u - sent[0].astype(F32)
    sent.append(jnp.where(iota((both, HALF), 1) == 0, label, rest).astype(BF))
    slot = slot_column(target[...])
    pair = iota((PAIRS, both), 1) % PAIRS == iota((PAIRS, both), 0)
    place = 2.0 * jnp.sum(jnp.where(pair, slot, 0.0), axis=0, keepdims=True)
    place = place.astype(jnp.int32) + iota((1, both), 1) // PAIRS
    chosen = jnp.where(iota((rows, both), 0) == place, 1.0, 0.0).astype(BF)
    out[...] = jnp.dot(chosen, jnp.concatenate(sent, axis=1), preferred_element_type=F32).astype(BF)


def combine(arrived, sst, marine, partial, chosen):
    rows = arrived.shape[0]
    label = arrived[:, (SENT - 1) * HALF :].astype(F32)[:, :1].astype(jnp.int32)
    chosen[...] = jnp.where(label == iota((rows, CHIP_ROWS), 1) + 1, 1.0, 0.0).astype(BF)
    total = lax.dot_general(
        chosen[...], arrived[...], (((0,), (0,)), ((), ())), preferred_element_type=F32
    )
    partial[:, : (SENT - 1) * HALF] = total[:, : (SENT - 1) * HALF]
    partial[: CHIP_ROWS // CORES, (SENT - 1) * HALF :] = halves_to_rows(sst[...])
    partial[CHIP_ROWS // CORES :, (SENT - 1) * HALF :] = halves_to_rows(marine[...].astype(F32))
    rest = total[:, (SENT - 1) * HALF :]
    partial[:, :HALF] += jnp.where(iota((CHIP_ROWS, HALF), 1) == 0, 0.0, rest)


def exchange(own, swapped, chosen, fluxes, out):
    both = 2 * TILES
    sums = (SENT - 1) * HALF
    total = own[:, :sums] + jnp.concatenate([swapped[both:, :sums], swapped[:both, :sums]], axis=0)
    u, v, ta, q, rad, pr = (total[:, f * HALF : (f + 1) * HALF] for f in range(SENT - 1))
    sst_rows = jnp.concatenate([own[:both, sums:], swapped[:both, sums:]], axis=0)
    w = jnp.concatenate([own[both:, sums:], swapped[both:, sums:]], axis=0)
    square = u * u + v * v + 0.25
    speed = jnp.sqrt(square)
    dth = sst_rows - ta
    dq = 0.4 * sst_rows - q
    lift = 2.0 * (dth + 0.5 * dq)
    c = jnp.ones_like(speed)
    for _ in range(3):
        c = 1.0 + 0.5 * jnp.tanh(lift / (1.0 + c * speed * speed))
    k = c * speed
    found = (k * u * w, k * v * w, (rad - k * dth - k * dq) * w, (pr - 0.5 * k * dq) * w)
    for f, x in enumerate(found):
        fluxes[:, f, :HALF] = x[:TILES]
        fluxes[:, f, HALF:] = x[TILES:both]
    back = jnp.concatenate([x.astype(BF) for x in found + (sst_rows * w,)], axis=1)
    out[...] = jnp.dot(chosen[...], back, preferred_element_type=F32).astype(BF)


def deliver(src, target, returned, weights, out, values, sums):
    rows = returned.shape[0]
    both = 2 * PAIRS
    slot = slot_column(target[...])
    place = jnp.concatenate([2.0 * slot, 2.0 * slot + 1.0], axis=0).astype(jnp.int32)
    chosen = jnp.where(iota((both, rows), 1) == place, 1.0, 0.0).astype(BF)
    picked = jnp.dot(chosen, returned[...], preferred_element_type=F32)
    values[...] = jnp.zeros_like(values)
    for f in range(BACK):
        for h in range(2):
            part = picked[h * PAIRS : (h + 1) * PAIRS, f * HALF : (f + 1) * HALF]
            values[h, pl.ds(f, PAIRS, stride=FIELDS), :] = part
    sums[...] = jnp.zeros_like(sums)
    for p in range(PAIRS):
        block = pl.ds(p * FIELDS, FIELDS)
        term = lax.dot_general(
            jnp.concatenate([values[h, block, :] for h in range(2)], axis=1).astype(BF),
            weights[p],
            (((1,), (1,)), ((), ())),
            preferred_element_type=F32,
        )
        at = pl.ds(pl.multiple_of(src[p] * FIELDS, FIELDS), FIELDS)
        for h in range(2):
            sums[h, at, :] += term[:, h * HALF : (h + 1) * HALF]
    for f in range(BACK):
        for h in range(2):
            out[f, :, h * HALF : (h + 1) * HALF] = sums[h, pl.ds(f, TILES, stride=FIELDS), :]


SMEM = pl.BlockSpec(memory_space=pltpu.SMEM)
VMEM = pl.BlockSpec(memory_space=pltpu.VMEM)
HBM = pl.BlockSpec(memory_space=pltpu.HBM)


def on_device(sky, weights, sky_block, target_device, sea_block, sst, marine):
    devices = lax.axis_size(("gx", "gy"))
    chips = devices // CORES
    rows = devices * SLOTS * 2
    params = pltpu.CompilerParams(vmem_limit_bytes=VMEM_LIMIT)
    target = target_device.reshape(1, PAIRS)
    sea = sea_block.reshape(1, PAIRS)
    inputs = (sky_block, target, sea, sky, weights)
    same_core = [list(range(core, devices, CORES)) for core in range(CORES)]

    def swap(x):
        width = x.shape[1]
        y = lax.all_to_all(
            x.reshape(chips, rows // chips, width),
            ("gx", "gy"),
            split_axis=0,
            concat_axis=0,
            axis_index_groups=same_core,
            tiled=True,
        )
        return y.reshape(rows, width)

    def other_core(x):
        return lax.ppermute(x, ("gx", "gy"), [(d, d ^ 1) for d in range(devices)])

    outgoing = pl.pallas_call(
        contribute,
        out_shape=jax.ShapeDtypeStruct((rows, SENT * HALF), BF),
        in_specs=[HBM] * 5,
        out_specs=VMEM,
        scratch_shapes=[
            pltpu.SMEM((PAIRS,), jnp.int32),
            pltpu.VMEM((1, PAIRS), jnp.int32),
            pltpu.VMEM((1, PAIRS), jnp.int32),
            pltpu.VMEM((TILES, FIELDS, CELLS), BF),
            pltpu.VMEM((PAIRS, CELLS, CELLS), BF),
            pltpu.VMEM((2, PAIRS * FIELDS, HALF), F32),
            pltpu.SemaphoreType.DMA((4 + PAIRS // GROUP,)),
        ],
        compiler_params=params,
    )(*(pltpu.with_memory_space_constraint(x, pltpu.HBM) for x in inputs))
    partial, chosen = pl.pallas_call(
        combine,
        out_shape=(
            jax.ShapeDtypeStruct((CHIP_ROWS, SENT * HALF), F32),
            jax.ShapeDtypeStruct((rows, CHIP_ROWS), BF),
        ),
        in_specs=[VMEM] * 3,
        out_specs=(VMEM, VMEM),
        compiler_params=params,
    )(swap(outgoing), sst, marine)
    fluxes, back = pl.pallas_call(
        exchange,
        out_shape=(
            jax.ShapeDtypeStruct((TILES, 4, CELLS), F32),
            jax.ShapeDtypeStruct((rows, BACK * HALF), BF),
        ),
        in_specs=[VMEM] * 3,
        out_specs=(VMEM, VMEM),
        compiler_params=params,
    )(partial, other_core(partial), chosen)
    atm_back = pl.pallas_call(
        deliver,
        out_shape=jax.ShapeDtypeStruct((BACK, TILES, CELLS), F32),
        in_specs=[SMEM] + [VMEM] * 3,
        out_specs=VMEM,
        scratch_shapes=[
            pltpu.VMEM((2, PAIRS * FIELDS, HALF), F32),
            pltpu.VMEM((2, TILES * FIELDS, HALF), F32),
        ],
        compiler_params=params,
    )(sky_block, target, swap(back), weights)
    return fluxes, jnp.transpose(atm_back, (1, 0, 2))


def solution(mesh):
    tiles = P(("gx", "gy"), None, None)
    cells = P(("gx", "gy"), None)
    flat = P(("gx", "gy"))
    return jax.shard_map(
        on_device,
        mesh=mesh,
        in_specs=(tiles, tiles, flat, cells, flat, cells, cells),
        out_specs=(tiles, tiles),
        check_vma=False,
    )
```

```python
import jax
import jax.numpy as jnp
from jax import lax
from jax.experimental import pallas as pl
from jax.experimental.pallas import tpu as pltpu
from jax.sharding import PartitionSpec as P

PAIRS = 16
TILES = 16
FIELDS = 8
CELLS = 256
HALF = 128
SLOTS = 2
SENT = 7
BACK = 5
ROWS_DEST = 2 * SLOTS
GROUP = 4
BF = jnp.bfloat16
F32 = jnp.float32
VMEM_LIMIT = 24 * 1024 * 1024


def iota(shape, dim):
    return lax.broadcasted_iota(jnp.int32, shape, dim)


def halves_to_rows(plane):
    return jnp.concatenate([plane[:, :HALF], plane[:, HALF:]], axis=0)


def field_rows(scratch, f):
    parts = [scratch[h, pl.ds(f, PAIRS, stride=FIELDS), :] for h in range(2)]
    return jnp.concatenate(parts, axis=0)


def slot_column(target_row):
    row = target_row.astype(F32)
    later, other = iota((PAIRS, PAIRS), 0), iota((PAIRS, PAIRS), 1)
    column = jnp.sum(jnp.where(later == other, row, 0.0), axis=1, keepdims=True)
    earlier = jnp.where((column == row) & (other < later), 1.0, 0.0)
    return SLOTS * column + jnp.sum(earlier, axis=1, keepdims=True)


def contribute(
    src_hbm, target_hbm, sea_hbm, sky_hbm, weights_hbm, out,
    src, target, sea, sky, weights, scratch, sems,
):
    rows = out.shape[0] * out.shape[1]
    small = ((src_hbm, src), (sky_hbm, sky), (target_hbm, target), (sea_hbm, sea))
    copies = [pltpu.make_async_copy(a, b, sems.at[i]) for i, (a, b) in enumerate(small)]
    for i in range(PAIRS // GROUP):
        part = pl.ds(i * GROUP, GROUP)
        copies.append(
            pltpu.make_async_copy(weights_hbm.at[part], weights.at[part], sems.at[len(small) + i])
        )
    for copy in copies:
        copy.start()
    for copy in copies[: len(small)]:
        copy.wait()
    for p in range(PAIRS):
        if p % GROUP == 0:
            copies[len(small) + p // GROUP].wait()
        term = jnp.dot(sky[src[p]], weights[p], preferred_element_type=F32)
        for h in range(2):
            scratch[h, p * FIELDS : (p + 1) * FIELDS, :] = term[:, h * HALF : (h + 1) * HALF]
    u, v, ta, qa, sw, lw, pr, ps = (field_rows(scratch, f) for f in range(FIELDS))
    sent = [x.astype(BF) for x in (u, v, ta, qa - 0.3 * ps, 0.5 * sw + 0.3 * lw, pr)]
    both = 2 * PAIRS
    mine = (iota((both, PAIRS), 0) % PAIRS) == iota((both, PAIRS), 1)
    tile = jnp.sum(jnp.where(mine, sea[...].astype(F32), 0.0), axis=1, keepdims=True)
    label = tile + (iota((both, 1), 0) // PAIRS * TILES + 1).astype(F32)
    rest = u - sent[0].astype(F32)
    sent.append(jnp.where(iota((both, HALF), 1) == 0, label, rest).astype(BF))
    slot = slot_column(target[...])
    pair = iota((PAIRS, both), 1) % PAIRS == iota((PAIRS, both), 0)
    place = 2.0 * jnp.sum(jnp.where(pair, slot, 0.0), axis=0, keepdims=True)
    place = place.astype(jnp.int32) + iota((1, both), 1) // PAIRS
    chosen = jnp.where(iota((rows, both), 0) == place, 1.0, 0.0).astype(BF)
    filled = jnp.dot(chosen, jnp.concatenate(sent, axis=1), preferred_element_type=F32)
    out[...] = filled.astype(BF).reshape(out.shape)


def exchange(arrived, sst, marine, fluxes, out):
    rows = arrived.shape[0] * arrived.shape[1]
    both = 2 * TILES
    slots = arrived[...].reshape(rows, SENT * HALF)
    label = slots[:, (SENT - 1) * HALF :].astype(F32)[:, :1].astype(jnp.int32)
    chosen = jnp.where(label == iota((rows, both), 1) + 1, 1.0, 0.0).astype(BF)
    total = lax.dot_general(chosen, slots, (((0,), (0,)), ((), ())), preferred_element_type=F32)
    u, v, ta, q, rad, pr, rest = (total[:, f * HALF : (f + 1) * HALF] for f in range(SENT))
    u = u + jnp.where(iota((both, HALF), 1) == 0, 0.0, rest)
    sst_rows = halves_to_rows(sst[...])
    w = halves_to_rows(marine[...].astype(F32))
    square = u * u + v * v + 0.25
    speed = jnp.sqrt(square)
    dth = sst_rows - ta
    dq = 0.4 * sst_rows - q
    lift = 2.0 * (dth + 0.5 * dq)
    c = jnp.ones_like(speed)
    for _ in range(3):
        c = 1.0 + 0.5 * jnp.tanh(lift / (1.0 + c * speed * speed))
    k = c * speed
    found = (k * u * w, k * v * w, (rad - k * dth - k * dq) * w, (pr - 0.5 * k * dq) * w)
    for f, x in enumerate(found):
        fluxes[:, f, :HALF] = x[:TILES]
        fluxes[:, f, HALF:] = x[TILES:]
    back = jnp.concatenate([x.astype(BF) for x in found + (sst_rows * w,)], axis=1)
    out[...] = jnp.dot(chosen, back, preferred_element_type=F32).astype(BF).reshape(out.shape)


def deliver(src_hbm, target, returned, weights, fluxes, fluxes_out, out, src, values, sums, sem):
    copy = pltpu.make_async_copy(src_hbm, src, sem)
    copy.start()
    fluxes_out[...] = fluxes[...]
    rows = returned.shape[0] * returned.shape[1]
    both = 2 * PAIRS
    slot = slot_column(target[...])
    place = jnp.concatenate([2.0 * slot, 2.0 * slot + 1.0], axis=0).astype(jnp.int32)
    chosen = jnp.where(iota((both, rows), 1) == place, 1.0, 0.0).astype(BF)
    slots = returned[...].reshape(rows, BACK * HALF)
    picked = jnp.dot(chosen, slots, preferred_element_type=F32)
    values[...] = jnp.zeros_like(values)
    for f in range(BACK):
        for h in range(2):
            part = picked[h * PAIRS : (h + 1) * PAIRS, f * HALF : (f + 1) * HALF]
            values[h, pl.ds(f, PAIRS, stride=FIELDS), :] = part
    sums[...] = jnp.zeros_like(sums)
    copy.wait()
    for p in range(PAIRS):
        block = pl.ds(p * FIELDS, FIELDS)
        term = lax.dot_general(
            jnp.concatenate([values[h, block, :] for h in range(2)], axis=1).astype(BF),
            weights[p],
            (((1,), (1,)), ((), ())),
            preferred_element_type=F32,
        )
        at = pl.ds(pl.multiple_of(src[p] * FIELDS, FIELDS), FIELDS)
        for h in range(2):
            sums[h, at, :] += term[:, h * HALF : (h + 1) * HALF]
    for f in range(BACK):
        for h in range(2):
            out[f, :, h * HALF : (h + 1) * HALF] = sums[h, pl.ds(f, TILES, stride=FIELDS), :]


VMEM = pl.BlockSpec(memory_space=pltpu.VMEM)
HBM = pl.BlockSpec(memory_space=pltpu.HBM)


def on_device(sky, weights, sky_block, target_device, sea_block, sst, marine):
    devices = lax.axis_size(("gx", "gy"))
    params = pltpu.CompilerParams(vmem_limit_bytes=VMEM_LIMIT)
    target = target_device.reshape(1, PAIRS)
    sea = sea_block.reshape(1, PAIRS)
    flux_shape = jax.ShapeDtypeStruct((TILES, 4, CELLS), F32)

    def wire(width):
        return jax.ShapeDtypeStruct((devices, ROWS_DEST, width), BF)

    def swap(x):
        return lax.all_to_all(x, ("gx", "gy"), split_axis=0, concat_axis=0, tiled=True)

    def stay(*arrays):
        return tuple(pltpu.with_memory_space_constraint(x, pltpu.HBM) for x in arrays)

    outgoing = pl.pallas_call(
        contribute,
        out_shape=wire(SENT * HALF),
        in_specs=[HBM] * 5,
        out_specs=VMEM,
        scratch_shapes=[
            pltpu.SMEM((PAIRS,), jnp.int32),
            pltpu.VMEM((1, PAIRS), jnp.int32),
            pltpu.VMEM((1, PAIRS), jnp.int32),
            pltpu.VMEM((TILES, FIELDS, CELLS), BF),
            pltpu.VMEM((PAIRS, CELLS, CELLS), BF),
            pltpu.VMEM((2, PAIRS * FIELDS, HALF), F32),
            pltpu.SemaphoreType.DMA((4 + PAIRS // GROUP,)),
        ],
        compiler_params=params,
    )(*stay(sky_block, target, sea, sky, weights))
    fluxes, back = pl.pallas_call(
        exchange,
        out_shape=(flux_shape, wire(BACK * HALF)),
        in_specs=[VMEM] * 3,
        out_specs=(VMEM, VMEM),
        compiler_params=params,
    )(swap(outgoing), sst, marine)
    fluxes, atm_back = pl.pallas_call(
        deliver,
        out_shape=(flux_shape, jax.ShapeDtypeStruct((BACK, TILES, CELLS), F32)),
        in_specs=[HBM] + [VMEM] * 4,
        out_specs=(VMEM, VMEM),
        scratch_shapes=[
            pltpu.SMEM((PAIRS,), jnp.int32),
            pltpu.VMEM((2, PAIRS * FIELDS, HALF), F32),
            pltpu.VMEM((2, TILES * FIELDS, HALF), F32),
            pltpu.SemaphoreType.DMA,
        ],
        compiler_params=params,
    )(*stay(sky_block), target, swap(back), weights, fluxes)
    return fluxes, jnp.transpose(atm_back, (1, 0, 2))


def solution(mesh):
    tiles = P(("gx", "gy"), None, None)
    cells = P(("gx", "gy"), None)
    flat = P(("gx", "gy"))
    return jax.shard_map(
        on_device,
        mesh=mesh,
        in_specs=(tiles, tiles, flat, cells, flat, cells, cells),
        out_specs=(tiles, tiles),
        check_vma=False,
    )
```

```python
import jax
import jax.numpy as jnp
from jax import lax
from jax.experimental import pallas as pl
from jax.experimental.pallas import tpu as pltpu
from jax.sharding import PartitionSpec as P

PAIRS = 16
TILES = 16
FIELDS = 8
SENT = 6
BACK = 5
CELLS = 256
LANES = 128
SLOTS = 2
GROUP = 4
OUT_WIDTH = SENT * CELLS + LANES
BACK_WIDTH = BACK * CELLS
BF = jnp.bfloat16
F32 = jnp.float32
VMEM_LIMIT = 24 * 1024 * 1024


def iota(shape, dim):
    return lax.broadcasted_iota(jnp.int32, shape, dim)


def to_column(row):
    same = iota((PAIRS, PAIRS), 0) == iota((PAIRS, PAIRS), 1)
    return jnp.sum(jnp.where(same, row, 0.0), axis=1, keepdims=True)


def to_row(column):
    same = iota((PAIRS, PAIRS), 0) == iota((PAIRS, PAIRS), 1)
    return jnp.sum(jnp.where(same, column, 0.0), axis=0, keepdims=True)


def slot_column(target):
    row = target.astype(F32)
    column = to_column(row)
    later, other = iota((PAIRS, PAIRS), 0), iota((PAIRS, PAIRS), 1)
    earlier = jnp.where((column == row) & (other < later), 1.0, 0.0)
    return SLOTS * column + jnp.sum(earlier, axis=1, keepdims=True)


def contribute(
    src_hbm, target_hbm, sea_hbm, sky_hbm, weights_hbm, out,
    src, target, sea, sky, weights, scratch, sems,
):
    rows = out.shape[0] * out.shape[1]
    small = ((target_hbm, target), (sea_hbm, sea), (src_hbm, src), (sky_hbm, sky))
    copies = [pltpu.make_async_copy(a, b, sems.at[i]) for i, (a, b) in enumerate(small)]
    for i in range(PAIRS // GROUP):
        part = pl.ds(i * GROUP, GROUP)
        copies.append(
            pltpu.make_async_copy(weights_hbm.at[part], weights.at[part], sems.at[len(small) + i])
        )
    for copy in copies:
        copy.start()
    for copy in copies[:2]:
        copy.wait()
    place = to_row(slot_column(target[...])).astype(jnp.int32)
    chosen = jnp.where(iota((rows, PAIRS), 0) == place, 1.0, 0.0).astype(BF)
    label = to_column(sea[...].astype(F32)) + 1.0
    for copy in copies[2 : len(small)]:
        copy.wait()
    for p in range(PAIRS):
        if p % GROUP == 0:
            copies[len(small) + p // GROUP].wait()
        term = jnp.dot(sky[src[p]], weights[p], preferred_element_type=F32)
        for h in range(2):
            scratch[h, p * FIELDS : (p + 1) * FIELDS, :] = term[:, h * LANES : (h + 1) * LANES]

    def field(f):
        parts = [scratch[h, pl.ds(f, PAIRS, stride=FIELDS), :] for h in range(2)]
        return jnp.concatenate(parts, axis=1)

    u, v, ta, qa, sw, lw, pr, ps = (field(f) for f in range(FIELDS))
    sent = [x.astype(BF) for x in (u, v, ta, qa - 0.3 * ps, 0.5 * sw + 0.3 * lw, pr)]
    rest = (u - sent[0].astype(F32))[:, :LANES]
    sent.append(jnp.where(iota((PAIRS, LANES), 1) == 0, label, rest).astype(BF))
    filled = jnp.dot(chosen, jnp.concatenate(sent, axis=1), preferred_element_type=F32)
    out[...] = filled.astype(BF).reshape(out.shape)


def exchange(arrived, sst, marine, fluxes, out):
    rows = arrived.shape[0] * arrived.shape[1]
    slots = arrived[...].reshape(rows, OUT_WIDTH)
    label = slots[:, SENT * CELLS :].astype(F32)[:, :1].astype(jnp.int32)
    chosen = jnp.where(label == iota((rows, TILES), 1) + 1, 1.0, 0.0).astype(BF)
    total = lax.dot_general(chosen, slots, (((0,), (0,)), ((), ())), preferred_element_type=F32)
    u, v, ta, q, rad, pr = (total[:, f * CELLS : (f + 1) * CELLS] for f in range(SENT))
    rest = jnp.where(iota((TILES, LANES), 1) == 0, 0.0, total[:, SENT * CELLS :])
    u = jnp.concatenate([u[:, :LANES] + rest, u[:, LANES:]], axis=1)
    warmth = sst[...]
    w = marine[...].astype(F32)
    speed = jnp.sqrt(u * u + v * v + 0.25)
    dth = warmth - ta
    dq = 0.4 * warmth - q
    lift = 2.0 * (dth + 0.5 * dq)
    c = jnp.ones_like(speed)
    for _ in range(3):
        c = 1.0 + 0.5 * jnp.tanh(lift / (1.0 + c * speed * speed))
    k = c * speed
    found = (k * u * w, k * v * w, (rad - k * dth - k * dq) * w, (pr - 0.5 * k * dq) * w)
    for f, x in enumerate(found):
        fluxes[:, f, :] = x
    back = jnp.concatenate([x.astype(BF) for x in found + (warmth * w,)], axis=1)
    out[...] = jnp.dot(chosen, back, preferred_element_type=F32).astype(BF).reshape(out.shape)


def deliver(
    src_hbm, target, returned, weights, fluxes, fluxes_hbm, out, src, values, sums, sems
):
    copies = [
        pltpu.make_async_copy(src_hbm, src, sems.at[0]),
        pltpu.make_async_copy(fluxes, fluxes_hbm, sems.at[1]),
    ]
    for copy in copies:
        copy.start()
    rows = returned.shape[0] * returned.shape[1]
    place = slot_column(target[...]).astype(jnp.int32)
    chosen = jnp.where(iota((PAIRS, rows), 1) == place, 1.0, 0.0).astype(BF)
    slots = returned[...].reshape(rows, BACK_WIDTH)
    picked = jnp.dot(chosen, slots, preferred_element_type=F32)
    values[...] = jnp.zeros_like(values)
    for f in range(BACK):
        for h in range(2):
            start = f * CELLS + h * LANES
            values[h, pl.ds(f, PAIRS, stride=FIELDS), :] = picked[:, start : start + LANES]
    sums[...] = jnp.zeros_like(sums)
    copies[0].wait()
    for p in range(PAIRS):
        block = pl.ds(p * FIELDS, FIELDS)
        term = lax.dot_general(
            jnp.concatenate([values[h, block, :] for h in range(2)], axis=1).astype(BF),
            weights[p],
            (((1,), (1,)), ((), ())),
            preferred_element_type=F32,
        )
        at = pl.ds(pl.multiple_of(src[p] * FIELDS, FIELDS), FIELDS)
        for h in range(2):
            sums[h, at, :] += term[:, h * LANES : (h + 1) * LANES]
    for f in range(BACK):
        for h in range(2):
            out[f, :, h * LANES : (h + 1) * LANES] = sums[h, pl.ds(f, TILES, stride=FIELDS), :]
    copies[1].wait()


VMEM = pl.BlockSpec(memory_space=pltpu.VMEM)
HBM = pl.BlockSpec(memory_space=pltpu.HBM)


def on_device(sky, weights, sky_block, target_device, sea_block, sst, marine):
    devices = lax.axis_size(("gx", "gy"))
    params = pltpu.CompilerParams(vmem_limit_bytes=VMEM_LIMIT)
    target = target_device.reshape(1, PAIRS)
    sea = sea_block.reshape(1, PAIRS)
    flux_shape = jax.ShapeDtypeStruct((TILES, 4, CELLS), F32)

    def wire(width):
        return jax.ShapeDtypeStruct((devices, SLOTS, width), BF)

    def swap(x):
        return lax.all_to_all(x, ("gx", "gy"), split_axis=0, concat_axis=0, tiled=True)

    def stay(*arrays):
        return tuple(pltpu.with_memory_space_constraint(x, pltpu.HBM) for x in arrays)

    outgoing = pl.pallas_call(
        contribute,
        out_shape=wire(OUT_WIDTH),
        in_specs=[HBM] * 5,
        out_specs=VMEM,
        scratch_shapes=[
            pltpu.SMEM((PAIRS,), jnp.int32),
            pltpu.VMEM((1, PAIRS), jnp.int32),
            pltpu.VMEM((1, PAIRS), jnp.int32),
            pltpu.VMEM((TILES, FIELDS, CELLS), BF),
            pltpu.VMEM((PAIRS, CELLS, CELLS), BF),
            pltpu.VMEM((2, PAIRS * FIELDS, LANES), F32),
            pltpu.SemaphoreType.DMA((4 + PAIRS // GROUP,)),
        ],
        compiler_params=params,
    )(*stay(sky_block, target, sea, sky, weights))
    fluxes, back = pl.pallas_call(
        exchange,
        out_shape=(flux_shape, wire(BACK_WIDTH)),
        in_specs=[VMEM] * 3,
        out_specs=(VMEM, VMEM),
        compiler_params=params,
    )(swap(outgoing), sst, marine)
    fluxes, atm_back = pl.pallas_call(
        deliver,
        out_shape=(flux_shape, jax.ShapeDtypeStruct((BACK, TILES, CELLS), F32)),
        in_specs=[HBM] + [VMEM] * 4,
        out_specs=(HBM, VMEM),
        scratch_shapes=[
            pltpu.SMEM((PAIRS,), jnp.int32),
            pltpu.VMEM((2, PAIRS * FIELDS, LANES), F32),
            pltpu.VMEM((2, TILES * FIELDS, LANES), F32),
            pltpu.SemaphoreType.DMA((2,)),
        ],
        compiler_params=params,
    )(*stay(sky_block), target, swap(back), weights, fluxes)
    return fluxes, jnp.transpose(atm_back, (1, 0, 2))


def solution(mesh):
    tiles = P(("gx", "gy"), None, None)
    cells = P(("gx", "gy"), None)
    flat = P(("gx", "gy"))
    return jax.shard_map(
        on_device,
        mesh=mesh,
        in_specs=(tiles, tiles, flat, cells, flat, cells, cells),
        out_specs=(tiles, tiles),
        check_vma=False,
    )
```

```python
import jax
import jax.numpy as jnp
from jax import lax
from jax.experimental import pallas as pl
from jax.experimental.pallas import tpu as pltpu
from jax.sharding import PartitionSpec as P

PAIRS = 16
TILES = 16
FIELDS = 8
SENT = 6
BACK = 5
CELLS = 256
LANES = 128
SLOTS = 2
STRIP = 16
OUT_WIDTH = SENT * CELLS + LANES
BACK_WIDTH = BACK * CELLS
BF = jnp.bfloat16
F32 = jnp.float32
VMEM_LIMIT = 24 * 1024 * 1024


def iota(shape, dim):
    return lax.broadcasted_iota(jnp.int32, shape, dim)


def to_column(row):
    same = iota((PAIRS, PAIRS), 0) == iota((PAIRS, PAIRS), 1)
    return jnp.sum(jnp.where(same, row, 0.0), axis=1, keepdims=True)


def to_row(column):
    same = iota((PAIRS, PAIRS), 0) == iota((PAIRS, PAIRS), 1)
    return jnp.sum(jnp.where(same, column, 0.0), axis=0, keepdims=True)


def slot_column(target):
    row = target.astype(F32)
    column = to_column(row)
    later, other = iota((PAIRS, PAIRS), 0), iota((PAIRS, PAIRS), 1)
    earlier = jnp.where((column == row) & (other < later), 1.0, 0.0)
    return SLOTS * column + jnp.sum(earlier, axis=1, keepdims=True)


def contribute(
    src_hbm, owner_hbm, sea_hbm, sky_hbm, weights_hbm, sst_hbm, marine_hbm, out, sst, marine,
    src, owner, sea, sky, blocks, top, middle, bottom, scratch, sems,
):
    copies = {}

    def fetch(name, source, held):
        copies[name] = pltpu.make_async_copy(source, held, sems.at[len(copies)])
        copies[name].start()

    left, right = pl.ds(0, LANES), pl.ds(LANES, LANES)
    every = pl.ds(0, PAIRS)
    fetch("upper", weights_hbm.at[every, left, left], blocks.at[0])
    fetch("lower", weights_hbm.at[every, right, right], blocks.at[1])
    fetch("top", weights_hbm.at[every, pl.ds(0, STRIP), right], top)
    fetch("middle", weights_hbm.at[every, pl.ds(LANES - STRIP, 2 * STRIP)], middle)
    fetch("bottom", weights_hbm.at[every, pl.ds(CELLS - STRIP, STRIP), left], bottom)
    fetch("owner", owner_hbm, owner)
    fetch("sea", sea_hbm, sea)
    fetch("src", src_hbm, src)
    fetch("sky", sky_hbm, sky)
    fetch("sst", sst_hbm, sst)
    fetch("marine", marine_hbm, marine)
    out[...] = jnp.zeros_like(out)
    copies["owner"].wait()
    copies["sea"].wait()
    at = iota((PAIRS, PAIRS), 1)
    row = jnp.zeros((PAIRS, PAIRS), jnp.int32)
    tiles = jnp.zeros((PAIRS, LANES), jnp.int32)
    for p in range(PAIRS):
        row = jnp.where(at == p, owner[p], row)
        tiles = jnp.where(iota((PAIRS, LANES), 0) == p, sea[p], tiles)
    row = row[:1].astype(F32)
    column = to_column(row)
    before = at < iota((PAIRS, PAIRS), 0)
    rank = jnp.sum(jnp.where((column == row) & before, 1.0, 0.0), axis=1, keepdims=True)
    both = SLOTS * PAIRS
    wanted, pair = iota((both, PAIRS), 0), iota((both, PAIRS), 1)
    mine = jnp.sum(jnp.where(wanted // SLOTS == pair, row, 0.0), axis=1, keepdims=True)
    fits = (mine == row) & ((wanted % SLOTS).astype(F32) == to_row(rank))
    chosen = jnp.where(fits, 1.0, 0.0).astype(BF)
    label = tiles.astype(F32) + 1.0
    for name in ("src", "sky", "top", "middle", "bottom", "upper", "lower"):
        copies[name].wait()
    gap = jnp.zeros((LANES - 2 * STRIP, LANES), BF)
    for p in range(PAIRS):
        upper = jnp.concatenate([top[p], gap, middle[p, :STRIP, LANES:]], axis=0)
        lower = jnp.concatenate([middle[p, STRIP:, :LANES], gap, bottom[p]], axis=0)
        weights = jnp.concatenate(
            [
                jnp.concatenate([blocks[0, p], upper], axis=1),
                jnp.concatenate([lower, blocks[1, p]], axis=1),
            ],
            axis=0,
        )
        term = jnp.dot(sky[src[p]], weights, preferred_element_type=F32)
        for h in range(2):
            scratch[h, p * FIELDS : (p + 1) * FIELDS, :] = term[:, h * LANES : (h + 1) * LANES]

    def field(f):
        parts = [scratch[h, pl.ds(f, PAIRS, stride=FIELDS), :] for h in range(2)]
        return jnp.concatenate(parts, axis=1)

    u, v, ta, qa, sw, lw, pr, ps = (field(f) for f in range(FIELDS))
    sent = [x.astype(BF) for x in (u, v, ta, qa - 0.3 * ps, 0.5 * sw + 0.3 * lw, pr)]
    rest = (u - sent[0].astype(F32))[:, :LANES]
    sent.append(jnp.where(iota((PAIRS, LANES), 1) == 0, label, rest).astype(BF))
    filled = jnp.dot(chosen, jnp.concatenate(sent, axis=1), preferred_element_type=F32)
    filled = filled.astype(BF).reshape(PAIRS, SLOTS, OUT_WIDTH)
    for p in range(PAIRS):
        out[owner[p]] = filled[p]
    copies["sst"].wait()
    copies["marine"].wait()


def exchange(arrived, sst, marine, fluxes, out):
    rows = arrived.shape[0] * arrived.shape[1]
    slots = arrived[...].reshape(rows, OUT_WIDTH)
    label = slots[:, SENT * CELLS :].astype(F32)[:, :1].astype(jnp.int32)
    chosen = jnp.where(label == iota((rows, TILES), 1) + 1, 1.0, 0.0).astype(BF)
    total = lax.dot_general(chosen, slots, (((0,), (0,)), ((), ())), preferred_element_type=F32)
    u, v, ta, q, rad, pr = (total[:, f * CELLS : (f + 1) * CELLS] for f in range(SENT))
    rest = jnp.where(iota((TILES, LANES), 1) == 0, 0.0, total[:, SENT * CELLS :])
    u = jnp.concatenate([u[:, :LANES] + rest, u[:, LANES:]], axis=1)
    warmth = sst[...]
    w = marine[...].astype(F32)
    speed = jnp.sqrt(u * u + v * v + 0.25)
    dth = warmth - ta
    dq = 0.4 * warmth - q
    lift = 2.0 * (dth + 0.5 * dq)
    c = jnp.ones_like(speed)
    for _ in range(3):
        c = 1.0 + 0.5 * jnp.tanh(lift / (1.0 + c * speed * speed))
    k = c * speed
    found = (k * u * w, k * v * w, (rad - k * dth - k * dq) * w, (pr - 0.5 * k * dq) * w)
    for f, x in enumerate(found):
        fluxes[:, f, :] = x
    back = jnp.concatenate([x.astype(BF) for x in found + (warmth * w,)], axis=1)
    out[...] = jnp.dot(chosen, back, preferred_element_type=F32).astype(BF).reshape(out.shape)


def deliver(
    src_row, target, returned, weights, fluxes, fluxes_hbm, out, src, values, terms, sums, sems
):
    copies = [
        pltpu.make_async_copy(src_row, src, sems.at[0]),
        pltpu.make_async_copy(fluxes, fluxes_hbm, sems.at[1]),
    ]
    for copy in copies:
        copy.start()
    rows = returned.shape[0] * returned.shape[1]
    place = slot_column(target[...]).astype(jnp.int32)
    chosen = jnp.where(iota((PAIRS, rows), 1) == place, 1.0, 0.0).astype(BF)
    slots = returned[...].reshape(rows, BACK_WIDTH)
    picked = jnp.dot(chosen, slots, preferred_element_type=F32)
    values[...] = jnp.zeros_like(values)
    for f in range(BACK):
        for h in range(2):
            start = f * CELLS + h * LANES
            values[h, pl.ds(f, PAIRS, stride=FIELDS), :] = picked[:, start : start + LANES]
    sums[...] = jnp.zeros_like(sums)
    for p in range(PAIRS):
        block = pl.ds(p * FIELDS, FIELDS)
        term = lax.dot_general(
            jnp.concatenate([values[h, block, :] for h in range(2)], axis=1).astype(BF),
            weights[p],
            (((1,), (1,)), ((), ())),
            preferred_element_type=F32,
        )
        for h in range(2):
            terms[h, block, :] = term[:, h * LANES : (h + 1) * LANES]
    copies[0].wait()
    for p in range(PAIRS):
        block = pl.ds(p * FIELDS, FIELDS)
        at = pl.ds(pl.multiple_of(src[p] * FIELDS, FIELDS), FIELDS)
        for h in range(2):
            sums[h, at, :] += terms[h, block, :]
    for f in range(BACK):
        for h in range(2):
            out[f, :, h * LANES : (h + 1) * LANES] = sums[h, pl.ds(f, TILES, stride=FIELDS), :]
    copies[1].wait()


VMEM = pl.BlockSpec(memory_space=pltpu.VMEM)
HBM = pl.BlockSpec(memory_space=pltpu.HBM)


def on_device(sky, weights, sky_block, target_device, sea_block, sst, marine):
    devices = lax.axis_size(("gx", "gy"))
    params = pltpu.CompilerParams(vmem_limit_bytes=VMEM_LIMIT)
    target = target_device.reshape(1, PAIRS)
    flux_shape = jax.ShapeDtypeStruct((TILES, 4, CELLS), F32)

    def wire(width):
        return jax.ShapeDtypeStruct((devices, SLOTS, width), BF)

    def swap(x):
        return lax.all_to_all(x, ("gx", "gy"), split_axis=0, concat_axis=0, tiled=True)

    def stay(*arrays):
        return tuple(pltpu.with_memory_space_constraint(x, pltpu.HBM) for x in arrays)

    outgoing, sst, marine = pl.pallas_call(
        contribute,
        out_shape=(
            wire(OUT_WIDTH),
            jax.ShapeDtypeStruct((TILES, CELLS), F32),
            jax.ShapeDtypeStruct((TILES, CELLS), jnp.int32),
        ),
        in_specs=[HBM] * 7,
        out_specs=(VMEM,) * 3,
        scratch_shapes=[
            pltpu.SMEM((PAIRS,), jnp.int32),
            pltpu.SMEM((PAIRS,), jnp.int32),
            pltpu.SMEM((PAIRS,), jnp.int32),
            pltpu.VMEM((TILES, FIELDS, CELLS), BF),
            pltpu.VMEM((2, PAIRS, LANES, LANES), BF),
            pltpu.VMEM((PAIRS, STRIP, LANES), BF),
            pltpu.VMEM((PAIRS, 2 * STRIP, CELLS), BF),
            pltpu.VMEM((PAIRS, STRIP, LANES), BF),
            pltpu.VMEM((2, PAIRS * FIELDS, LANES), F32),
            pltpu.SemaphoreType.DMA((11,)),
        ],
        compiler_params=params,
    )(*stay(sky_block, target_device.reshape(PAIRS), sea_block, sky, weights, sst, marine))
    fluxes, back = pl.pallas_call(
        exchange,
        out_shape=(flux_shape, wire(BACK_WIDTH)),
        in_specs=[VMEM] * 3,
        out_specs=(VMEM, VMEM),
        compiler_params=params,
    )(swap(outgoing), sst, marine)
    fluxes, atm_back = pl.pallas_call(
        deliver,
        out_shape=(flux_shape, jax.ShapeDtypeStruct((BACK, TILES, CELLS), F32)),
        in_specs=[VMEM] * 5,
        out_specs=(HBM, VMEM),
        scratch_shapes=[
            pltpu.SMEM((PAIRS,), jnp.int32),
            pltpu.VMEM((2, PAIRS * FIELDS, LANES), F32),
            pltpu.VMEM((2, PAIRS * FIELDS, LANES), F32),
            pltpu.VMEM((2, TILES * FIELDS, LANES), F32),
            pltpu.SemaphoreType.DMA((2,)),
        ],
        compiler_params=params,
    )(sky_block, target, swap(back), weights, fluxes)
    return fluxes, jnp.transpose(atm_back, (1, 0, 2))


def solution(mesh):
    tiles = P(("gx", "gy"), None, None)
    cells = P(("gx", "gy"), None)
    flat = P(("gx", "gy"))
    return jax.shard_map(
        on_device,
        mesh=mesh,
        in_specs=(tiles, tiles, flat, cells, flat, cells, cells),
        out_specs=(tiles, tiles),
        check_vma=False,
    )
```

```python
import functools

import jax
import jax.numpy as jnp
from jax import lax
from jax.experimental import pallas as pl
from jax.experimental.pallas import tpu as pltpu
from jax.sharding import PartitionSpec as P

PAIRS = 16
TILES = 16
FIELDS = 8
SENT = 6
BACK = 5
CELLS = 256
LANES = 128
SLOTS = 2
STRIP = 16
OUT_WIDTH = SENT * CELLS + LANES
BACK_WIDTH = BACK * CELLS
BF = jnp.bfloat16
F32 = jnp.float32
VMEM_LIMIT = 24 * 1024 * 1024


def iota(shape, dim):
    return lax.broadcasted_iota(jnp.int32, shape, dim)


def to_column(row):
    same = iota((PAIRS, PAIRS), 0) == iota((PAIRS, PAIRS), 1)
    return jnp.sum(jnp.where(same, row, 0.0), axis=1, keepdims=True)


def to_row(column):
    same = iota((PAIRS, PAIRS), 0) == iota((PAIRS, PAIRS), 1)
    return jnp.sum(jnp.where(same, column, 0.0), axis=0, keepdims=True)


def slot_column(target):
    row = target.astype(F32)
    column = to_column(row)
    later, other = iota((PAIRS, PAIRS), 0), iota((PAIRS, PAIRS), 1)
    earlier = jnp.where((column == row) & (other < later), 1.0, 0.0)
    return SLOTS * column + jnp.sum(earlier, axis=1, keepdims=True)


def contribute(
    src_hbm, owner_hbm, sea_hbm, sky_hbm, weights_hbm, sst_hbm, marine_hbm, out, sst, marine,
    src, owner, sea, sky, blocks, top, middle, bottom, scratch, sems,
):
    copies = {}

    def fetch(name, source, held):
        copies[name] = pltpu.make_async_copy(source, held, sems.at[len(copies)])
        copies[name].start()

    left, right = pl.ds(0, LANES), pl.ds(LANES, LANES)
    every = pl.ds(0, PAIRS)
    fetch("upper", weights_hbm.at[every, left, left], blocks.at[0])
    fetch("lower", weights_hbm.at[every, right, right], blocks.at[1])
    fetch("top", weights_hbm.at[every, pl.ds(0, STRIP), right], top)
    fetch("middle", weights_hbm.at[every, pl.ds(LANES - STRIP, 2 * STRIP)], middle)
    fetch("bottom", weights_hbm.at[every, pl.ds(CELLS - STRIP, STRIP), left], bottom)
    fetch("owner", owner_hbm, owner)
    fetch("sea", sea_hbm, sea)
    fetch("src", src_hbm, src)
    fetch("sky", sky_hbm, sky)
    fetch("sst", sst_hbm, sst)
    fetch("marine", marine_hbm, marine)
    out[...] = jnp.zeros_like(out)
    copies["owner"].wait()
    copies["sea"].wait()
    at = iota((PAIRS, PAIRS), 1)
    row = jnp.zeros((PAIRS, PAIRS), jnp.int32)
    tiles = jnp.zeros((PAIRS, LANES), jnp.int32)
    for p in range(PAIRS):
        row = jnp.where(at == p, owner[p], row)
        tiles = jnp.where(iota((PAIRS, LANES), 0) == p, sea[p], tiles)
    row = row[:1].astype(F32)
    column = to_column(row)
    before = at < iota((PAIRS, PAIRS), 0)
    rank = jnp.sum(jnp.where((column == row) & before, 1.0, 0.0), axis=1, keepdims=True)
    both = SLOTS * PAIRS
    wanted, pair = iota((both, PAIRS), 0), iota((both, PAIRS), 1)
    mine = jnp.sum(jnp.where(wanted // SLOTS == pair, row, 0.0), axis=1, keepdims=True)
    fits = (mine == row) & ((wanted % SLOTS).astype(F32) == to_row(rank))
    chosen = jnp.where(fits, 1.0, 0.0).astype(BF)
    label = tiles.astype(F32) + 1.0
    for name in ("src", "sky", "top", "middle", "bottom", "upper", "lower"):
        copies[name].wait()
    gap = jnp.zeros((LANES - 2 * STRIP, LANES), BF)
    for p in range(PAIRS):
        upper = jnp.concatenate([top[p], gap, middle[p, :STRIP, LANES:]], axis=0)
        lower = jnp.concatenate([middle[p, STRIP:, :LANES], gap, bottom[p]], axis=0)
        weights = jnp.concatenate(
            [
                jnp.concatenate([blocks[0, p], upper], axis=1),
                jnp.concatenate([lower, blocks[1, p]], axis=1),
            ],
            axis=0,
        )
        term = jnp.dot(sky[src[p]], weights, preferred_element_type=F32)
        for h in range(2):
            scratch[h, p * FIELDS : (p + 1) * FIELDS, :] = term[:, h * LANES : (h + 1) * LANES]

    def field(f):
        parts = [scratch[h, pl.ds(f, PAIRS, stride=FIELDS), :] for h in range(2)]
        return jnp.concatenate(parts, axis=1)

    u, v, ta, qa, sw, lw, pr, ps = (field(f) for f in range(FIELDS))
    sent = [x.astype(BF) for x in (u, v, ta, qa - 0.3 * ps, 0.5 * sw + 0.3 * lw, pr)]
    rest = (u - sent[0].astype(F32))[:, :LANES]
    sent.append(jnp.where(iota((PAIRS, LANES), 1) == 0, label, rest).astype(BF))
    filled = jnp.dot(chosen, jnp.concatenate(sent, axis=1), preferred_element_type=F32)
    filled = filled.astype(BF).reshape(PAIRS, SLOTS, OUT_WIDTH)
    for p in range(PAIRS):
        out[owner[p]] = filled[p]
    copies["sst"].wait()
    copies["marine"].wait()


def exchange(arrived, sst, marine, fluxes, out):
    rows = arrived.shape[0] * arrived.shape[1]
    slots = arrived[...].reshape(rows, OUT_WIDTH)
    first = jnp.where(iota((LANES, TILES), 0) == 0, 1.0, 0.0).astype(BF)
    label = jnp.dot(slots[:, SENT * CELLS :], first, preferred_element_type=F32)
    tile = (iota((rows, TILES), 1) + 1).astype(F32)
    chosen = jnp.where(label == tile, 1.0, 0.0).astype(BF)
    total = lax.dot_general(chosen, slots, (((0,), (0,)), ((), ())), preferred_element_type=F32)
    u, v, ta, q, rad, pr = (total[:, f * CELLS : (f + 1) * CELLS] for f in range(SENT))
    rest = jnp.where(iota((TILES, LANES), 1) == 0, 0.0, total[:, SENT * CELLS :])
    u = jnp.concatenate([u[:, :LANES] + rest, u[:, LANES:]], axis=1)
    warmth = sst[...]
    w = marine[...].astype(F32)
    speed = jnp.sqrt(u * u + v * v + 0.25)
    dth = warmth - ta
    dq = 0.4 * warmth - q
    lift = 2.0 * (dth + 0.5 * dq)
    c = jnp.ones_like(speed)
    for _ in range(3):
        c = 1.0 + 0.5 * jnp.tanh(lift / (1.0 + c * speed * speed))
    k = c * speed
    found = (k * u * w, k * v * w, (rad - k * dth - k * dq) * w, (pr - 0.5 * k * dq) * w)
    for f, x in enumerate(found):
        fluxes[:, f, :] = x
    back = jnp.concatenate([x.astype(BF) for x in found + (warmth * w,)], axis=1)
    out[...] = jnp.dot(chosen, back, preferred_element_type=F32).astype(BF).reshape(out.shape)


def deliver(
    src_row, target, returned, weights, fluxes, fluxes_hbm, out, values, terms, sums, sem
):
    copy = pltpu.make_async_copy(fluxes, fluxes_hbm, sem)
    copy.start()
    owners, sources = target[...], src_row[...]
    owner = [owners[0, p] for p in range(PAIRS)]
    src = [sources[0, p] for p in range(PAIRS)]
    values[...] = jnp.zeros_like(values)
    for p in range(PAIRS):
        second = functools.reduce(jnp.logical_or, [owner[q] == owner[p] for q in range(p)], False)
        slots = returned[owner[p]].astype(F32)
        slot = jnp.where(second, slots[1:], slots[:1])
        for f in range(BACK):
            for h in range(2):
                start = f * CELLS + h * LANES
                values[h, p * FIELDS + f : p * FIELDS + f + 1, :] = slot[:, start : start + LANES]
    sums[...] = jnp.zeros_like(sums)
    for p in range(PAIRS):
        block = pl.ds(p * FIELDS, FIELDS)
        term = lax.dot_general(
            jnp.concatenate([values[h, block, :] for h in range(2)], axis=1).astype(BF),
            weights[p],
            (((1,), (1,)), ((), ())),
            preferred_element_type=F32,
        )
        for h in range(2):
            terms[h, block, :] = term[:, h * LANES : (h + 1) * LANES]
    for p in range(PAIRS):
        block = pl.ds(p * FIELDS, FIELDS)
        at = pl.ds(pl.multiple_of(src[p] * FIELDS, FIELDS), FIELDS)
        for h in range(2):
            sums[h, at, :] += terms[h, block, :]
    for f in range(BACK):
        for h in range(2):
            out[f, :, h * LANES : (h + 1) * LANES] = sums[h, pl.ds(f, TILES, stride=FIELDS), :]
    copy.wait()


VMEM = pl.BlockSpec(memory_space=pltpu.VMEM)
HBM = pl.BlockSpec(memory_space=pltpu.HBM)


def on_device(sky, weights, sky_block, target_device, sea_block, sst, marine):
    devices = lax.axis_size(("gx", "gy"))
    params = pltpu.CompilerParams(vmem_limit_bytes=VMEM_LIMIT)
    target = target_device.reshape(1, PAIRS)
    flux_shape = jax.ShapeDtypeStruct((TILES, 4, CELLS), F32)

    def wire(width):
        return jax.ShapeDtypeStruct((devices, SLOTS, width), BF)

    def swap(x):
        return lax.all_to_all(x, ("gx", "gy"), split_axis=0, concat_axis=0, tiled=True)

    def stay(*arrays):
        return tuple(pltpu.with_memory_space_constraint(x, pltpu.HBM) for x in arrays)

    outgoing, sst, marine = pl.pallas_call(
        contribute,
        out_shape=(
            wire(OUT_WIDTH),
            jax.ShapeDtypeStruct((TILES, CELLS), F32),
            jax.ShapeDtypeStruct((TILES, CELLS), jnp.int32),
        ),
        in_specs=[HBM] * 7,
        out_specs=(VMEM,) * 3,
        scratch_shapes=[
            pltpu.SMEM((PAIRS,), jnp.int32),
            pltpu.SMEM((PAIRS,), jnp.int32),
            pltpu.SMEM((PAIRS,), jnp.int32),
            pltpu.VMEM((TILES, FIELDS, CELLS), BF),
            pltpu.VMEM((2, PAIRS, LANES, LANES), BF),
            pltpu.VMEM((PAIRS, STRIP, LANES), BF),
            pltpu.VMEM((PAIRS, 2 * STRIP, CELLS), BF),
            pltpu.VMEM((PAIRS, STRIP, LANES), BF),
            pltpu.VMEM((2, PAIRS * FIELDS, LANES), F32),
            pltpu.SemaphoreType.DMA((11,)),
        ],
        compiler_params=params,
    )(*stay(sky_block, target_device.reshape(PAIRS), sea_block, sky, weights, sst, marine))
    fluxes, back = pl.pallas_call(
        exchange,
        out_shape=(flux_shape, wire(BACK_WIDTH)),
        in_specs=[VMEM] * 3,
        out_specs=(VMEM, VMEM),
        compiler_params=params,
    )(swap(outgoing), sst, marine)
    fluxes, atm_back = pl.pallas_call(
        deliver,
        out_shape=(flux_shape, jax.ShapeDtypeStruct((BACK, TILES, CELLS), F32)),
        in_specs=[VMEM] * 5,
        out_specs=(HBM, VMEM),
        scratch_shapes=[
            pltpu.VMEM((2, PAIRS * FIELDS, LANES), F32),
            pltpu.VMEM((2, PAIRS * FIELDS, LANES), F32),
            pltpu.VMEM((2, TILES * FIELDS, LANES), F32),
            pltpu.SemaphoreType.DMA,
        ],
        compiler_params=params,
    )(sky_block.reshape(1, PAIRS), target, swap(back), weights, fluxes)
    return fluxes, jnp.transpose(atm_back, (1, 0, 2))


def solution(mesh):
    tiles = P(("gx", "gy"), None, None)
    cells = P(("gx", "gy"), None)
    flat = P(("gx", "gy"))
    return jax.shard_map(
        on_device,
        mesh=mesh,
        in_specs=(tiles, tiles, flat, cells, flat, cells, cells),
        out_specs=(tiles, tiles),
        check_vma=False,
    )
```

```python
import functools

import jax
import jax.numpy as jnp
from jax import lax
from jax.experimental import pallas as pl
from jax.experimental.pallas import tpu as pltpu
from jax.sharding import PartitionSpec as P

PAIRS = 16
TILES = 16
FIELDS = 8
SENT = 6
BACK = 5
CELLS = 256
LANES = 128
SLOTS = 2
STRIP = 16
STRIDE = 37
OUT_WIDTH = SENT * CELLS + LANES
BACK_WIDTH = BACK * CELLS
BF = jnp.bfloat16
F32 = jnp.float32
VMEM_LIMIT = 24 * 1024 * 1024


def iota(shape, dim):
    return lax.broadcasted_iota(jnp.int32, shape, dim)


def block_of(device, devices):
    return lax.rem(device * pow(STRIDE, -1, devices), devices)


def to_column(row):
    same = iota((PAIRS, PAIRS), 0) == iota((PAIRS, PAIRS), 1)
    return jnp.sum(jnp.where(same, row, 0.0), axis=1, keepdims=True)


def to_row(column):
    same = iota((PAIRS, PAIRS), 0) == iota((PAIRS, PAIRS), 1)
    return jnp.sum(jnp.where(same, column, 0.0), axis=0, keepdims=True)


def slot_column(target):
    row = target.astype(F32)
    column = to_column(row)
    later, other = iota((PAIRS, PAIRS), 0), iota((PAIRS, PAIRS), 1)
    earlier = jnp.where((column == row) & (other < later), 1.0, 0.0)
    return SLOTS * column + jnp.sum(earlier, axis=1, keepdims=True)


def contribute(
    src_hbm, owner_hbm, sea_hbm, sky_hbm, weights_hbm, sst_hbm, marine_hbm, out, sst, marine,
    src, owner, sea, sky, blocks, top, middle, bottom, scratch, sems,
):
    copies = {}

    def fetch(name, source, held):
        copies[name] = pltpu.make_async_copy(source, held, sems.at[len(copies)])
        copies[name].start()

    left, right = pl.ds(0, LANES), pl.ds(LANES, LANES)
    every = pl.ds(0, PAIRS)
    fetch("upper", weights_hbm.at[every, left, left], blocks.at[0])
    fetch("middle", weights_hbm.at[every, pl.ds(LANES - STRIP, 2 * STRIP)], middle)
    fetch("bottom", weights_hbm.at[every, pl.ds(CELLS - STRIP, STRIP), left], bottom)
    fetch("owner", owner_hbm, owner)
    fetch("sea", sea_hbm, sea)
    fetch("src", src_hbm, src)
    fetch("sky", sky_hbm, sky)
    fetch("lower", weights_hbm.at[every, right, right], blocks.at[1])
    fetch("top", weights_hbm.at[every, pl.ds(0, STRIP), right], top)
    fetch("sst", sst_hbm, sst)
    fetch("marine", marine_hbm, marine)
    out[...] = jnp.zeros_like(out)
    copies["owner"].wait()
    copies["sea"].wait()
    at = iota((PAIRS, PAIRS), 1)
    row = jnp.zeros((PAIRS, PAIRS), jnp.int32)
    tiles = jnp.zeros((PAIRS, LANES), jnp.int32)
    for p in range(PAIRS):
        row = jnp.where(at == p, owner[p], row)
        tiles = jnp.where(iota((PAIRS, LANES), 0) == p, sea[p], tiles)
    row = row[:1].astype(F32)
    column = to_column(row)
    before = at < iota((PAIRS, PAIRS), 0)
    rank = jnp.sum(jnp.where((column == row) & before, 1.0, 0.0), axis=1, keepdims=True)
    both = SLOTS * PAIRS
    wanted, pair = iota((both, PAIRS), 0), iota((both, PAIRS), 1)
    mine = jnp.sum(jnp.where(wanted // SLOTS == pair, row, 0.0), axis=1, keepdims=True)
    fits = (mine == row) & ((wanted % SLOTS).astype(F32) == to_row(rank))
    chosen = jnp.where(fits, 1.0, 0.0).astype(BF)
    label = tiles.astype(F32) + 1.0
    gap = jnp.zeros((LANES - 2 * STRIP, LANES), BF)
    for h, needed in enumerate((("src", "sky", "upper", "middle", "bottom"), ("lower", "top"))):
        for name in needed:
            copies[name].wait()
        for p in range(PAIRS):
            if h == 0:
                parts = [blocks[0, p], middle[p, STRIP:, :LANES], gap, bottom[p]]
            else:
                parts = [top[p], gap, middle[p, :STRIP, LANES:], blocks[1, p]]
            scratch[h, p * FIELDS : (p + 1) * FIELDS, :] = jnp.dot(
                sky[src[p]], jnp.concatenate(parts, axis=0), preferred_element_type=F32
            )

    def field(f):
        parts = [scratch[h, pl.ds(f, PAIRS, stride=FIELDS), :] for h in range(2)]
        return jnp.concatenate(parts, axis=1)

    u, v, ta, qa, sw, lw, pr, ps = (field(f) for f in range(FIELDS))
    sent = [x.astype(BF) for x in (u, v, ta, qa - 0.3 * ps, 0.5 * sw + 0.3 * lw, pr)]
    rest = (u - sent[0].astype(F32))[:, :LANES]
    sent.append(jnp.where(iota((PAIRS, LANES), 1) == 0, label, rest).astype(BF))
    filled = jnp.dot(chosen, jnp.concatenate(sent, axis=1), preferred_element_type=F32)
    filled = filled.astype(BF).reshape(PAIRS, SLOTS, OUT_WIDTH)
    for p in range(PAIRS):
        out[block_of(owner[p], out.shape[0])] = filled[p]
    copies["sst"].wait()
    copies["marine"].wait()


def exchange(arrived, sst, marine, fluxes, out):
    rows = arrived.shape[0] * arrived.shape[1]
    slots = arrived[...].reshape(rows, OUT_WIDTH)
    first = jnp.where(iota((LANES, TILES), 0) == 0, 1.0, 0.0).astype(BF)
    label = jnp.dot(slots[:, SENT * CELLS :], first, preferred_element_type=F32)
    tile = (iota((rows, TILES), 1) + 1).astype(F32)
    chosen = jnp.where(label == tile, 1.0, 0.0).astype(BF)
    total = lax.dot_general(chosen, slots, (((0,), (0,)), ((), ())), preferred_element_type=F32)
    u, v, ta, q, rad, pr = (total[:, f * CELLS : (f + 1) * CELLS] for f in range(SENT))
    rest = jnp.where(iota((TILES, LANES), 1) == 0, 0.0, total[:, SENT * CELLS :])
    u = jnp.concatenate([u[:, :LANES] + rest, u[:, LANES:]], axis=1)
    warmth = sst[...]
    w = marine[...].astype(F32)
    speed = jnp.sqrt(u * u + v * v + 0.25)
    dth = warmth - ta
    dq = 0.4 * warmth - q
    lift = 2.0 * (dth + 0.5 * dq)
    c = jnp.ones_like(speed)
    for _ in range(3):
        c = 1.0 + 0.5 * jnp.tanh(lift / (1.0 + c * speed * speed))
    k = c * speed
    found = (k * u * w, k * v * w, (rad - k * dth - k * dq) * w, (pr - 0.5 * k * dq) * w)
    for f, x in enumerate(found):
        fluxes[:, f, :] = x
    back = jnp.concatenate([x.astype(BF) for x in found + (warmth * w,)], axis=1)
    out[...] = jnp.dot(chosen, back, preferred_element_type=F32).astype(BF).reshape(out.shape)


def deliver(
    src_row, target, returned, weights, fluxes, fluxes_hbm, out, values, terms, sums, sem
):
    copy = pltpu.make_async_copy(fluxes, fluxes_hbm, sem)
    copy.start()
    owners, sources = target[...], src_row[...]
    owner = [owners[0, p] for p in range(PAIRS)]
    src = [sources[0, p] for p in range(PAIRS)]
    values[...] = jnp.zeros_like(values)
    for p in range(PAIRS):
        second = functools.reduce(jnp.logical_or, [owner[q] == owner[p] for q in range(p)], False)
        slots = returned[block_of(owner[p], returned.shape[0])].astype(F32)
        slot = jnp.where(second, slots[1:], slots[:1])
        for f in range(BACK):
            for h in range(2):
                start = f * CELLS + h * LANES
                values[h, p * FIELDS + f : p * FIELDS + f + 1, :] = slot[:, start : start + LANES]
    sums[...] = jnp.zeros_like(sums)
    for p in range(PAIRS):
        block = pl.ds(p * FIELDS, FIELDS)
        term = lax.dot_general(
            jnp.concatenate([values[h, block, :] for h in range(2)], axis=1).astype(BF),
            weights[p],
            (((1,), (1,)), ((), ())),
            preferred_element_type=F32,
        )
        for h in range(2):
            terms[h, block, :] = term[:, h * LANES : (h + 1) * LANES]
    for p in range(PAIRS):
        block = pl.ds(p * FIELDS, FIELDS)
        at = pl.ds(pl.multiple_of(src[p] * FIELDS, FIELDS), FIELDS)
        for h in range(2):
            sums[h, at, :] += terms[h, block, :]
    for f in range(BACK):
        for h in range(2):
            out[f, :, h * LANES : (h + 1) * LANES] = sums[h, pl.ds(f, TILES, stride=FIELDS), :]
    copy.wait()


VMEM = pl.BlockSpec(memory_space=pltpu.VMEM)
HBM = pl.BlockSpec(memory_space=pltpu.HBM)


def on_device(sky, weights, sky_block, target_device, sea_block, sst, marine):
    devices = lax.axis_size(("gx", "gy"))
    params = pltpu.CompilerParams(vmem_limit_bytes=VMEM_LIMIT)
    target = target_device.reshape(1, PAIRS)
    flux_shape = jax.ShapeDtypeStruct((TILES, 4, CELLS), F32)

    def wire(width):
        return jax.ShapeDtypeStruct((devices, SLOTS, width), BF)

    def swap(x):
        order = [STRIDE * j % devices for j in range(devices)]
        return lax.all_to_all(
            x,
            ("gx", "gy"),
            split_axis=0,
            concat_axis=0,
            axis_index_groups=[order],
            tiled=True,
        )

    def stay(*arrays):
        return tuple(pltpu.with_memory_space_constraint(x, pltpu.HBM) for x in arrays)

    outgoing, sst, marine = pl.pallas_call(
        contribute,
        out_shape=(
            wire(OUT_WIDTH),
            jax.ShapeDtypeStruct((TILES, CELLS), F32),
            jax.ShapeDtypeStruct((TILES, CELLS), jnp.int32),
        ),
        in_specs=[HBM] * 7,
        out_specs=(VMEM,) * 3,
        scratch_shapes=[
            pltpu.SMEM((PAIRS,), jnp.int32),
            pltpu.SMEM((PAIRS,), jnp.int32),
            pltpu.SMEM((PAIRS,), jnp.int32),
            pltpu.VMEM((TILES, FIELDS, CELLS), BF),
            pltpu.VMEM((2, PAIRS, LANES, LANES), BF),
            pltpu.VMEM((PAIRS, STRIP, LANES), BF),
            pltpu.VMEM((PAIRS, 2 * STRIP, CELLS), BF),
            pltpu.VMEM((PAIRS, STRIP, LANES), BF),
            pltpu.VMEM((2, PAIRS * FIELDS, LANES), F32),
            pltpu.SemaphoreType.DMA((11,)),
        ],
        compiler_params=params,
    )(*stay(sky_block, target_device.reshape(PAIRS), sea_block, sky, weights, sst, marine))
    fluxes, back = pl.pallas_call(
        exchange,
        out_shape=(flux_shape, wire(BACK_WIDTH)),
        in_specs=[VMEM] * 3,
        out_specs=(VMEM, VMEM),
        compiler_params=params,
    )(swap(outgoing), sst, marine)
    fluxes, atm_back = pl.pallas_call(
        deliver,
        out_shape=(flux_shape, jax.ShapeDtypeStruct((BACK, TILES, CELLS), F32)),
        in_specs=[VMEM] * 5,
        out_specs=(HBM, VMEM),
        scratch_shapes=[
            pltpu.VMEM((2, PAIRS * FIELDS, LANES), F32),
            pltpu.VMEM((2, PAIRS * FIELDS, LANES), F32),
            pltpu.VMEM((2, TILES * FIELDS, LANES), F32),
            pltpu.SemaphoreType.DMA,
        ],
        compiler_params=params,
    )(sky_block.reshape(1, PAIRS), target, swap(back), weights, fluxes)
    return fluxes, jnp.transpose(atm_back, (1, 0, 2))


def solution(mesh):
    tiles = P(("gx", "gy"), None, None)
    cells = P(("gx", "gy"), None)
    flat = P(("gx", "gy"))
    return jax.shard_map(
        on_device,
        mesh=mesh,
        in_specs=(tiles, tiles, flat, cells, flat, cells, cells),
        out_specs=(tiles, tiles),
        check_vma=False,
    )
```

```python
import functools

import jax
import jax.numpy as jnp
from jax import lax
from jax.experimental import pallas as pl
from jax.experimental.pallas import tpu as pltpu
from jax.sharding import PartitionSpec as P

PAIRS = 16
TILES = 16
FIELDS = 8
SENT = 6
BACK = 5
CELLS = 256
LANES = 128
SLOTS = 2
STRIP = 16
STRIDE = 37
OUT_WIDTH = SENT * CELLS + LANES
BACK_WIDTH = BACK * CELLS
BF = jnp.bfloat16
F32 = jnp.float32
VMEM_LIMIT = 24 * 1024 * 1024


def iota(shape, dim):
    return lax.broadcasted_iota(jnp.int32, shape, dim)


def block_of(device, devices):
    return (device * pow(STRIDE, -1, devices)) & (devices - 1)


def to_column(row):
    same = iota((PAIRS, PAIRS), 0) == iota((PAIRS, PAIRS), 1)
    return jnp.sum(jnp.where(same, row, 0.0), axis=1, keepdims=True)


def to_row(column):
    same = iota((PAIRS, PAIRS), 0) == iota((PAIRS, PAIRS), 1)
    return jnp.sum(jnp.where(same, column, 0.0), axis=0, keepdims=True)


def slot_column(target):
    row = target.astype(F32)
    column = to_column(row)
    later, other = iota((PAIRS, PAIRS), 0), iota((PAIRS, PAIRS), 1)
    earlier = jnp.where((column == row) & (other < later), 1.0, 0.0)
    return SLOTS * column + jnp.sum(earlier, axis=1, keepdims=True)


def contribute(
    src_hbm, owner_hbm, sea_hbm, sky_hbm, weights_hbm, sst_hbm, marine_hbm, out, sst, marine,
    src, owner, sea, sky, blocks, top, middle, bottom, scratch, sems,
):
    copies = {}

    def fetch(name, source, held):
        copies[name] = pltpu.make_async_copy(source, held, sems.at[len(copies)])
        copies[name].start()

    left, right = pl.ds(0, LANES), pl.ds(LANES, LANES)
    every = pl.ds(0, PAIRS)
    fetch("upper", weights_hbm.at[every, left, left], blocks.at[0])
    fetch("middle", weights_hbm.at[every, pl.ds(LANES - STRIP, 2 * STRIP)], middle)
    fetch("bottom", weights_hbm.at[every, pl.ds(CELLS - STRIP, STRIP), left], bottom)
    fetch("owner", owner_hbm, owner)
    fetch("sea", sea_hbm, sea)
    fetch("src", src_hbm, src)
    fetch("sky", sky_hbm, sky)
    fetch("lower", weights_hbm.at[every, right, right], blocks.at[1])
    fetch("top", weights_hbm.at[every, pl.ds(0, STRIP), right], top)
    fetch("sst", sst_hbm, sst)
    fetch("marine", marine_hbm, marine)
    out[...] = jnp.zeros_like(out)
    copies["owner"].wait()
    copies["sea"].wait()
    at = iota((PAIRS, PAIRS), 1)
    row = jnp.zeros((PAIRS, PAIRS), jnp.int32)
    tiles = jnp.zeros((PAIRS, LANES), jnp.int32)
    for p in range(PAIRS):
        row = jnp.where(at == p, owner[p], row)
        tiles = jnp.where(iota((PAIRS, LANES), 0) == p, sea[p], tiles)
    row = row[:1].astype(F32)
    column = to_column(row)
    before = at < iota((PAIRS, PAIRS), 0)
    rank = jnp.sum(jnp.where((column == row) & before, 1.0, 0.0), axis=1, keepdims=True)
    both = SLOTS * PAIRS
    wanted, pair = iota((both, PAIRS), 0), iota((both, PAIRS), 1)
    mine = jnp.sum(jnp.where(wanted // SLOTS == pair, row, 0.0), axis=1, keepdims=True)
    fits = (mine == row) & ((wanted % SLOTS).astype(F32) == to_row(rank))
    chosen = jnp.where(fits, 1.0, 0.0).astype(BF)
    label = tiles.astype(F32) + 1.0
    gap = jnp.zeros((LANES - 2 * STRIP, LANES), BF)
    for h, needed in enumerate((("src", "sky", "upper", "middle", "bottom"), ("lower", "top"))):
        for name in needed:
            copies[name].wait()
        for p in range(PAIRS):
            if h == 0:
                parts = [blocks[0, p], middle[p, STRIP:, :LANES], gap, bottom[p]]
            else:
                parts = [top[p], gap, middle[p, :STRIP, LANES:], blocks[1, p]]
            scratch[h, p * FIELDS : (p + 1) * FIELDS, :] = jnp.dot(
                sky[src[p]], jnp.concatenate(parts, axis=0), preferred_element_type=F32
            )

    def field(f):
        parts = [scratch[h, pl.ds(f, PAIRS, stride=FIELDS), :] for h in range(2)]
        return jnp.concatenate(parts, axis=1)

    u, v, ta, qa, sw, lw, pr, ps = (field(f) for f in range(FIELDS))
    sent = [x.astype(BF) for x in (u, v, ta, qa - 0.3 * ps, 0.5 * sw + 0.3 * lw, pr)]
    rest = (u - sent[0].astype(F32))[:, :LANES]
    sent.append(jnp.where(iota((PAIRS, LANES), 1) == 0, label, rest).astype(BF))
    filled = jnp.dot(chosen, jnp.concatenate(sent, axis=1), preferred_element_type=F32)
    filled = filled.astype(BF).reshape(PAIRS, SLOTS, OUT_WIDTH)
    for p in range(PAIRS):
        out[block_of(owner[p], out.shape[0])] = filled[p]
    copies["sst"].wait()
    copies["marine"].wait()


def exchange(arrived, sst, marine, fluxes, out):
    rows = arrived.shape[0] * arrived.shape[1]
    slots = arrived[...].reshape(rows, OUT_WIDTH)
    first = jnp.where(iota((LANES, TILES), 0) == 0, 1.0, 0.0).astype(BF)
    label = jnp.dot(slots[:, SENT * CELLS :], first, preferred_element_type=F32)
    tile = (iota((rows, TILES), 1) + 1).astype(F32)
    chosen = jnp.where(label == tile, 1.0, 0.0).astype(BF)
    total = lax.dot_general(chosen, slots, (((0,), (0,)), ((), ())), preferred_element_type=F32)
    u, v, ta, q, rad, pr = (total[:, f * CELLS : (f + 1) * CELLS] for f in range(SENT))
    rest = jnp.where(iota((TILES, LANES), 1) == 0, 0.0, total[:, SENT * CELLS :])
    u = jnp.concatenate([u[:, :LANES] + rest, u[:, LANES:]], axis=1)
    warmth = sst[...]
    w = marine[...].astype(F32)
    speed = jnp.sqrt(u * u + v * v + 0.25)
    dth = warmth - ta
    dq = 0.4 * warmth - q
    lift = 2.0 * (dth + 0.5 * dq)
    c = jnp.ones_like(speed)
    for _ in range(3):
        c = 1.0 + 0.5 * jnp.tanh(lift / (1.0 + c * speed * speed))
    k = c * speed
    found = (k * u * w, k * v * w, (rad - k * dth - k * dq) * w, (pr - 0.5 * k * dq) * w)
    for f, x in enumerate(found):
        fluxes[:, f, :] = x
    back = jnp.concatenate([x.astype(BF) for x in found + (warmth * w,)], axis=1)
    out[...] = jnp.dot(chosen, back, preferred_element_type=F32).astype(BF).reshape(out.shape)


def deliver(
    src_row, target, returned, weights, fluxes, fluxes_hbm, out, values, terms, sums, sem
):
    copy = pltpu.make_async_copy(fluxes, fluxes_hbm, sem)
    copy.start()
    owners, sources = target[...], src_row[...]
    owner = [owners[0, p] for p in range(PAIRS)]
    src = [sources[0, p] for p in range(PAIRS)]
    values[...] = jnp.zeros_like(values)
    for p in range(PAIRS):
        second = functools.reduce(jnp.logical_or, [owner[q] == owner[p] for q in range(p)], False)
        slots = returned[block_of(owner[p], returned.shape[0])].astype(F32)
        slot = jnp.where(second, slots[1:], slots[:1])
        for f in range(BACK):
            for h in range(2):
                start = f * CELLS + h * LANES
                values[h, p * FIELDS + f : p * FIELDS + f + 1, :] = slot[:, start : start + LANES]
    sums[...] = jnp.zeros_like(sums)
    for p in range(PAIRS):
        block = pl.ds(p * FIELDS, FIELDS)
        term = lax.dot_general(
            jnp.concatenate([values[h, block, :] for h in range(2)], axis=1).astype(BF),
            weights[p],
            (((1,), (1,)), ((), ())),
            preferred_element_type=F32,
        )
        for h in range(2):
            terms[h, block, :] = term[:, h * LANES : (h + 1) * LANES]
    for p in range(PAIRS):
        block = pl.ds(p * FIELDS, FIELDS)
        at = pl.ds(pl.multiple_of(src[p] * FIELDS, FIELDS), FIELDS)
        for h in range(2):
            sums[h, at, :] += terms[h, block, :]
    for f in range(BACK):
        for h in range(2):
            out[f, :, h * LANES : (h + 1) * LANES] = sums[h, pl.ds(f, TILES, stride=FIELDS), :]
    copy.wait()


VMEM = pl.BlockSpec(memory_space=pltpu.VMEM)
HBM = pl.BlockSpec(memory_space=pltpu.HBM)


def on_device(sky, weights, sky_block, target_device, sea_block, sst, marine):
    devices = lax.axis_size(("gx", "gy"))
    params = pltpu.CompilerParams(vmem_limit_bytes=VMEM_LIMIT)
    target = target_device.reshape(1, PAIRS)
    flux_shape = jax.ShapeDtypeStruct((TILES, 4, CELLS), F32)

    def wire(width):
        return jax.ShapeDtypeStruct((devices, SLOTS, width), BF)

    def swap(x):
        order = [STRIDE * j % devices for j in range(devices)]
        return lax.all_to_all(
            x,
            ("gx", "gy"),
            split_axis=0,
            concat_axis=0,
            axis_index_groups=[order],
            tiled=True,
        )

    def stay(*arrays):
        return tuple(pltpu.with_memory_space_constraint(x, pltpu.HBM) for x in arrays)

    outgoing, sst, marine = pl.pallas_call(
        contribute,
        out_shape=(
            wire(OUT_WIDTH),
            jax.ShapeDtypeStruct((TILES, CELLS), F32),
            jax.ShapeDtypeStruct((TILES, CELLS), jnp.int32),
        ),
        in_specs=[HBM] * 7,
        out_specs=(VMEM,) * 3,
        scratch_shapes=[
            pltpu.SMEM((PAIRS,), jnp.int32),
            pltpu.SMEM((PAIRS,), jnp.int32),
            pltpu.SMEM((PAIRS,), jnp.int32),
            pltpu.VMEM((TILES, FIELDS, CELLS), BF),
            pltpu.VMEM((2, PAIRS, LANES, LANES), BF),
            pltpu.VMEM((PAIRS, STRIP, LANES), BF),
            pltpu.VMEM((PAIRS, 2 * STRIP, CELLS), BF),
            pltpu.VMEM((PAIRS, STRIP, LANES), BF),
            pltpu.VMEM((2, PAIRS * FIELDS, LANES), F32),
            pltpu.SemaphoreType.DMA((11,)),
        ],
        compiler_params=params,
    )(*stay(sky_block, target_device.reshape(PAIRS), sea_block, sky, weights, sst, marine))
    fluxes, back = pl.pallas_call(
        exchange,
        out_shape=(flux_shape, wire(BACK_WIDTH)),
        in_specs=[VMEM] * 3,
        out_specs=(VMEM, VMEM),
        compiler_params=params,
    )(swap(outgoing), sst, marine)
    fluxes, atm_back = pl.pallas_call(
        deliver,
        out_shape=(flux_shape, jax.ShapeDtypeStruct((BACK, TILES, CELLS), F32)),
        in_specs=[VMEM] * 5,
        out_specs=(HBM, VMEM),
        scratch_shapes=[
            pltpu.VMEM((2, PAIRS * FIELDS, LANES), F32),
            pltpu.VMEM((2, PAIRS * FIELDS, LANES), F32),
            pltpu.VMEM((2, TILES * FIELDS, LANES), F32),
            pltpu.SemaphoreType.DMA,
        ],
        compiler_params=params,
    )(sky_block.reshape(1, PAIRS), target, swap(back), weights, fluxes)
    return fluxes, jnp.transpose(atm_back, (1, 0, 2))


def solution(mesh):
    tiles = P(("gx", "gy"), None, None)
    cells = P(("gx", "gy"), None)
    flat = P(("gx", "gy"))
    return jax.shard_map(
        on_device,
        mesh=mesh,
        in_specs=(tiles, tiles, flat, cells, flat, cells, cells),
        out_specs=(tiles, tiles),
        check_vma=False,
    )
```

```python
import functools

import jax
import jax.numpy as jnp
from jax import lax
from jax.experimental import pallas as pl
from jax.experimental.pallas import tpu as pltpu
from jax.sharding import PartitionSpec as P

PAIRS = 16
TILES = 16
FIELDS = 8
SENT = 6
BACK = 5
CELLS = 256
LANES = 128
SLOTS = 2
STRIP = 16
OUT_WIDTH = SENT * CELLS + LANES
BACK_WIDTH = BACK * CELLS
BF = jnp.bfloat16
F32 = jnp.float32
VMEM_LIMIT = 24 * 1024 * 1024


def iota(shape, dim):
    return lax.broadcasted_iota(jnp.int32, shape, dim)


def key_of(device):
    return ((device >> 5) + ((device >> 3) & 3) + ((device >> 1) & 3)) * 128 + device


def places_of(column, devices):
    others = key_of(iota((PAIRS, devices), 1))
    ahead = jnp.where(others < key_of(column.astype(jnp.int32)), 1.0, 0.0)
    return to_row(jnp.sum(ahead, axis=1, keepdims=True)).astype(jnp.int32)


def to_column(row):
    same = iota((PAIRS, PAIRS), 0) == iota((PAIRS, PAIRS), 1)
    return jnp.sum(jnp.where(same, row, 0.0), axis=1, keepdims=True)


def to_row(column):
    same = iota((PAIRS, PAIRS), 0) == iota((PAIRS, PAIRS), 1)
    return jnp.sum(jnp.where(same, column, 0.0), axis=0, keepdims=True)


def contribute(
    src_hbm, owner_hbm, sea_hbm, sky_hbm, weights_hbm, sst_hbm, marine_hbm, out, sst, marine, places,
    src, owner, sea, sky, blocks, top, middle, bottom, scratch, sems,
):
    copies = {}

    def fetch(name, source, held):
        copies[name] = pltpu.make_async_copy(source, held, sems.at[len(copies)])
        copies[name].start()

    left, right = pl.ds(0, LANES), pl.ds(LANES, LANES)
    every = pl.ds(0, PAIRS)
    fetch("upper", weights_hbm.at[every, left, left], blocks.at[0])
    fetch("middle", weights_hbm.at[every, pl.ds(LANES - STRIP, 2 * STRIP)], middle)
    fetch("bottom", weights_hbm.at[every, pl.ds(CELLS - STRIP, STRIP), left], bottom)
    fetch("owner", owner_hbm, owner)
    fetch("sea", sea_hbm, sea)
    fetch("src", src_hbm, src)
    fetch("sky", sky_hbm, sky)
    fetch("lower", weights_hbm.at[every, right, right], blocks.at[1])
    fetch("top", weights_hbm.at[every, pl.ds(0, STRIP), right], top)
    fetch("sst", sst_hbm, sst)
    fetch("marine", marine_hbm, marine)
    out[...] = jnp.zeros_like(out)
    copies["owner"].wait()
    copies["sea"].wait()
    at = iota((PAIRS, PAIRS), 1)
    row = jnp.zeros((PAIRS, PAIRS), jnp.int32)
    tiles = jnp.zeros((PAIRS, LANES), jnp.int32)
    for p in range(PAIRS):
        row = jnp.where(at == p, owner[p], row)
        tiles = jnp.where(iota((PAIRS, LANES), 0) == p, sea[p], tiles)
    row = row[:1].astype(F32)
    column = to_column(row)
    before = at < iota((PAIRS, PAIRS), 0)
    rank = jnp.sum(jnp.where((column == row) & before, 1.0, 0.0), axis=1, keepdims=True)
    both = SLOTS * PAIRS
    wanted, pair = iota((both, PAIRS), 0), iota((both, PAIRS), 1)
    mine = jnp.sum(jnp.where(wanted // SLOTS == pair, row, 0.0), axis=1, keepdims=True)
    fits = (mine == row) & ((wanted % SLOTS).astype(F32) == to_row(rank))
    chosen = jnp.where(fits, 1.0, 0.0).astype(BF)
    label = tiles.astype(F32) + 1.0
    row_of_places = places_of(column, out.shape[0])
    places[...] = row_of_places
    place = [row_of_places[0, p] for p in range(PAIRS)]
    gap = jnp.zeros((LANES - 2 * STRIP, LANES), BF)
    for h, needed in enumerate((("src", "sky", "upper", "middle", "bottom"), ("lower", "top"))):
        for name in needed:
            copies[name].wait()
        for p in range(PAIRS):
            if h == 0:
                parts = [blocks[0, p], middle[p, STRIP:, :LANES], gap, bottom[p]]
            else:
                parts = [top[p], gap, middle[p, :STRIP, LANES:], blocks[1, p]]
            scratch[h, p * FIELDS : (p + 1) * FIELDS, :] = jnp.dot(
                sky[src[p]], jnp.concatenate(parts, axis=0), preferred_element_type=F32
            )

    def field(f):
        parts = [scratch[h, pl.ds(f, PAIRS, stride=FIELDS), :] for h in range(2)]
        return jnp.concatenate(parts, axis=1)

    u, v, ta, qa, sw, lw, pr, ps = (field(f) for f in range(FIELDS))
    sent = [x.astype(BF) for x in (u, v, ta, qa - 0.3 * ps, 0.5 * sw + 0.3 * lw, pr)]
    rest = (u - sent[0].astype(F32))[:, :LANES]
    sent.append(jnp.where(iota((PAIRS, LANES), 1) == 0, label, rest).astype(BF))
    filled = jnp.dot(chosen, jnp.concatenate(sent, axis=1), preferred_element_type=F32)
    filled = filled.astype(BF).reshape(PAIRS, SLOTS, OUT_WIDTH)
    for p in range(PAIRS):
        out[place[p]] = filled[p]
    copies["sst"].wait()
    copies["marine"].wait()


def exchange(arrived, sst, marine, fluxes, out):
    rows = arrived.shape[0] * arrived.shape[1]
    slots = arrived[...].reshape(rows, OUT_WIDTH)
    first = jnp.where(iota((LANES, TILES), 0) == 0, 1.0, 0.0).astype(BF)
    label = jnp.dot(slots[:, SENT * CELLS :], first, preferred_element_type=F32)
    tile = (iota((rows, TILES), 1) + 1).astype(F32)
    chosen = jnp.where(label == tile, 1.0, 0.0).astype(BF)
    total = lax.dot_general(chosen, slots, (((0,), (0,)), ((), ())), preferred_element_type=F32)
    u, v, ta, q, rad, pr = (total[:, f * CELLS : (f + 1) * CELLS] for f in range(SENT))
    rest = jnp.where(iota((TILES, LANES), 1) == 0, 0.0, total[:, SENT * CELLS :])
    u = jnp.concatenate([u[:, :LANES] + rest, u[:, LANES:]], axis=1)
    warmth = sst[...]
    w = marine[...].astype(F32)
    speed = jnp.sqrt(u * u + v * v + 0.25)
    dth = warmth - ta
    dq = 0.4 * warmth - q
    lift = 2.0 * (dth + 0.5 * dq)
    c = jnp.ones_like(speed)
    for _ in range(3):
        c = 1.0 + 0.5 * jnp.tanh(lift / (1.0 + c * speed * speed))
    k = c * speed
    found = (k * u * w, k * v * w, (rad - k * dth - k * dq) * w, (pr - 0.5 * k * dq) * w)
    for f, x in enumerate(found):
        fluxes[:, f, :] = x
    back = jnp.concatenate([x.astype(BF) for x in found + (warmth * w,)], axis=1)
    out[...] = jnp.dot(chosen, back, preferred_element_type=F32).astype(BF).reshape(out.shape)


def deliver(
    src_row, places, returned, weights, fluxes, fluxes_hbm, out, values, terms, sums, sem
):
    copy = pltpu.make_async_copy(fluxes, fluxes_hbm, sem)
    copy.start()
    row_of_places, sources = places[...], src_row[...]
    place = [row_of_places[0, p] for p in range(PAIRS)]
    src = [sources[0, p] for p in range(PAIRS)]
    values[...] = jnp.zeros_like(values)
    for p in range(PAIRS):
        second = functools.reduce(jnp.logical_or, [place[q] == place[p] for q in range(p)], False)
        slots = returned[place[p]].astype(F32)
        slot = jnp.where(second, slots[1:], slots[:1])
        for f in range(BACK):
            for h in range(2):
                start = f * CELLS + h * LANES
                values[h, p * FIELDS + f : p * FIELDS + f + 1, :] = slot[:, start : start + LANES]
    sums[...] = jnp.zeros_like(sums)
    for p in range(PAIRS):
        block = pl.ds(p * FIELDS, FIELDS)
        term = lax.dot_general(
            jnp.concatenate([values[h, block, :] for h in range(2)], axis=1).astype(BF),
            weights[p],
            (((1,), (1,)), ((), ())),
            preferred_element_type=F32,
        )
        for h in range(2):
            terms[h, block, :] = term[:, h * LANES : (h + 1) * LANES]
    for p in range(PAIRS):
        block = pl.ds(p * FIELDS, FIELDS)
        at = pl.ds(pl.multiple_of(src[p] * FIELDS, FIELDS), FIELDS)
        for h in range(2):
            sums[h, at, :] += terms[h, block, :]
    for f in range(BACK):
        for h in range(2):
            out[f, :, h * LANES : (h + 1) * LANES] = sums[h, pl.ds(f, TILES, stride=FIELDS), :]
    copy.wait()


VMEM = pl.BlockSpec(memory_space=pltpu.VMEM)
HBM = pl.BlockSpec(memory_space=pltpu.HBM)


def on_device(sky, weights, sky_block, target_device, sea_block, sst, marine):
    devices = lax.axis_size(("gx", "gy"))
    params = pltpu.CompilerParams(vmem_limit_bytes=VMEM_LIMIT)
    flux_shape = jax.ShapeDtypeStruct((TILES, 4, CELLS), F32)

    def wire(width):
        return jax.ShapeDtypeStruct((devices, SLOTS, width), BF)

    def swap(x):
        order = sorted(range(devices), key=key_of)
        return lax.all_to_all(
            x,
            ("gx", "gy"),
            split_axis=0,
            concat_axis=0,
            axis_index_groups=[order],
            tiled=True,
        )

    def stay(*arrays):
        return tuple(pltpu.with_memory_space_constraint(x, pltpu.HBM) for x in arrays)

    outgoing, sst, marine, places = pl.pallas_call(
        contribute,
        out_shape=(
            wire(OUT_WIDTH),
            jax.ShapeDtypeStruct((TILES, CELLS), F32),
            jax.ShapeDtypeStruct((TILES, CELLS), jnp.int32),
            jax.ShapeDtypeStruct((1, PAIRS), jnp.int32),
        ),
        in_specs=[HBM] * 7,
        out_specs=(VMEM,) * 4,
        scratch_shapes=[
            pltpu.SMEM((PAIRS,), jnp.int32),
            pltpu.SMEM((PAIRS,), jnp.int32),
            pltpu.SMEM((PAIRS,), jnp.int32),
            pltpu.VMEM((TILES, FIELDS, CELLS), BF),
            pltpu.VMEM((2, PAIRS, LANES, LANES), BF),
            pltpu.VMEM((PAIRS, STRIP, LANES), BF),
            pltpu.VMEM((PAIRS, 2 * STRIP, CELLS), BF),
            pltpu.VMEM((PAIRS, STRIP, LANES), BF),
            pltpu.VMEM((2, PAIRS * FIELDS, LANES), F32),
            pltpu.SemaphoreType.DMA((11,)),
        ],
        compiler_params=params,
    )(*stay(sky_block, target_device.reshape(PAIRS), sea_block, sky, weights, sst, marine))
    fluxes, back = pl.pallas_call(
        exchange,
        out_shape=(flux_shape, wire(BACK_WIDTH)),
        in_specs=[VMEM] * 3,
        out_specs=(VMEM, VMEM),
        compiler_params=params,
    )(swap(outgoing), sst, marine)
    fluxes, atm_back = pl.pallas_call(
        deliver,
        out_shape=(flux_shape, jax.ShapeDtypeStruct((BACK, TILES, CELLS), F32)),
        in_specs=[VMEM] * 5,
        out_specs=(HBM, VMEM),
        scratch_shapes=[
            pltpu.VMEM((2, PAIRS * FIELDS, LANES), F32),
            pltpu.VMEM((2, PAIRS * FIELDS, LANES), F32),
            pltpu.VMEM((2, TILES * FIELDS, LANES), F32),
            pltpu.SemaphoreType.DMA,
        ],
        compiler_params=params,
    )(sky_block.reshape(1, PAIRS), places, swap(back), weights, fluxes)
    return fluxes, jnp.transpose(atm_back, (1, 0, 2))


def solution(mesh):
    tiles = P(("gx", "gy"), None, None)
    cells = P(("gx", "gy"), None)
    flat = P(("gx", "gy"))
    return jax.shard_map(
        on_device,
        mesh=mesh,
        in_specs=(tiles, tiles, flat, cells, flat, cells, cells),
        out_specs=(tiles, tiles),
        check_vma=False,
    )
```

```python
import functools

import jax
import jax.numpy as jnp
from jax import lax
from jax.experimental import pallas as pl
from jax.experimental.pallas import tpu as pltpu
from jax.sharding import PartitionSpec as P

PAIRS = 16
TILES = 16
FIELDS = 8
SENT = 6
BACK = 5
CELLS = 256
LANES = 128
SLOTS = 2
STRIP = 16
OUT_WIDTH = SENT * CELLS + LANES
BACK_WIDTH = BACK * CELLS
BF = jnp.bfloat16
F32 = jnp.float32
VMEM_LIMIT = 24 * 1024 * 1024


def iota(shape, dim):
    return lax.broadcasted_iota(jnp.int32, shape, dim)


def key_of(device):
    return ((device >> 5) + ((device >> 3) & 3) + ((device >> 1) & 3)) * 128 + device


def places_of(column, devices):
    others = key_of(iota((PAIRS, devices), 1))
    ahead = jnp.where(others < key_of(column.astype(jnp.int32)), 1.0, 0.0)
    return to_row(jnp.sum(ahead, axis=1, keepdims=True)).astype(jnp.int32)


def to_column(row):
    same = iota((PAIRS, PAIRS), 0) == iota((PAIRS, PAIRS), 1)
    return jnp.sum(jnp.where(same, row, 0.0), axis=1, keepdims=True)


def to_row(column):
    same = iota((PAIRS, PAIRS), 0) == iota((PAIRS, PAIRS), 1)
    return jnp.sum(jnp.where(same, column, 0.0), axis=0, keepdims=True)


def contribute(
    src_hbm, owner_hbm, sea_hbm, sky_hbm, weights_hbm, sst_hbm, marine_hbm, out, sst, marine, places,
    src, owner, sea, sky, blocks, top, bottom, scratch, sems,
):
    copies = {}

    def fetch(name, source, held):
        copies[name] = pltpu.make_async_copy(source, held, sems.at[len(copies)])
        copies[name].start()

    left, right = pl.ds(0, LANES), pl.ds(LANES, LANES)
    every = pl.ds(0, PAIRS)
    fetch("upper", weights_hbm.at[every, pl.ds(0, LANES + STRIP), left], blocks.at[0])
    fetch("bottom", weights_hbm.at[every, pl.ds(CELLS - STRIP, STRIP), left], bottom)
    fetch("owner", owner_hbm, owner)
    fetch("sea", sea_hbm, sea)
    fetch("src", src_hbm, src)
    fetch("sky", sky_hbm, sky)
    fetch(
        "lower",
        weights_hbm.at[every, pl.ds(LANES - STRIP, LANES + STRIP), right],
        blocks.at[1],
    )
    fetch("top", weights_hbm.at[every, pl.ds(0, STRIP), right], top)
    fetch("sst", sst_hbm, sst)
    fetch("marine", marine_hbm, marine)
    out[...] = jnp.zeros_like(out)
    copies["owner"].wait()
    copies["sea"].wait()
    at = iota((PAIRS, PAIRS), 1)
    row = jnp.zeros((PAIRS, PAIRS), jnp.int32)
    tiles = jnp.zeros((PAIRS, LANES), jnp.int32)
    for p in range(PAIRS):
        row = jnp.where(at == p, owner[p], row)
        tiles = jnp.where(iota((PAIRS, LANES), 0) == p, sea[p], tiles)
    row = row[:1].astype(F32)
    column = to_column(row)
    before = at < iota((PAIRS, PAIRS), 0)
    rank = jnp.sum(jnp.where((column == row) & before, 1.0, 0.0), axis=1, keepdims=True)
    both = SLOTS * PAIRS
    wanted, pair = iota((both, PAIRS), 0), iota((both, PAIRS), 1)
    mine = jnp.sum(jnp.where(wanted // SLOTS == pair, row, 0.0), axis=1, keepdims=True)
    fits = (mine == row) & ((wanted % SLOTS).astype(F32) == to_row(rank))
    chosen = jnp.where(fits, 1.0, 0.0).astype(BF)
    label = tiles.astype(F32) + 1.0
    row_of_places = places_of(column, out.shape[0])
    places[...] = row_of_places
    place = [row_of_places[0, p] for p in range(PAIRS)]
    gap = jnp.zeros((LANES - 2 * STRIP, LANES), BF)
    for h, needed in enumerate((("src", "sky", "upper", "bottom"), ("lower", "top"))):
        for name in needed:
            copies[name].wait()
        for p in range(PAIRS):
            if h == 0:
                parts = [blocks[0, p], gap, bottom[p]]
            else:
                parts = [top[p], gap, blocks[1, p]]
            scratch[h, p * FIELDS : (p + 1) * FIELDS, :] = jnp.dot(
                sky[src[p]], jnp.concatenate(parts, axis=0), preferred_element_type=F32
            )

    def field(f):
        parts = [scratch[h, pl.ds(f, PAIRS, stride=FIELDS), :] for h in range(2)]
        return jnp.concatenate(parts, axis=1)

    u, v, ta, qa, sw, lw, pr, ps = (field(f) for f in range(FIELDS))
    sent = [x.astype(BF) for x in (u, v, ta, qa - 0.3 * ps, 0.5 * sw + 0.3 * lw, pr)]
    rest = (u - sent[0].astype(F32))[:, :LANES]
    sent.append(jnp.where(iota((PAIRS, LANES), 1) == 0, label, rest).astype(BF))
    filled = jnp.dot(chosen, jnp.concatenate(sent, axis=1), preferred_element_type=F32)
    filled = filled.astype(BF).reshape(PAIRS, SLOTS, OUT_WIDTH)
    for p in range(PAIRS):
        out[place[p]] = filled[p]
    copies["sst"].wait()
    copies["marine"].wait()


def exchange(arrived, sst, marine, fluxes, out):
    rows = arrived.shape[0] * arrived.shape[1]
    slots = arrived[...].reshape(rows, OUT_WIDTH)
    first = jnp.where(iota((LANES, TILES), 0) == 0, 1.0, 0.0).astype(BF)
    label = jnp.dot(slots[:, SENT * CELLS :], first, preferred_element_type=F32)
    tile = (iota((rows, TILES), 1) + 1).astype(F32)
    chosen = jnp.where(label == tile, 1.0, 0.0).astype(BF)
    total = lax.dot_general(chosen, slots, (((0,), (0,)), ((), ())), preferred_element_type=F32)
    u, v, ta, q, rad, pr = (total[:, f * CELLS : (f + 1) * CELLS] for f in range(SENT))
    rest = jnp.where(iota((TILES, LANES), 1) == 0, 0.0, total[:, SENT * CELLS :])
    u = jnp.concatenate([u[:, :LANES] + rest, u[:, LANES:]], axis=1)
    warmth = sst[...]
    w = marine[...].astype(F32)
    speed = jnp.sqrt(u * u + v * v + 0.25)
    dth = warmth - ta
    dq = 0.4 * warmth - q
    lift = 2.0 * (dth + 0.5 * dq)
    c = jnp.ones_like(speed)
    for _ in range(3):
        c = 1.0 + 0.5 * jnp.tanh(lift / (1.0 + c * speed * speed))
    k = c * speed
    found = (k * u * w, k * v * w, (rad - k * dth - k * dq) * w, (pr - 0.5 * k * dq) * w)
    for f, x in enumerate(found):
        fluxes[:, f, :] = x
    back = jnp.concatenate([x.astype(BF) for x in found + (warmth * w,)], axis=1)
    out[...] = jnp.dot(chosen, back, preferred_element_type=F32).astype(BF).reshape(out.shape)


def deliver(
    src_row, places, returned, weights, fluxes, fluxes_hbm, out, values, terms, sums, sem
):
    copy = pltpu.make_async_copy(fluxes, fluxes_hbm, sem)
    copy.start()
    row_of_places, sources = places[...], src_row[...]
    place = [row_of_places[0, p] for p in range(PAIRS)]
    src = [sources[0, p] for p in range(PAIRS)]
    values[...] = jnp.zeros_like(values)
    for p in range(PAIRS):
        second = functools.reduce(jnp.logical_or, [place[q] == place[p] for q in range(p)], False)
        slots = returned[place[p]].astype(F32)
        slot = jnp.where(second, slots[1:], slots[:1])
        for f in range(BACK):
            for h in range(2):
                start = f * CELLS + h * LANES
                values[h, p * FIELDS + f : p * FIELDS + f + 1, :] = slot[:, start : start + LANES]
    sums[...] = jnp.zeros_like(sums)
    for p in range(PAIRS):
        block = pl.ds(p * FIELDS, FIELDS)
        term = lax.dot_general(
            jnp.concatenate([values[h, block, :] for h in range(2)], axis=1).astype(BF),
            weights[p],
            (((1,), (1,)), ((), ())),
            preferred_element_type=F32,
        )
        for h in range(2):
            terms[h, block, :] = term[:, h * LANES : (h + 1) * LANES]
    for p in range(PAIRS):
        block = pl.ds(p * FIELDS, FIELDS)
        at = pl.ds(pl.multiple_of(src[p] * FIELDS, FIELDS), FIELDS)
        for h in range(2):
            sums[h, at, :] += terms[h, block, :]
    for f in range(BACK):
        for h in range(2):
            out[f, :, h * LANES : (h + 1) * LANES] = sums[h, pl.ds(f, TILES, stride=FIELDS), :]
    copy.wait()


VMEM = pl.BlockSpec(memory_space=pltpu.VMEM)
HBM = pl.BlockSpec(memory_space=pltpu.HBM)


def on_device(sky, weights, sky_block, target_device, sea_block, sst, marine):
    devices = lax.axis_size(("gx", "gy"))
    params = pltpu.CompilerParams(vmem_limit_bytes=VMEM_LIMIT)
    flux_shape = jax.ShapeDtypeStruct((TILES, 4, CELLS), F32)

    def wire(width):
        return jax.ShapeDtypeStruct((devices, SLOTS, width), BF)

    def swap(x):
        order = sorted(range(devices), key=key_of)
        return lax.all_to_all(
            x,
            ("gx", "gy"),
            split_axis=0,
            concat_axis=0,
            axis_index_groups=[order],
            tiled=True,
        )

    def stay(*arrays):
        return tuple(pltpu.with_memory_space_constraint(x, pltpu.HBM) for x in arrays)

    outgoing, sst, marine, places = pl.pallas_call(
        contribute,
        out_shape=(
            wire(OUT_WIDTH),
            jax.ShapeDtypeStruct((TILES, CELLS), F32),
            jax.ShapeDtypeStruct((TILES, CELLS), jnp.int32),
            jax.ShapeDtypeStruct((1, PAIRS), jnp.int32),
        ),
        in_specs=[HBM] * 7,
        out_specs=(VMEM,) * 4,
        scratch_shapes=[
            pltpu.SMEM((PAIRS,), jnp.int32),
            pltpu.SMEM((PAIRS,), jnp.int32),
            pltpu.SMEM((PAIRS,), jnp.int32),
            pltpu.VMEM((TILES, FIELDS, CELLS), BF),
            pltpu.VMEM((2, PAIRS, LANES + STRIP, LANES), BF),
            pltpu.VMEM((PAIRS, STRIP, LANES), BF),
            pltpu.VMEM((PAIRS, STRIP, LANES), BF),
            pltpu.VMEM((2, PAIRS * FIELDS, LANES), F32),
            pltpu.SemaphoreType.DMA((10,)),
        ],
        compiler_params=params,
    )(*stay(sky_block, target_device.reshape(PAIRS), sea_block, sky, weights, sst, marine))
    fluxes, back = pl.pallas_call(
        exchange,
        out_shape=(flux_shape, wire(BACK_WIDTH)),
        in_specs=[VMEM] * 3,
        out_specs=(VMEM, VMEM),
        compiler_params=params,
    )(swap(outgoing), sst, marine)
    fluxes, atm_back = pl.pallas_call(
        deliver,
        out_shape=(flux_shape, jax.ShapeDtypeStruct((BACK, TILES, CELLS), F32)),
        in_specs=[VMEM] * 5,
        out_specs=(HBM, VMEM),
        scratch_shapes=[
            pltpu.VMEM((2, PAIRS * FIELDS, LANES), F32),
            pltpu.VMEM((2, PAIRS * FIELDS, LANES), F32),
            pltpu.VMEM((2, TILES * FIELDS, LANES), F32),
            pltpu.SemaphoreType.DMA,
        ],
        compiler_params=params,
    )(sky_block.reshape(1, PAIRS), places, swap(back), weights, fluxes)
    return fluxes, jnp.transpose(atm_back, (1, 0, 2))


def solution(mesh):
    tiles = P(("gx", "gy"), None, None)
    cells = P(("gx", "gy"), None)
    flat = P(("gx", "gy"))
    return jax.shard_map(
        on_device,
        mesh=mesh,
        in_specs=(tiles, tiles, flat, cells, flat, cells, cells),
        out_specs=(tiles, tiles),
        check_vma=False,
    )
```

```python
import functools

import jax
import jax.numpy as jnp
from jax import lax
from jax.experimental import pallas as pl
from jax.experimental.pallas import tpu as pltpu
from jax.sharding import PartitionSpec as P

PAIRS = 16
TILES = 16
FIELDS = 8
SENT = 6
BACK = 5
CELLS = 256
LANES = 128
SLOTS = 2
STRIP = 16
OUT_WIDTH = SENT * CELLS + LANES
BACK_WIDTH = BACK * CELLS
BF = jnp.bfloat16
F32 = jnp.float32
VMEM_LIMIT = 24 * 1024 * 1024


def iota(shape, dim):
    return lax.broadcasted_iota(jnp.int32, shape, dim)


def key_of(device):
    return ((device >> 5) + ((device >> 3) & 3) + ((device >> 1) & 3)) * 128 + device


def places_of(column, devices):
    others = key_of(iota((PAIRS, devices), 1))
    ahead = jnp.where(others < key_of(column.astype(jnp.int32)), 1.0, 0.0)
    return to_row(jnp.sum(ahead, axis=1, keepdims=True)).astype(jnp.int32)


def to_column(row):
    same = iota((PAIRS, PAIRS), 0) == iota((PAIRS, PAIRS), 1)
    return jnp.sum(jnp.where(same, row, 0.0), axis=1, keepdims=True)


def to_row(column):
    same = iota((PAIRS, PAIRS), 0) == iota((PAIRS, PAIRS), 1)
    return jnp.sum(jnp.where(same, column, 0.0), axis=0, keepdims=True)


def contribute(
    src_hbm, owner_hbm, sea_hbm, sky_hbm, weights_hbm, sst_hbm, marine_hbm, out, sst, marine, places,
    src, owner, sea, sky, cells, blocks, top, bottom, scratch, sems,
):
    copies = {}

    def fetch(name, source, held):
        copies[name] = pltpu.make_async_copy(source, held, sems.at[len(copies)])
        copies[name].start()

    left, right = pl.ds(0, LANES), pl.ds(LANES, LANES)
    every = pl.ds(0, PAIRS)
    fetch("upper", weights_hbm.at[every, pl.ds(0, LANES + STRIP), left], blocks.at[0])
    fetch("bottom", weights_hbm.at[every, pl.ds(CELLS - STRIP, STRIP), left], bottom)
    fetch("owner", owner_hbm, owner)
    fetch("sea", sea_hbm, sea)
    fetch("src", src_hbm, src)
    fetch("sky", sky_hbm, sky)
    fetch(
        "lower",
        weights_hbm.at[every, pl.ds(LANES - STRIP, LANES + STRIP), right],
        blocks.at[1],
    )
    fetch("top", weights_hbm.at[every, pl.ds(0, STRIP), right], top)
    fetch("sst", sst_hbm, sst)
    fetch("marine", marine_hbm, marine)
    out[...] = jnp.zeros_like(out)
    copies["owner"].wait()
    copies["sea"].wait()
    at = iota((PAIRS, PAIRS), 1)
    row = jnp.zeros((PAIRS, PAIRS), jnp.int32)
    tiles = jnp.zeros((PAIRS, LANES), jnp.int32)
    for p in range(PAIRS):
        row = jnp.where(at == p, owner[p], row)
        tiles = jnp.where(iota((PAIRS, LANES), 0) == p, sea[p], tiles)
    row = row[:1].astype(F32)
    column = to_column(row)
    before = at < iota((PAIRS, PAIRS), 0)
    rank = jnp.sum(jnp.where((column == row) & before, 1.0, 0.0), axis=1, keepdims=True)
    both = SLOTS * PAIRS
    wanted, pair = iota((both, PAIRS), 0), iota((both, PAIRS), 1)
    mine = jnp.sum(jnp.where(wanted // SLOTS == pair, row, 0.0), axis=1, keepdims=True)
    fits = (mine == row) & ((wanted % SLOTS).astype(F32) == to_row(rank))
    chosen = jnp.where(fits, 1.0, 0.0).astype(BF)
    label = tiles.astype(F32) + 1.0
    row_of_places = places_of(column, out.shape[0])
    places[...] = row_of_places
    place = [row_of_places[0, p] for p in range(PAIRS)]
    for name in ("src", "sky"):
        copies[name].wait()
    wide = sky[...].astype(F32).reshape(TILES * FIELDS, CELLS)
    sides = (wide[:, :LANES], wide[:, LANES:])
    lane = iota((TILES * FIELDS, LANES), 1)
    for h in range(2):
        ends = jnp.where(lane < STRIP, sides[1 - h], pltpu.roll(sides[1 - h], 2 * STRIP, 1))
        gathered = jnp.concatenate([sides[h], ends], axis=1).astype(BF)
        cells[h] = gathered.reshape(TILES, FIELDS, CELLS)
    for h, needed in enumerate((("upper", "bottom"), ("lower", "top"))):
        for name in needed:
            copies[name].wait()
        for p in range(PAIRS):
            if h == 0:
                parts = [blocks[0, p], bottom[p]]
            else:
                parts = [blocks[1, p, STRIP:], top[p], blocks[1, p, :STRIP]]
            scratch[h, p * FIELDS : (p + 1) * FIELDS, :] = jnp.dot(
                cells[h, src[p]][:, : LANES + 2 * STRIP],
                jnp.concatenate(parts, axis=0),
                preferred_element_type=F32,
            )

    def field(f):
        parts = [scratch[h, pl.ds(f, PAIRS, stride=FIELDS), :] for h in range(2)]
        return jnp.concatenate(parts, axis=1)

    u, v, ta, qa, sw, lw, pr, ps = (field(f) for f in range(FIELDS))
    sent = [x.astype(BF) for x in (u, v, ta, qa - 0.3 * ps, 0.5 * sw + 0.3 * lw, pr)]
    rest = (u - sent[0].astype(F32))[:, :LANES]
    sent.append(jnp.where(iota((PAIRS, LANES), 1) == 0, label, rest).astype(BF))
    filled = jnp.dot(chosen, jnp.concatenate(sent, axis=1), preferred_element_type=F32)
    filled = filled.astype(BF).reshape(PAIRS, SLOTS, OUT_WIDTH)
    for p in range(PAIRS):
        out[place[p]] = filled[p]
    copies["sst"].wait()
    copies["marine"].wait()


def exchange(arrived, sst, marine, fluxes, out):
    rows = arrived.shape[0] * arrived.shape[1]
    slots = arrived[...].reshape(rows, OUT_WIDTH)
    first = jnp.where(iota((LANES, TILES), 0) == 0, 1.0, 0.0).astype(BF)
    label = jnp.dot(slots[:, SENT * CELLS :], first, preferred_element_type=F32)
    tile = (iota((rows, TILES), 1) + 1).astype(F32)
    chosen = jnp.where(label == tile, 1.0, 0.0).astype(BF)
    total = lax.dot_general(chosen, slots, (((0,), (0,)), ((), ())), preferred_element_type=F32)
    u, v, ta, q, rad, pr = (total[:, f * CELLS : (f + 1) * CELLS] for f in range(SENT))
    rest = jnp.where(iota((TILES, LANES), 1) == 0, 0.0, total[:, SENT * CELLS :])
    u = jnp.concatenate([u[:, :LANES] + rest, u[:, LANES:]], axis=1)
    warmth = sst[...]
    w = marine[...].astype(F32)
    speed = jnp.sqrt(u * u + v * v + 0.25)
    dth = warmth - ta
    dq = 0.4 * warmth - q
    lift = 2.0 * (dth + 0.5 * dq)
    c = jnp.ones_like(speed)
    for _ in range(3):
        c = 1.0 + 0.5 * jnp.tanh(lift / (1.0 + c * speed * speed))
    k = c * speed
    found = (k * u * w, k * v * w, (rad - k * dth - k * dq) * w, (pr - 0.5 * k * dq) * w)
    for f, x in enumerate(found):
        fluxes[:, f, :] = x
    back = jnp.concatenate([x.astype(BF) for x in found + (warmth * w,)], axis=1)
    out[...] = jnp.dot(chosen, back, preferred_element_type=F32).astype(BF).reshape(out.shape)


def deliver(
    src_row, places, returned, weights, fluxes, fluxes_hbm, out, values, terms, sums, sem
):
    copy = pltpu.make_async_copy(fluxes, fluxes_hbm, sem)
    copy.start()
    row_of_places, sources = places[...], src_row[...]
    place = [row_of_places[0, p] for p in range(PAIRS)]
    src = [sources[0, p] for p in range(PAIRS)]
    values[...] = jnp.zeros_like(values)
    for p in range(PAIRS):
        second = functools.reduce(jnp.logical_or, [place[q] == place[p] for q in range(p)], False)
        slots = returned[place[p]].astype(F32)
        slot = jnp.where(second, slots[1:], slots[:1])
        for f in range(BACK):
            for h in range(2):
                start = f * CELLS + h * LANES
                values[h, p * FIELDS + f : p * FIELDS + f + 1, :] = slot[:, start : start + LANES]
    sums[...] = jnp.zeros_like(sums)
    for p in range(PAIRS):
        block = pl.ds(p * FIELDS, FIELDS)
        term = lax.dot_general(
            jnp.concatenate([values[h, block, :] for h in range(2)], axis=1).astype(BF),
            weights[p],
            (((1,), (1,)), ((), ())),
            preferred_element_type=F32,
        )
        for h in range(2):
            terms[h, block, :] = term[:, h * LANES : (h + 1) * LANES]
    for p in range(PAIRS):
        block = pl.ds(p * FIELDS, FIELDS)
        at = pl.ds(pl.multiple_of(src[p] * FIELDS, FIELDS), FIELDS)
        for h in range(2):
            sums[h, at, :] += terms[h, block, :]
    for f in range(BACK):
        for h in range(2):
            out[f, :, h * LANES : (h + 1) * LANES] = sums[h, pl.ds(f, TILES, stride=FIELDS), :]
    copy.wait()


VMEM = pl.BlockSpec(memory_space=pltpu.VMEM)
HBM = pl.BlockSpec(memory_space=pltpu.HBM)


def on_device(sky, weights, sky_block, target_device, sea_block, sst, marine):
    devices = lax.axis_size(("gx", "gy"))
    params = pltpu.CompilerParams(vmem_limit_bytes=VMEM_LIMIT)
    flux_shape = jax.ShapeDtypeStruct((TILES, 4, CELLS), F32)

    def wire(width):
        return jax.ShapeDtypeStruct((devices, SLOTS, width), BF)

    def swap(x):
        order = sorted(range(devices), key=key_of)
        return lax.all_to_all(
            x,
            ("gx", "gy"),
            split_axis=0,
            concat_axis=0,
            axis_index_groups=[order],
            tiled=True,
        )

    def stay(*arrays):
        return tuple(pltpu.with_memory_space_constraint(x, pltpu.HBM) for x in arrays)

    outgoing, sst, marine, places = pl.pallas_call(
        contribute,
        out_shape=(
            wire(OUT_WIDTH),
            jax.ShapeDtypeStruct((TILES, CELLS), F32),
            jax.ShapeDtypeStruct((TILES, CELLS), jnp.int32),
            jax.ShapeDtypeStruct((1, PAIRS), jnp.int32),
        ),
        in_specs=[HBM] * 7,
        out_specs=(VMEM,) * 4,
        scratch_shapes=[
            pltpu.SMEM((PAIRS,), jnp.int32),
            pltpu.SMEM((PAIRS,), jnp.int32),
            pltpu.SMEM((PAIRS,), jnp.int32),
            pltpu.VMEM((TILES, FIELDS, CELLS), BF),
            pltpu.VMEM((2, TILES, FIELDS, CELLS), BF),
            pltpu.VMEM((2, PAIRS, LANES + STRIP, LANES), BF),
            pltpu.VMEM((PAIRS, STRIP, LANES), BF),
            pltpu.VMEM((PAIRS, STRIP, LANES), BF),
            pltpu.VMEM((2, PAIRS * FIELDS, LANES), F32),
            pltpu.SemaphoreType.DMA((10,)),
        ],
        compiler_params=params,
    )(*stay(sky_block, target_device.reshape(PAIRS), sea_block, sky, weights, sst, marine))
    fluxes, back = pl.pallas_call(
        exchange,
        out_shape=(flux_shape, wire(BACK_WIDTH)),
        in_specs=[VMEM] * 3,
        out_specs=(VMEM, VMEM),
        compiler_params=params,
    )(swap(outgoing), sst, marine)
    fluxes, atm_back = pl.pallas_call(
        deliver,
        out_shape=(flux_shape, jax.ShapeDtypeStruct((BACK, TILES, CELLS), F32)),
        in_specs=[VMEM] * 5,
        out_specs=(HBM, VMEM),
        scratch_shapes=[
            pltpu.VMEM((2, PAIRS * FIELDS, LANES), F32),
            pltpu.VMEM((2, PAIRS * FIELDS, LANES), F32),
            pltpu.VMEM((2, TILES * FIELDS, LANES), F32),
            pltpu.SemaphoreType.DMA,
        ],
        compiler_params=params,
    )(sky_block.reshape(1, PAIRS), places, swap(back), weights, fluxes)
    return fluxes, jnp.transpose(atm_back, (1, 0, 2))


def solution(mesh):
    tiles = P(("gx", "gy"), None, None)
    cells = P(("gx", "gy"), None)
    flat = P(("gx", "gy"))
    return jax.shard_map(
        on_device,
        mesh=mesh,
        in_specs=(tiles, tiles, flat, cells, flat, cells, cells),
        out_specs=(tiles, tiles),
        check_vma=False,
    )
```

```python
import functools

import jax
import jax.numpy as jnp
from jax import lax
from jax.experimental import pallas as pl
from jax.experimental.pallas import tpu as pltpu
from jax.sharding import PartitionSpec as P

PAIRS = 16
TILES = 16
FIELDS = 8
SENT = 6
BACK = 5
CELLS = 256
LANES = 128
SLOTS = 2
STRIP = 16
OUT_WIDTH = SENT * CELLS + LANES
BACK_WIDTH = BACK * CELLS
BF = jnp.bfloat16
F32 = jnp.float32
VMEM_LIMIT = 24 * 1024 * 1024


def iota(shape, dim):
    return lax.broadcasted_iota(jnp.int32, shape, dim)


def key_of(device):
    return ((device >> 5) + ((device >> 3) & 3) + ((device >> 1) & 3)) * 128 + device


def places_of(column, devices):
    others = key_of(iota((PAIRS, devices), 1))
    ahead = jnp.where(others < key_of(column.astype(jnp.int32)), 1.0, 0.0)
    return to_row(jnp.sum(ahead, axis=1, keepdims=True)).astype(jnp.int32)


def to_column(row):
    same = iota((PAIRS, PAIRS), 0) == iota((PAIRS, PAIRS), 1)
    return jnp.sum(jnp.where(same, row, 0.0), axis=1, keepdims=True)


def to_row(column):
    same = iota((PAIRS, PAIRS), 0) == iota((PAIRS, PAIRS), 1)
    return jnp.sum(jnp.where(same, column, 0.0), axis=0, keepdims=True)


def contribute(
    src_hbm, owner_hbm, sea_hbm, sky_hbm, weights_hbm, sst_hbm, marine_hbm, out, sst, marine, places,
    src, owner, sea, sky, blocks, top, bottom, scratch, sems,
):
    copies = {}

    def fetch(name, source, held):
        copies[name] = pltpu.make_async_copy(source, held, sems.at[len(copies)])
        copies[name].start()

    left, right = pl.ds(0, LANES), pl.ds(LANES, LANES)
    every = pl.ds(0, PAIRS)
    fetch("upper", weights_hbm.at[every, pl.ds(0, LANES + STRIP), left], blocks.at[0])
    fetch("bottom", weights_hbm.at[every, pl.ds(CELLS - STRIP, STRIP), left], bottom)
    fetch("owner", owner_hbm, owner)
    fetch("sea", sea_hbm, sea)
    fetch("src", src_hbm, src)
    fetch("sky", sky_hbm, sky)
    fetch(
        "lower",
        weights_hbm.at[every, pl.ds(LANES - STRIP, LANES + STRIP), right],
        blocks.at[1],
    )
    fetch("top", weights_hbm.at[every, pl.ds(0, STRIP), right], top)
    fetch("sst", sst_hbm, sst)
    fetch("marine", marine_hbm, marine)
    out[...] = jnp.zeros_like(out)
    gap = jnp.zeros((LANES - 2 * STRIP, LANES), BF)

    def product(h, p):
        parts = [top[p], gap, blocks[1, p]] if h else [blocks[0, p], gap, bottom[p]]
        scratch[h, p * FIELDS : (p + 1) * FIELDS, :] = jnp.dot(
            sky[src[p]], jnp.concatenate(parts, axis=0), preferred_element_type=F32
        )

    for name in ("owner", "sea", "src", "sky", "upper", "bottom"):
        copies[name].wait()
    for p in range(PAIRS):
        product(0, p)
    at = iota((PAIRS, PAIRS), 1)
    row = jnp.zeros((PAIRS, PAIRS), jnp.int32)
    tiles = jnp.zeros((PAIRS, LANES), jnp.int32)
    for p in range(PAIRS):
        row = jnp.where(at == p, owner[p], row)
        tiles = jnp.where(iota((PAIRS, LANES), 0) == p, sea[p], tiles)
    row = row[:1].astype(F32)
    column = to_column(row)
    before = at < iota((PAIRS, PAIRS), 0)
    rank = jnp.sum(jnp.where((column == row) & before, 1.0, 0.0), axis=1, keepdims=True)
    both = SLOTS * PAIRS
    wanted, pair = iota((both, PAIRS), 0), iota((both, PAIRS), 1)
    mine = jnp.sum(jnp.where(wanted // SLOTS == pair, row, 0.0), axis=1, keepdims=True)
    fits = (mine == row) & ((wanted % SLOTS).astype(F32) == to_row(rank))
    chosen = jnp.where(fits, 1.0, 0.0).astype(BF)
    label = tiles.astype(F32) + 1.0
    row_of_places = places_of(column, out.shape[0])
    places[...] = row_of_places
    place = [row_of_places[0, p] for p in range(PAIRS)]
    for name in ("lower", "top"):
        copies[name].wait()
    for p in range(PAIRS):
        product(1, p)

    def field(f):
        parts = [scratch[h, pl.ds(f, PAIRS, stride=FIELDS), :] for h in range(2)]
        return jnp.concatenate(parts, axis=1)

    u, v, ta, qa, sw, lw, pr, ps = (field(f) for f in range(FIELDS))
    sent = [x.astype(BF) for x in (u, v, ta, qa - 0.3 * ps, 0.5 * sw + 0.3 * lw, pr)]
    rest = (u - sent[0].astype(F32))[:, :LANES]
    sent.append(jnp.where(iota((PAIRS, LANES), 1) == 0, label, rest).astype(BF))
    filled = jnp.dot(chosen, jnp.concatenate(sent, axis=1), preferred_element_type=F32)
    filled = filled.astype(BF).reshape(PAIRS, SLOTS, OUT_WIDTH)
    for p in range(PAIRS):
        out[place[p]] = filled[p]
    copies["sst"].wait()
    copies["marine"].wait()


def exchange(arrived, sst, marine, fluxes, out):
    rows = arrived.shape[0] * arrived.shape[1]
    slots = arrived[...].reshape(rows, OUT_WIDTH)
    first = jnp.where(iota((LANES, TILES), 0) == 0, 1.0, 0.0).astype(BF)
    label = jnp.dot(slots[:, SENT * CELLS :], first, preferred_element_type=F32)
    tile = (iota((rows, TILES), 1) + 1).astype(F32)
    chosen = jnp.where(label == tile, 1.0, 0.0).astype(BF)
    total = lax.dot_general(chosen, slots, (((0,), (0,)), ((), ())), preferred_element_type=F32)
    u, v, ta, q, rad, pr = (total[:, f * CELLS : (f + 1) * CELLS] for f in range(SENT))
    rest = jnp.where(iota((TILES, LANES), 1) == 0, 0.0, total[:, SENT * CELLS :])
    u = jnp.concatenate([u[:, :LANES] + rest, u[:, LANES:]], axis=1)
    warmth = sst[...]
    w = marine[...].astype(F32)
    speed = jnp.sqrt(u * u + v * v + 0.25)
    dth = warmth - ta
    dq = 0.4 * warmth - q
    lift = 2.0 * (dth + 0.5 * dq)
    c = jnp.ones_like(speed)
    for _ in range(3):
        c = 1.0 + 0.5 * jnp.tanh(lift / (1.0 + c * speed * speed))
    k = c * speed
    found = (k * u * w, k * v * w, (rad - k * dth - k * dq) * w, (pr - 0.5 * k * dq) * w)
    for f, x in enumerate(found):
        fluxes[:, f, :] = x
    back = jnp.concatenate([x.astype(BF) for x in found + (warmth * w,)], axis=1)
    out[...] = jnp.dot(chosen, back, preferred_element_type=F32).astype(BF).reshape(out.shape)


def deliver(
    src_row, places, returned, weights, fluxes, fluxes_hbm, out, values, terms, sums, sem
):
    copy = pltpu.make_async_copy(fluxes, fluxes_hbm, sem)
    copy.start()
    row_of_places, sources = places[...], src_row[...]
    place = [row_of_places[0, p] for p in range(PAIRS)]
    src = [sources[0, p] for p in range(PAIRS)]
    values[...] = jnp.zeros_like(values)
    for p in range(PAIRS):
        second = functools.reduce(jnp.logical_or, [place[q] == place[p] for q in range(p)], False)
        slots = returned[place[p]].astype(F32)
        slot = jnp.where(second, slots[1:], slots[:1])
        for f in range(BACK):
            for h in range(2):
                start = f * CELLS + h * LANES
                values[h, p * FIELDS + f : p * FIELDS + f + 1, :] = slot[:, start : start + LANES]
    sums[...] = jnp.zeros_like(sums)
    for p in range(PAIRS):
        block = pl.ds(p * FIELDS, FIELDS)
        term = lax.dot_general(
            jnp.concatenate([values[h, block, :] for h in range(2)], axis=1).astype(BF),
            weights[p],
            (((1,), (1,)), ((), ())),
            preferred_element_type=F32,
        )
        for h in range(2):
            terms[h, block, :] = term[:, h * LANES : (h + 1) * LANES]
    for p in range(PAIRS):
        block = pl.ds(p * FIELDS, FIELDS)
        at = pl.ds(pl.multiple_of(src[p] * FIELDS, FIELDS), FIELDS)
        for h in range(2):
            sums[h, at, :] += terms[h, block, :]
    for f in range(BACK):
        for h in range(2):
            out[f, :, h * LANES : (h + 1) * LANES] = sums[h, pl.ds(f, TILES, stride=FIELDS), :]
    copy.wait()


VMEM = pl.BlockSpec(memory_space=pltpu.VMEM)
HBM = pl.BlockSpec(memory_space=pltpu.HBM)


def on_device(sky, weights, sky_block, target_device, sea_block, sst, marine):
    devices = lax.axis_size(("gx", "gy"))
    params = pltpu.CompilerParams(vmem_limit_bytes=VMEM_LIMIT)
    flux_shape = jax.ShapeDtypeStruct((TILES, 4, CELLS), F32)

    def wire(width):
        return jax.ShapeDtypeStruct((devices, SLOTS, width), BF)

    def swap(x):
        order = sorted(range(devices), key=key_of)
        return lax.all_to_all(
            x,
            ("gx", "gy"),
            split_axis=0,
            concat_axis=0,
            axis_index_groups=[order],
            tiled=True,
        )

    def stay(*arrays):
        return tuple(pltpu.with_memory_space_constraint(x, pltpu.HBM) for x in arrays)

    outgoing, sst, marine, places = pl.pallas_call(
        contribute,
        out_shape=(
            wire(OUT_WIDTH),
            jax.ShapeDtypeStruct((TILES, CELLS), F32),
            jax.ShapeDtypeStruct((TILES, CELLS), jnp.int32),
            jax.ShapeDtypeStruct((1, PAIRS), jnp.int32),
        ),
        in_specs=[HBM] * 7,
        out_specs=(VMEM,) * 4,
        scratch_shapes=[
            pltpu.SMEM((PAIRS,), jnp.int32),
            pltpu.SMEM((PAIRS,), jnp.int32),
            pltpu.SMEM((PAIRS,), jnp.int32),
            pltpu.VMEM((TILES, FIELDS, CELLS), BF),
            pltpu.VMEM((2, PAIRS, LANES + STRIP, LANES), BF),
            pltpu.VMEM((PAIRS, STRIP, LANES), BF),
            pltpu.VMEM((PAIRS, STRIP, LANES), BF),
            pltpu.VMEM((2, PAIRS * FIELDS, LANES), F32),
            pltpu.SemaphoreType.DMA((10,)),
        ],
        compiler_params=params,
    )(*stay(sky_block, target_device.reshape(PAIRS), sea_block, sky, weights, sst, marine))
    fluxes, back = pl.pallas_call(
        exchange,
        out_shape=(flux_shape, wire(BACK_WIDTH)),
        in_specs=[VMEM] * 3,
        out_specs=(VMEM, VMEM),
        compiler_params=params,
    )(swap(outgoing), sst, marine)
    fluxes, atm_back = pl.pallas_call(
        deliver,
        out_shape=(flux_shape, jax.ShapeDtypeStruct((BACK, TILES, CELLS), F32)),
        in_specs=[VMEM] * 5,
        out_specs=(HBM, VMEM),
        scratch_shapes=[
            pltpu.VMEM((2, PAIRS * FIELDS, LANES), F32),
            pltpu.VMEM((2, PAIRS * FIELDS, LANES), F32),
            pltpu.VMEM((2, TILES * FIELDS, LANES), F32),
            pltpu.SemaphoreType.DMA,
        ],
        compiler_params=params,
    )(sky_block.reshape(1, PAIRS), places, swap(back), weights, fluxes)
    return fluxes, jnp.transpose(atm_back, (1, 0, 2))


def solution(mesh):
    tiles = P(("gx", "gy"), None, None)
    cells = P(("gx", "gy"), None)
    flat = P(("gx", "gy"))
    return jax.shard_map(
        on_device,
        mesh=mesh,
        in_specs=(tiles, tiles, flat, cells, flat, cells, cells),
        out_specs=(tiles, tiles),
        check_vma=False,
    )
```

```python
import functools

import jax
import jax.numpy as jnp
from jax import lax
from jax.experimental import pallas as pl
from jax.experimental.pallas import tpu as pltpu
from jax.sharding import PartitionSpec as P

PAIRS = 16
TILES = 16
FIELDS = 8
SENT = 6
BACK = 5
CELLS = 256
LANES = 128
SLOTS = 2
STRIP = 16
OUT_WIDTH = SENT * CELLS + LANES
BACK_WIDTH = BACK * CELLS
BF = jnp.bfloat16
F32 = jnp.float32
VMEM_LIMIT = 24 * 1024 * 1024


def iota(shape, dim):
    return lax.broadcasted_iota(jnp.int32, shape, dim)


def key_of(device):
    return ((device >> 5) + ((device >> 3) & 3) + ((device >> 1) & 3)) * 128 + device


def places_of(column, devices):
    others = key_of(iota((PAIRS, devices), 1))
    ahead = jnp.where(others < key_of(column.astype(jnp.int32)), 1.0, 0.0)
    return to_row(jnp.sum(ahead, axis=1, keepdims=True)).astype(jnp.int32)


def to_column(row):
    same = iota((PAIRS, PAIRS), 0) == iota((PAIRS, PAIRS), 1)
    return jnp.sum(jnp.where(same, row, 0.0), axis=1, keepdims=True)


def to_row(column):
    same = iota((PAIRS, PAIRS), 0) == iota((PAIRS, PAIRS), 1)
    return jnp.sum(jnp.where(same, column, 0.0), axis=0, keepdims=True)


def contribute(
    src_hbm, owner_hbm, sea_hbm, sky_hbm, weights_hbm, sst_hbm, marine_hbm, out, sst, marine, places,
    src, owner, sea, sky, blocks, top, bottom, scratch, sems,
):
    copies = {}

    def fetch(name, source, held):
        copies[name] = pltpu.make_async_copy(source, held, sems.at[len(copies)])
        copies[name].start()

    left, right = pl.ds(0, LANES), pl.ds(LANES, LANES)
    every = pl.ds(0, PAIRS)
    fetch("upper", weights_hbm.at[every, pl.ds(0, LANES + STRIP), left], blocks.at[0])
    fetch("bottom", weights_hbm.at[every, pl.ds(CELLS - STRIP, STRIP), left], bottom)
    fetch("owner", owner_hbm, owner)
    fetch("sea", sea_hbm, sea)
    fetch("src", src_hbm, src)
    fetch("sky", sky_hbm, sky)
    fetch(
        "lower",
        weights_hbm.at[every, pl.ds(LANES - STRIP, LANES + STRIP), right],
        blocks.at[1],
    )
    fetch("top", weights_hbm.at[every, pl.ds(0, STRIP), right], top)
    fetch("sst", sst_hbm, sst)
    fetch("marine", marine_hbm, marine)
    out[...] = jnp.zeros_like(out)
    gap = jnp.zeros((LANES - 2 * STRIP, LANES), BF)

    def product(h, p):
        parts = [top[p], gap, blocks[1, p]] if h else [blocks[0, p], gap, bottom[p]]
        scratch[h, p * FIELDS : (p + 1) * FIELDS, :] = jnp.dot(
            sky[src[p]], jnp.concatenate(parts, axis=0), preferred_element_type=F32
        )

    for name in ("owner", "sea", "src", "sky", "upper", "bottom"):
        copies[name].wait()
    for p in range(PAIRS):
        product(0, p)
    at = iota((PAIRS, PAIRS), 1)
    row = jnp.zeros((PAIRS, PAIRS), jnp.int32)
    tiles = jnp.zeros((PAIRS, LANES), jnp.int32)
    for p in range(PAIRS):
        row = jnp.where(at == p, owner[p], row)
        tiles = jnp.where(iota((PAIRS, LANES), 0) == p, sea[p], tiles)
    row = row[:1].astype(F32)
    column = to_column(row)
    before = at < iota((PAIRS, PAIRS), 0)
    rank = jnp.sum(jnp.where((column == row) & before, 1.0, 0.0), axis=1, keepdims=True)
    both = SLOTS * PAIRS
    wanted, pair = iota((both, PAIRS), 0), iota((both, PAIRS), 1)
    mine = jnp.sum(jnp.where(wanted // SLOTS == pair, row, 0.0), axis=1, keepdims=True)
    fits = (mine == row) & ((wanted % SLOTS).astype(F32) == to_row(rank))
    chosen = jnp.where(fits, 1.0, 0.0).astype(BF)
    label = tiles.astype(F32) + 1.0
    row_of_places = places_of(column, out.shape[0])
    places[...] = row_of_places
    place = [row_of_places[0, p] for p in range(PAIRS)]
    for name in ("lower", "top"):
        copies[name].wait()
    for p in range(PAIRS):
        product(1, p)

    def field(f):
        parts = [scratch[h, pl.ds(f, PAIRS, stride=FIELDS), :] for h in range(2)]
        return jnp.concatenate(parts, axis=1)

    u, v, ta, qa, sw, lw, pr, ps = (field(f) for f in range(FIELDS))
    sent = [x.astype(BF) for x in (u, v, ta, qa - 0.3 * ps, 0.5 * sw + 0.3 * lw, pr)]
    rest = (u - sent[0].astype(F32))[:, :LANES]
    sent.append(jnp.where(iota((PAIRS, LANES), 1) == 0, label, rest).astype(BF))
    filled = jnp.dot(chosen, jnp.concatenate(sent, axis=1), preferred_element_type=F32)
    filled = filled.astype(BF).reshape(PAIRS, SLOTS, OUT_WIDTH)
    for p in range(PAIRS):
        out[place[p]] = filled[p]
    copies["sst"].wait()
    copies["marine"].wait()


def exchange(arrived, sst, marine, fluxes, out):
    rows = arrived.shape[0] * arrived.shape[1]
    slots = arrived[...].reshape(rows, OUT_WIDTH)
    first = jnp.where(iota((LANES, TILES), 0) == 0, 1.0, 0.0).astype(BF)
    label = jnp.dot(slots[:, SENT * CELLS :], first, preferred_element_type=F32)
    tile = (iota((rows, TILES), 1) + 1).astype(F32)
    chosen = jnp.where(label == tile, 1.0, 0.0).astype(BF)
    total = lax.dot_general(chosen, slots, (((0,), (0,)), ((), ())), preferred_element_type=F32)
    u, v, ta, q, rad, pr = (total[:, f * CELLS : (f + 1) * CELLS] for f in range(SENT))
    rest = jnp.where(iota((TILES, LANES), 1) == 0, 0.0, total[:, SENT * CELLS :])
    u = jnp.concatenate([u[:, :LANES] + rest, u[:, LANES:]], axis=1)
    warmth = sst[...]
    w = marine[...].astype(F32)
    speed = jnp.sqrt(u * u + v * v + 0.25)
    dth = warmth - ta
    dq = 0.4 * warmth - q
    lift = 2.0 * (dth + 0.5 * dq)
    c = jnp.ones_like(speed)
    for _ in range(3):
        c = 1.0 + 0.5 * jnp.tanh(lift / (1.0 + c * speed * speed))
    k = c * speed
    found = (k * u * w, k * v * w, (rad - k * dth - k * dq) * w, (pr - 0.5 * k * dq) * w)
    for f, x in enumerate(found):
        fluxes[:, f, :] = x
    back = jnp.concatenate([x.astype(BF) for x in found + (warmth * w,)], axis=1)
    out[...] = jnp.dot(chosen, back, preferred_element_type=F32).astype(BF).reshape(out.shape)


def deliver(
    src_row, places, returned, weights, fluxes, fluxes_hbm, out, values, sums, sem
):
    copy = pltpu.make_async_copy(fluxes, fluxes_hbm, sem)
    copy.start()
    row_of_places, sources = places[...], src_row[...]
    place = [row_of_places[0, p] for p in range(PAIRS)]
    src = [sources[0, p] for p in range(PAIRS)]
    values[...] = jnp.zeros_like(values)
    for p in range(PAIRS):
        second = functools.reduce(jnp.logical_or, [place[q] == place[p] for q in range(p)], False)
        slots = returned[place[p]].astype(F32)
        slot = jnp.where(second, slots[1:], slots[:1])
        for f in range(BACK):
            for h in range(2):
                start = f * CELLS + h * LANES
                values[h, p * FIELDS + f : p * FIELDS + f + 1, :] = slot[:, start : start + LANES]
    sums[...] = jnp.zeros_like(sums)
    for p in range(PAIRS):
        block = pl.ds(p * FIELDS, FIELDS)
        term = lax.dot_general(
            jnp.concatenate([values[h, block, :] for h in range(2)], axis=1).astype(BF),
            weights[p],
            (((1,), (1,)), ((), ())),
            preferred_element_type=F32,
        )
        at = pl.ds(pl.multiple_of(src[p] * FIELDS, FIELDS), FIELDS)
        for h in range(2):
            sums[h, at, :] += term[:, h * LANES : (h + 1) * LANES]
    for f in range(BACK):
        for h in range(2):
            out[f, :, h * LANES : (h + 1) * LANES] = sums[h, pl.ds(f, TILES, stride=FIELDS), :]
    copy.wait()


VMEM = pl.BlockSpec(memory_space=pltpu.VMEM)
HBM = pl.BlockSpec(memory_space=pltpu.HBM)


def on_device(sky, weights, sky_block, target_device, sea_block, sst, marine):
    devices = lax.axis_size(("gx", "gy"))
    params = pltpu.CompilerParams(vmem_limit_bytes=VMEM_LIMIT)
    flux_shape = jax.ShapeDtypeStruct((TILES, 4, CELLS), F32)

    def wire(width):
        return jax.ShapeDtypeStruct((devices, SLOTS, width), BF)

    def swap(x):
        order = sorted(range(devices), key=key_of)
        return lax.all_to_all(
            x,
            ("gx", "gy"),
            split_axis=0,
            concat_axis=0,
            axis_index_groups=[order],
            tiled=True,
        )

    def stay(*arrays):
        return tuple(pltpu.with_memory_space_constraint(x, pltpu.HBM) for x in arrays)

    outgoing, sst, marine, places = pl.pallas_call(
        contribute,
        out_shape=(
            wire(OUT_WIDTH),
            jax.ShapeDtypeStruct((TILES, CELLS), F32),
            jax.ShapeDtypeStruct((TILES, CELLS), jnp.int32),
            jax.ShapeDtypeStruct((1, PAIRS), jnp.int32),
        ),
        in_specs=[HBM] * 7,
        out_specs=(VMEM,) * 4,
        scratch_shapes=[
            pltpu.SMEM((PAIRS,), jnp.int32),
            pltpu.SMEM((PAIRS,), jnp.int32),
            pltpu.SMEM((PAIRS,), jnp.int32),
            pltpu.VMEM((TILES, FIELDS, CELLS), BF),
            pltpu.VMEM((2, PAIRS, LANES + STRIP, LANES), BF),
            pltpu.VMEM((PAIRS, STRIP, LANES), BF),
            pltpu.VMEM((PAIRS, STRIP, LANES), BF),
            pltpu.VMEM((2, PAIRS * FIELDS, LANES), F32),
            pltpu.SemaphoreType.DMA((10,)),
        ],
        compiler_params=params,
    )(*stay(sky_block, target_device.reshape(PAIRS), sea_block, sky, weights, sst, marine))
    fluxes, back = pl.pallas_call(
        exchange,
        out_shape=(flux_shape, wire(BACK_WIDTH)),
        in_specs=[VMEM] * 3,
        out_specs=(VMEM, VMEM),
        compiler_params=params,
    )(swap(outgoing), sst, marine)
    fluxes, atm_back = pl.pallas_call(
        deliver,
        out_shape=(flux_shape, jax.ShapeDtypeStruct((BACK, TILES, CELLS), F32)),
        in_specs=[VMEM] * 5,
        out_specs=(HBM, VMEM),
        scratch_shapes=[
            pltpu.VMEM((2, PAIRS * FIELDS, LANES), F32),
            pltpu.VMEM((2, TILES * FIELDS, LANES), F32),
            pltpu.SemaphoreType.DMA,
        ],
        compiler_params=params,
    )(sky_block.reshape(1, PAIRS), places, swap(back), weights, fluxes)
    return fluxes, jnp.transpose(atm_back, (1, 0, 2))


def solution(mesh):
    tiles = P(("gx", "gy"), None, None)
    cells = P(("gx", "gy"), None)
    flat = P(("gx", "gy"))
    return jax.shard_map(
        on_device,
        mesh=mesh,
        in_specs=(tiles, tiles, flat, cells, flat, cells, cells),
        out_specs=(tiles, tiles),
        check_vma=False,
    )
```

```python
import functools

import jax
import jax.numpy as jnp
from jax import lax
from jax.experimental import pallas as pl
from jax.experimental.pallas import tpu as pltpu
from jax.sharding import PartitionSpec as P

PAIRS = 16
TILES = 16
FIELDS = 8
SENT = 6
BACK = 5
CELLS = 256
LANES = 128
SLOTS = 2
STRIP = 16
OUT_WIDTH = SENT * CELLS + LANES
BACK_WIDTH = BACK * CELLS
BF = jnp.bfloat16
F32 = jnp.float32
VMEM_LIMIT = 24 * 1024 * 1024


def iota(shape, dim):
    return lax.broadcasted_iota(jnp.int32, shape, dim)


def key_of(device):
    return ((device >> 5) + ((device >> 3) & 3) + ((device >> 1) & 3)) * 128 + device


def places_of(column, devices):
    others = key_of(iota((PAIRS, devices), 1))
    ahead = jnp.where(others < key_of(column.astype(jnp.int32)), 1.0, 0.0)
    return to_row(jnp.sum(ahead, axis=1, keepdims=True)).astype(jnp.int32)


def to_column(row):
    same = iota((PAIRS, PAIRS), 0) == iota((PAIRS, PAIRS), 1)
    return jnp.sum(jnp.where(same, row, 0.0), axis=1, keepdims=True)


def to_row(column):
    same = iota((PAIRS, PAIRS), 0) == iota((PAIRS, PAIRS), 1)
    return jnp.sum(jnp.where(same, column, 0.0), axis=0, keepdims=True)


def contribute(
    src_hbm, owner_hbm, sea_hbm, sky_hbm, weights_hbm, sst_hbm, marine_hbm, out, sst, marine, places,
    src, owner, sea, sky, blocks, top, bottom, scratch, sems,
):
    copies = {}

    def fetch(name, source, held):
        copies[name] = pltpu.make_async_copy(source, held, sems.at[len(copies)])
        copies[name].start()

    left, right = pl.ds(0, LANES), pl.ds(LANES, LANES)
    every = pl.ds(0, PAIRS)
    fetch("upper", weights_hbm.at[every, pl.ds(0, LANES + STRIP), left], blocks.at[0])
    fetch("bottom", weights_hbm.at[every, pl.ds(CELLS - STRIP, STRIP), left], bottom)
    fetch("owner", owner_hbm, owner)
    fetch("sea", sea_hbm, sea)
    fetch("src", src_hbm, src)
    fetch("sky", sky_hbm, sky)
    fetch(
        "lower",
        weights_hbm.at[every, pl.ds(LANES - STRIP, LANES + STRIP), right],
        blocks.at[1],
    )
    fetch("top", weights_hbm.at[every, pl.ds(0, STRIP), right], top)
    fetch("sst", sst_hbm, sst)
    fetch("marine", marine_hbm, marine)
    out[...] = jnp.zeros_like(out)
    gap = jnp.zeros((LANES - 2 * STRIP, LANES), BF)

    def product(h, p):
        parts = [top[p], gap, blocks[1, p]] if h else [blocks[0, p], gap, bottom[p]]
        scratch[h, p * FIELDS : (p + 1) * FIELDS, :] = jnp.dot(
            sky[src[p]], jnp.concatenate(parts, axis=0), preferred_element_type=F32
        )

    for name in ("owner", "sea", "src", "sky", "upper", "bottom"):
        copies[name].wait()
    for p in range(PAIRS):
        product(0, p)
    at = iota((PAIRS, PAIRS), 1)
    row = jnp.zeros((PAIRS, PAIRS), jnp.int32)
    tiles = jnp.zeros((PAIRS, LANES), jnp.int32)
    for p in range(PAIRS):
        row = jnp.where(at == p, owner[p], row)
        tiles = jnp.where(iota((PAIRS, LANES), 0) == p, sea[p], tiles)
    row = row[:1].astype(F32)
    column = to_column(row)
    before = at < iota((PAIRS, PAIRS), 0)
    rank = jnp.sum(jnp.where((column == row) & before, 1.0, 0.0), axis=1, keepdims=True)
    both = SLOTS * PAIRS
    wanted, pair = iota((both, PAIRS), 0), iota((both, PAIRS), 1)
    mine = jnp.sum(jnp.where(wanted // SLOTS == pair, row, 0.0), axis=1, keepdims=True)
    fits = (mine == row) & ((wanted % SLOTS).astype(F32) == to_row(rank))
    chosen = jnp.where(fits, 1.0, 0.0).astype(BF)
    label = tiles.astype(F32) + 1.0
    row_of_places = places_of(column, out.shape[0])
    places[...] = row_of_places
    place = [row_of_places[0, p] for p in range(PAIRS)]
    for name in ("lower", "top"):
        copies[name].wait()
    for p in range(PAIRS):
        product(1, p)

    def field(f):
        parts = [scratch[h, pl.ds(f, PAIRS, stride=FIELDS), :] for h in range(2)]
        return jnp.concatenate(parts, axis=1)

    u, v, ta, qa, sw, lw, pr, ps = (field(f) for f in range(FIELDS))
    sent = [x.astype(BF) for x in (u, v, ta, qa - 0.3 * ps, 0.5 * sw + 0.3 * lw, pr)]
    rest = (u - sent[0].astype(F32))[:, :LANES]
    sent.append(jnp.where(iota((PAIRS, LANES), 1) == 0, label, rest).astype(BF))
    filled = jnp.dot(chosen, jnp.concatenate(sent, axis=1), preferred_element_type=F32)
    filled = filled.astype(BF).reshape(PAIRS, SLOTS, OUT_WIDTH)
    for p in range(PAIRS):
        out[place[p]] = filled[p]
    copies["sst"].wait()
    copies["marine"].wait()


def exchange(arrived, sst, marine, fluxes, out):
    rows = arrived.shape[0] * arrived.shape[1]
    slots = arrived[...].reshape(rows, OUT_WIDTH)
    tail = slots[:, SENT * CELLS :]
    first = jnp.where(iota((TILES, LANES), 1) == 0, 1.0, 0.0).astype(BF)

    def against(a, b):
        return lax.dot_general(a, b, (((1,), (1,)), ((), ())), preferred_element_type=F32)

    wanted = (iota((TILES, rows), 0) + 1).astype(F32)
    summed = jnp.where(against(first, tail) == wanted, 1.0, 0.0).astype(BF)
    tile = (iota((rows, TILES), 1) + 1).astype(F32)
    chosen = jnp.where(against(tail, first) == tile, 1.0, 0.0).astype(BF)
    total = jnp.dot(summed, slots, preferred_element_type=F32)
    u, v, ta, q, rad, pr = (total[:, f * CELLS : (f + 1) * CELLS] for f in range(SENT))
    rest = jnp.where(iota((TILES, LANES), 1) == 0, 0.0, total[:, SENT * CELLS :])
    u = jnp.concatenate([u[:, :LANES] + rest, u[:, LANES:]], axis=1)
    warmth = sst[...]
    w = marine[...].astype(F32)
    speed = jnp.sqrt(u * u + v * v + 0.25)
    dth = warmth - ta
    dq = 0.4 * warmth - q
    lift = 2.0 * (dth + 0.5 * dq)
    c = jnp.ones_like(speed)
    for _ in range(3):
        c = 1.0 + 0.5 * jnp.tanh(lift / (1.0 + c * speed * speed))
    k = c * speed
    found = (k * u * w, k * v * w, (rad - k * dth - k * dq) * w, (pr - 0.5 * k * dq) * w)
    for f, x in enumerate(found):
        fluxes[:, f, :] = x
    back = jnp.concatenate([x.astype(BF) for x in found + (warmth * w,)], axis=1)
    out[...] = jnp.dot(chosen, back, preferred_element_type=F32).astype(BF).reshape(out.shape)


def deliver(
    src_row, places, returned, weights, fluxes, fluxes_hbm, out, values, sums, sem
):
    copy = pltpu.make_async_copy(fluxes, fluxes_hbm, sem)
    copy.start()
    row_of_places, sources = places[...], src_row[...]
    place = [row_of_places[0, p] for p in range(PAIRS)]
    src = [sources[0, p] for p in range(PAIRS)]
    values[...] = jnp.zeros_like(values)
    for p in range(PAIRS):
        second = functools.reduce(jnp.logical_or, [place[q] == place[p] for q in range(p)], False)
        slots = returned[place[p]].astype(F32)
        slot = jnp.where(second, slots[1:], slots[:1])
        for f in range(BACK):
            for h in range(2):
                start = f * CELLS + h * LANES
                values[h, p * FIELDS + f : p * FIELDS + f + 1, :] = slot[:, start : start + LANES]
    sums[...] = jnp.zeros_like(sums)
    for p in range(PAIRS):
        block = pl.ds(p * FIELDS, FIELDS)
        term = lax.dot_general(
            jnp.concatenate([values[h, block, :] for h in range(2)], axis=1).astype(BF),
            weights[p],
            (((1,), (1,)), ((), ())),
            preferred_element_type=F32,
        )
        at = pl.ds(pl.multiple_of(src[p] * FIELDS, FIELDS), FIELDS)
        for h in range(2):
            sums[h, at, :] += term[:, h * LANES : (h + 1) * LANES]
    for f in range(BACK):
        for h in range(2):
            out[f, :, h * LANES : (h + 1) * LANES] = sums[h, pl.ds(f, TILES, stride=FIELDS), :]
    copy.wait()


VMEM = pl.BlockSpec(memory_space=pltpu.VMEM)
HBM = pl.BlockSpec(memory_space=pltpu.HBM)


def on_device(sky, weights, sky_block, target_device, sea_block, sst, marine):
    devices = lax.axis_size(("gx", "gy"))
    params = pltpu.CompilerParams(vmem_limit_bytes=VMEM_LIMIT)
    flux_shape = jax.ShapeDtypeStruct((TILES, 4, CELLS), F32)

    def wire(width):
        return jax.ShapeDtypeStruct((devices, SLOTS, width), BF)

    def swap(x):
        order = sorted(range(devices), key=key_of)
        return lax.all_to_all(
            x,
            ("gx", "gy"),
            split_axis=0,
            concat_axis=0,
            axis_index_groups=[order],
            tiled=True,
        )

    def stay(*arrays):
        return tuple(pltpu.with_memory_space_constraint(x, pltpu.HBM) for x in arrays)

    outgoing, sst, marine, places = pl.pallas_call(
        contribute,
        out_shape=(
            wire(OUT_WIDTH),
            jax.ShapeDtypeStruct((TILES, CELLS), F32),
            jax.ShapeDtypeStruct((TILES, CELLS), jnp.int32),
            jax.ShapeDtypeStruct((1, PAIRS), jnp.int32),
        ),
        in_specs=[HBM] * 7,
        out_specs=(VMEM,) * 4,
        scratch_shapes=[
            pltpu.SMEM((PAIRS,), jnp.int32),
            pltpu.SMEM((PAIRS,), jnp.int32),
            pltpu.SMEM((PAIRS,), jnp.int32),
            pltpu.VMEM((TILES, FIELDS, CELLS), BF),
            pltpu.VMEM((2, PAIRS, LANES + STRIP, LANES), BF),
            pltpu.VMEM((PAIRS, STRIP, LANES), BF),
            pltpu.VMEM((PAIRS, STRIP, LANES), BF),
            pltpu.VMEM((2, PAIRS * FIELDS, LANES), F32),
            pltpu.SemaphoreType.DMA((10,)),
        ],
        compiler_params=params,
    )(*stay(sky_block, target_device.reshape(PAIRS), sea_block, sky, weights, sst, marine))
    fluxes, back = pl.pallas_call(
        exchange,
        out_shape=(flux_shape, wire(BACK_WIDTH)),
        in_specs=[VMEM] * 3,
        out_specs=(VMEM, VMEM),
        compiler_params=params,
    )(swap(outgoing), sst, marine)
    fluxes, atm_back = pl.pallas_call(
        deliver,
        out_shape=(flux_shape, jax.ShapeDtypeStruct((BACK, TILES, CELLS), F32)),
        in_specs=[VMEM] * 5,
        out_specs=(HBM, VMEM),
        scratch_shapes=[
            pltpu.VMEM((2, PAIRS * FIELDS, LANES), F32),
            pltpu.VMEM((2, TILES * FIELDS, LANES), F32),
            pltpu.SemaphoreType.DMA,
        ],
        compiler_params=params,
    )(sky_block.reshape(1, PAIRS), places, swap(back), weights, fluxes)
    return fluxes, jnp.transpose(atm_back, (1, 0, 2))


def solution(mesh):
    tiles = P(("gx", "gy"), None, None)
    cells = P(("gx", "gy"), None)
    flat = P(("gx", "gy"))
    return jax.shard_map(
        on_device,
        mesh=mesh,
        in_specs=(tiles, tiles, flat, cells, flat, cells, cells),
        out_specs=(tiles, tiles),
        check_vma=False,
    )
```

```python
import functools

import jax
import jax.numpy as jnp
from jax import lax
from jax.experimental import pallas as pl
from jax.experimental.pallas import tpu as pltpu
from jax.sharding import PartitionSpec as P

PAIRS = 16
TILES = 16
FIELDS = 8
SENT = 6
BACK = 5
CELLS = 256
LANES = 128
SLOTS = 2
STRIP = 16
OUT_WIDTH = SENT * CELLS + LANES
BACK_WIDTH = BACK * CELLS
BF = jnp.bfloat16
F32 = jnp.float32
VMEM_LIMIT = 24 * 1024 * 1024


def iota(shape, dim):
    return lax.broadcasted_iota(jnp.int32, shape, dim)


def key_of(device):
    return ((device >> 5) + ((device >> 3) & 3) + ((device >> 1) & 3)) * 128 + device


def places_of(column, devices):
    others = key_of(iota((PAIRS, devices), 1))
    ahead = jnp.where(others < key_of(column.astype(jnp.int32)), 1.0, 0.0)
    return to_row(jnp.sum(ahead, axis=1, keepdims=True)).astype(jnp.int32)


def to_column(row):
    same = iota((PAIRS, PAIRS), 0) == iota((PAIRS, PAIRS), 1)
    return jnp.sum(jnp.where(same, row, 0.0), axis=1, keepdims=True)


def to_row(column):
    same = iota((PAIRS, PAIRS), 0) == iota((PAIRS, PAIRS), 1)
    return jnp.sum(jnp.where(same, column, 0.0), axis=0, keepdims=True)


def contribute(
    src_hbm, owner_hbm, sea_hbm, sky_hbm, weights_hbm, sst_hbm, marine_hbm, out, sst, marine, places,
    src, owner, sea, sky, blocks, top, bottom, scratch, sems,
):
    copies = {}

    def fetch(name, source, held):
        copies[name] = pltpu.make_async_copy(source, held, sems.at[len(copies)])
        copies[name].start()

    left, right = pl.ds(0, LANES), pl.ds(LANES, LANES)
    every = pl.ds(0, PAIRS)
    fetch("upper", weights_hbm.at[every, pl.ds(0, LANES + STRIP), left], blocks.at[0])
    fetch("bottom", weights_hbm.at[every, pl.ds(CELLS - STRIP, STRIP), left], bottom)
    fetch("owner", owner_hbm, owner)
    fetch("sea", sea_hbm, sea)
    fetch("src", src_hbm, src)
    fetch("sky", sky_hbm, sky)
    fetch(
        "lower",
        weights_hbm.at[every, pl.ds(LANES - STRIP, LANES + STRIP), right],
        blocks.at[1],
    )
    fetch("top", weights_hbm.at[every, pl.ds(0, STRIP), right], top)
    fetch("sst", sst_hbm, sst)
    fetch("marine", marine_hbm, marine)
    out[...] = jnp.zeros_like(out)
    gap = jnp.zeros((LANES - 2 * STRIP, LANES), BF)

    def product(h, p):
        parts = [top[p], gap, blocks[1, p]] if h else [blocks[0, p], gap, bottom[p]]
        scratch[h, p * FIELDS : (p + 1) * FIELDS, :] = jnp.dot(
            sky[src[p]], jnp.concatenate(parts, axis=0), preferred_element_type=F32
        )

    for name in ("owner", "sea", "src", "sky", "upper", "bottom"):
        copies[name].wait()
    for p in range(PAIRS):
        product(0, p)
    at = iota((PAIRS, PAIRS), 1)
    row = jnp.zeros((PAIRS, PAIRS), jnp.int32)
    tiles = jnp.zeros((PAIRS, LANES), jnp.int32)
    for p in range(PAIRS):
        row = jnp.where(at == p, owner[p], row)
        tiles = jnp.where(iota((PAIRS, LANES), 0) == p, sea[p], tiles)
    row = row[:1].astype(F32)
    column = to_column(row)
    before = at < iota((PAIRS, PAIRS), 0)
    rank = jnp.sum(jnp.where((column == row) & before, 1.0, 0.0), axis=1, keepdims=True)
    both = SLOTS * PAIRS
    wanted, pair = iota((both, PAIRS), 0), iota((both, PAIRS), 1)
    mine = jnp.sum(jnp.where(wanted // SLOTS == pair, row, 0.0), axis=1, keepdims=True)
    fits = (mine == row) & ((wanted % SLOTS).astype(F32) == to_row(rank))
    chosen = jnp.where(fits, 1.0, 0.0).astype(BF)
    label = tiles.astype(F32) + 1.0
    row_of_places = places_of(column, out.shape[0])
    places[...] = row_of_places
    place = [row_of_places[0, p] for p in range(PAIRS)]
    for name in ("lower", "top"):
        copies[name].wait()
    for p in range(PAIRS):
        product(1, p)

    def field(f):
        parts = [scratch[h, pl.ds(f, PAIRS, stride=FIELDS), :] for h in range(2)]
        return jnp.concatenate(parts, axis=1)

    u, v, ta, qa, sw, lw, pr, ps = (field(f) for f in range(FIELDS))
    sent = [x.astype(BF) for x in (u, v, ta, qa - 0.3 * ps, 0.5 * sw + 0.3 * lw, pr)]
    rest = (u - sent[0].astype(F32))[:, :LANES]
    sent.append(jnp.where(iota((PAIRS, LANES), 1) == 0, label, rest).astype(BF))
    filled = jnp.dot(chosen, jnp.concatenate(sent, axis=1), preferred_element_type=F32)
    filled = filled.astype(BF).reshape(PAIRS, SLOTS, OUT_WIDTH)
    for p in range(PAIRS):
        out[place[p]] = filled[p]
    copies["sst"].wait()
    copies["marine"].wait()


def exchange(arrived, sst, marine, fluxes, out):
    rows = arrived.shape[0] * arrived.shape[1]
    slots = arrived[...].reshape(rows, OUT_WIDTH)
    tail = slots[:, SENT * CELLS :]
    first = jnp.where(iota((TILES, LANES), 1) == 0, 1.0, 0.0).astype(BF)

    def against(a, b):
        return lax.dot_general(a, b, (((1,), (1,)), ((), ())), preferred_element_type=F32)

    wanted = (iota((TILES, rows), 0) + 1).astype(F32)
    summed = jnp.where(against(first, tail) == wanted, 1.0, 0.0).astype(BF)
    tile = (iota((rows, TILES), 1) + 1).astype(F32)
    chosen = jnp.where(against(tail, first) == tile, 1.0, 0.0).astype(BF)
    total = jnp.dot(summed, slots, preferred_element_type=F32)
    u, v, ta, q, rad, pr = (total[:, f * CELLS : (f + 1) * CELLS] for f in range(SENT))
    rest = jnp.where(iota((TILES, LANES), 1) == 0, 0.0, total[:, SENT * CELLS :])
    u = jnp.concatenate([u[:, :LANES] + rest, u[:, LANES:]], axis=1)
    warmth = sst[...]
    w = marine[...].astype(F32)
    square = u * u + v * v + 0.25
    dth = warmth - ta
    dq = 0.4 * warmth - q
    lift = 2.0 * (dth + 0.5 * dq)
    c = jnp.ones_like(square)
    for _ in range(3):
        c = 1.0 + 0.5 * jnp.tanh(lift / (1.0 + c * square))
    k = c * jnp.sqrt(square)
    found = (k * u * w, k * v * w, (rad - k * dth - k * dq) * w, (pr - 0.5 * k * dq) * w)
    for f, x in enumerate(found):
        fluxes[:, f, :] = x
    back = jnp.concatenate([x.astype(BF) for x in found + (warmth * w,)], axis=1)
    out[...] = jnp.dot(chosen, back, preferred_element_type=F32).astype(BF).reshape(out.shape)


def deliver(
    src_row, places, returned, weights, fluxes, fluxes_hbm, out, values, sums, sem
):
    copy = pltpu.make_async_copy(fluxes, fluxes_hbm, sem)
    copy.start()
    row_of_places, sources = places[...], src_row[...]
    place = [row_of_places[0, p] for p in range(PAIRS)]
    src = [sources[0, p] for p in range(PAIRS)]
    values[...] = jnp.zeros_like(values)
    for p in range(PAIRS):
        second = functools.reduce(jnp.logical_or, [place[q] == place[p] for q in range(p)], False)
        slots = returned[place[p]].astype(F32)
        slot = jnp.where(second, slots[1:], slots[:1])
        for f in range(BACK):
            for h in range(2):
                start = f * CELLS + h * LANES
                values[h, p * FIELDS + f : p * FIELDS + f + 1, :] = slot[:, start : start + LANES]
    sums[...] = jnp.zeros_like(sums)
    for p in range(PAIRS):
        block = pl.ds(p * FIELDS, FIELDS)
        term = lax.dot_general(
            jnp.concatenate([values[h, block, :] for h in range(2)], axis=1).astype(BF),
            weights[p],
            (((1,), (1,)), ((), ())),
            preferred_element_type=F32,
        )
        at = pl.ds(pl.multiple_of(src[p] * FIELDS, FIELDS), FIELDS)
        for h in range(2):
            sums[h, at, :] += term[:, h * LANES : (h + 1) * LANES]
    for f in range(BACK):
        for h in range(2):
            out[f, :, h * LANES : (h + 1) * LANES] = sums[h, pl.ds(f, TILES, stride=FIELDS), :]
    copy.wait()


VMEM = pl.BlockSpec(memory_space=pltpu.VMEM)
HBM = pl.BlockSpec(memory_space=pltpu.HBM)


def on_device(sky, weights, sky_block, target_device, sea_block, sst, marine):
    devices = lax.axis_size(("gx", "gy"))
    params = pltpu.CompilerParams(vmem_limit_bytes=VMEM_LIMIT)
    flux_shape = jax.ShapeDtypeStruct((TILES, 4, CELLS), F32)

    def wire(width):
        return jax.ShapeDtypeStruct((devices, SLOTS, width), BF)

    def swap(x):
        order = sorted(range(devices), key=key_of)
        return lax.all_to_all(
            x,
            ("gx", "gy"),
            split_axis=0,
            concat_axis=0,
            axis_index_groups=[order],
            tiled=True,
        )

    def stay(*arrays):
        return tuple(pltpu.with_memory_space_constraint(x, pltpu.HBM) for x in arrays)

    outgoing, sst, marine, places = pl.pallas_call(
        contribute,
        out_shape=(
            wire(OUT_WIDTH),
            jax.ShapeDtypeStruct((TILES, CELLS), F32),
            jax.ShapeDtypeStruct((TILES, CELLS), jnp.int32),
            jax.ShapeDtypeStruct((1, PAIRS), jnp.int32),
        ),
        in_specs=[HBM] * 7,
        out_specs=(VMEM,) * 4,
        scratch_shapes=[
            pltpu.SMEM((PAIRS,), jnp.int32),
            pltpu.SMEM((PAIRS,), jnp.int32),
            pltpu.SMEM((PAIRS,), jnp.int32),
            pltpu.VMEM((TILES, FIELDS, CELLS), BF),
            pltpu.VMEM((2, PAIRS, LANES + STRIP, LANES), BF),
            pltpu.VMEM((PAIRS, STRIP, LANES), BF),
            pltpu.VMEM((PAIRS, STRIP, LANES), BF),
            pltpu.VMEM((2, PAIRS * FIELDS, LANES), F32),
            pltpu.SemaphoreType.DMA((10,)),
        ],
        compiler_params=params,
    )(*stay(sky_block, target_device.reshape(PAIRS), sea_block, sky, weights, sst, marine))
    fluxes, back = pl.pallas_call(
        exchange,
        out_shape=(flux_shape, wire(BACK_WIDTH)),
        in_specs=[VMEM] * 3,
        out_specs=(VMEM, VMEM),
        compiler_params=params,
    )(swap(outgoing), sst, marine)
    fluxes, atm_back = pl.pallas_call(
        deliver,
        out_shape=(flux_shape, jax.ShapeDtypeStruct((BACK, TILES, CELLS), F32)),
        in_specs=[VMEM] * 5,
        out_specs=(HBM, VMEM),
        scratch_shapes=[
            pltpu.VMEM((2, PAIRS * FIELDS, LANES), F32),
            pltpu.VMEM((2, TILES * FIELDS, LANES), F32),
            pltpu.SemaphoreType.DMA,
        ],
        compiler_params=params,
    )(sky_block.reshape(1, PAIRS), places, swap(back), weights, fluxes)
    return fluxes, jnp.transpose(atm_back, (1, 0, 2))


def solution(mesh):
    tiles = P(("gx", "gy"), None, None)
    cells = P(("gx", "gy"), None)
    flat = P(("gx", "gy"))
    return jax.shard_map(
        on_device,
        mesh=mesh,
        in_specs=(tiles, tiles, flat, cells, flat, cells, cells),
        out_specs=(tiles, tiles),
        check_vma=False,
    )
```
